32 devices in a mesh: groups: 2 (over y), ep: 16 (over z, x, core).
Axes of the slice: x: 2, y: 2, z: 4, core: 2. Of those that a mesh axis runs over, the one named last changes fastest.
Arguments:
- handoff_rows: bfloat16 [32, 256, 576], P(('groups', 'ep')), parts along dimension 0, may hold values from -6 to 6
- handoff_dest: int32 [32], P('groups'), parts along dimension 0, may hold values from 0 to 15, as said below
- handoff_len: int32 [32], P('groups'), parts along dimension 0, may hold values from 128 to 256, as said below
- resident_cache: bfloat16 [32, 2048, 576], P(('groups', 'ep')), parts along dimension 0, may hold values from -6 to 6
- resident_len: int32 [32], P(('groups', 'ep')), parts along dimension 0, may hold values from 512 to 2048, as said below
- queries: bfloat16 [1, 64, 128, 576], P(None, ('groups', 'ep')), parts along dimension 1
- new_latent: bfloat16 [1, 64, 576], P(None, ('groups', 'ep')), parts along dimension 1
- residual_in: bfloat16 [1, 64, 7168], P(None, ('groups', 'ep')), parts along dimension 1, may hold values from -3 to 3
- value_upward: bfloat16 [128, 512, 128], P('ep'), may hold values from -1 to 1
- out_proj: bfloat16 [128, 128, 7168], P('ep'), may hold values from -0.046875 to 0.046875
- norm_gain: bfloat16 [7168], replicated, may hold values from 0.099609375 to 1.8984375
- expert_ids: int32 [1, 64, 1], P(None, ('groups', 'ep')), parts along dimension 1, may hold values from 0 to 1
- expert_gates: float32 [1, 64, 1], P(None, ('groups', 'ep')), parts along dimension 1, may hold values from 0.1 to 0.6
- gate_proj: bfloat16 [2048, 7168], P('ep'), may hold values from -0.0625 to 0.0625
- up_proj: bfloat16 [2048, 7168], P('ep'), may hold values from -0.0625 to 0.0625
- down_proj: bfloat16 [2048, 7168], P('ep'), may hold values from -0.1875 to 0.1875
Outputs:
- hidden_leaving: bfloat16 [1, 64, 7168], P(None, ('groups', 'ep')), parts along dimension 1
The draws below stay inside these ranges and needn't reach their ends.
There are 2 independent parts, one for each index of `groups`. The reference program is written for one: setup_inputs(seed, part) draws one part's arguments, and reference() takes and returns one part's arrays. A program takes and returns all parts, laid end to end along the dimension named above; an argument that names none is the same for every part. Nothing has to cross between parts.
Inputs may be any that keep to these rules, and one draw needn't show every extreme that they name: `handoff_dest`: no decode device is named by more than two prefill devices; some is named by two, some by none. `handoff_len`: some decode device receives two prompts of 256 rows. `resident_len`: some resident cache is full.
All inputs are finite; a program needn't handle non-finite values.
Results may differ from the reference program's by a relative error of at most 0.006.
Values may be sent and summed in bfloat16 or wider, within the bound.
No kernel may reach another device: no remote copies, remote signals or barrier semaphores. Data moves between devices by JAX's collectives and lax.ppermute only.
A program may use at most 128 MiB of HBM per device.

```python
import math
import jax
import jax.numpy as jnp
from jax import lax

D = 7168
H = 128
KVR = 512
VDIM = 128
MOE_FF = 1024
UNITS = 128
CACHE = 2048
PROMPT = 256
STEPS = 1
LAT = 576
ROWS = 32
SPLIT = 8
EXPERTS = 2
TOPK = 1
N_EP = 16


def shared_latents(key):
    first_key, rest_key = jax.random.split(key)
    anchor = jnp.clip(jax.random.normal(first_key, (ROWS, LAT), jnp.float32), -6.0, 6.0)
    others = jnp.clip(jax.random.normal(rest_key, (STEPS, ROWS, LAT), jnp.float32), -6.0, 6.0)
    return (anchor, others)


def handoff_plan(key):
    order = jax.random.permutation(jax.random.fold_in(key, 41), N_EP).astype(jnp.int32)
    targets = jax.random.permutation(jax.random.fold_in(key, 43), N_EP).astype(jnp.int32)
    position = jnp.argsort(order).astype(jnp.int32)
    group = jnp.where(position < N_EP // 2, position // 2, N_EP // 4 + position - N_EP // 2)
    return (order, targets[group].astype(jnp.int32))


def draw_handoff_dest(key, part):
    order, destination = handoff_plan(key)
    return destination


def draw_handoff_len(key, part):
    order, destination = handoff_plan(key)
    key = jax.random.fold_in(key, 13)
    lengths = jax.random.randint(key, (N_EP,), PROMPT // 2, PROMPT + 1)
    source_prompts = jnp.arange(N_EP, dtype=jnp.int32)
    full_pair = (source_prompts == order[0]) | (source_prompts == order[1])
    return jnp.where(full_pair, PROMPT, lengths).astype(jnp.int32)


def draw_new_latent(key, part):
    anchor, others = shared_latents(key)
    later = others
    stacked = jnp.concatenate([anchor[None], later[1:]], axis=0)
    return stacked.astype(jnp.bfloat16)


def draw_queries(key, part):
    key = jax.random.fold_in(key, 7)
    base_key = jax.random.fold_in(key, 0)
    value_rows = jnp.clip(jax.random.normal(base_key, (STEPS, ROWS, H, LAT), jnp.float32), -6.0, 6.0)
    return value_rows.astype(jnp.bfloat16)


def draw_resident_len(key, part):
    key = jax.random.fold_in(key, 31)
    length_key, complete_key = jax.random.split(key)
    lengths = jax.random.randint(length_key, (N_EP,), CACHE // 4, CACHE + 1)
    full_row = jax.random.randint(complete_key, (), 0, N_EP)
    return jnp.where(jnp.arange(N_EP, dtype=jnp.int32) == full_row, CACHE, lengths).astype(jnp.int32)


def shard_levels(own_key, extent, cuts, smallest, high):
    loudness, own = 1.0, jax.random.fold_in(own_key, 6)
    for axis_at, parts in cuts:
        draws = jnp.exp(jax.random.uniform(jax.random.fold_in(own, axis_at), (parts,), jnp.float32, smallest / len(cuts), high / len(cuts)))
        loudness = loudness * jnp.repeat(draws, extent[axis_at] // parts).reshape([-1 if axis == axis_at else 1 for axis in range(len(extent))])
    return loudness


def choose_distinct(rng, rows, count, top, lift):
    ranking = jax.random.permutation(jax.random.fold_in(rng, 1), count)
    boost = ranking
    for power in range(3):
        boost = boost * boost // count
    boost = boost * lift // count
    lots = jax.random.randint(jax.random.fold_in(rng, 2), (rows, count), 0, 4096) + boost
    sure = jax.random.permutation(jax.random.fold_in(rng, 3), rows)[jnp.arange(count) % rows]
    lots = jnp.where(jnp.arange(rows)[:, None] == sure[None, :], 1 << 14, lots)
    merit = lots * count + jnp.arange(count)
    return lax.top_k(merit.astype(jnp.int32), top)[1].astype(jnp.int32)


def normal_values(rng, shape, scale, bound, pieces=(), kind=jnp.bfloat16):
    values = scale * jax.random.normal(rng, shape, jnp.float32)
    if pieces:
        values = values * shard_levels(rng, shape, pieces, -0.22, 0.18)
    return jnp.clip(values, -bound, bound).astype(kind)


def setup_inputs(seed: int = 0, part: int = 0) -> dict:
    arg_keys = jax.random.split(jax.random.key(seed), 17)
    part_splits = jax.random.split(jax.random.fold_in(arg_keys[16], part), 17)
    handoff_rows = normal_values(part_splits[0], (N_EP, PROMPT, LAT), 1.0, 6.0, ((0, 16),))
    handoff_dest = draw_handoff_dest(jax.random.fold_in(jax.random.fold_in(arg_keys[16], part), 71), part)
    handoff_len = draw_handoff_len(jax.random.fold_in(jax.random.fold_in(arg_keys[16], part), 71), part)
    resident_cache = normal_values(part_splits[3], (N_EP, CACHE, LAT), 1.0, 6.0, ((0, 16),))
    resident_len = draw_resident_len(jax.random.fold_in(jax.random.fold_in(arg_keys[16], part), 71), part)
    queries = draw_queries(jax.random.fold_in(jax.random.fold_in(arg_keys[16], part), 71), part)
    new_latent = draw_new_latent(jax.random.fold_in(jax.random.fold_in(arg_keys[16], part), 71), part)
    residual_in = normal_values(part_splits[7], (STEPS, ROWS, D), 0.5, 3.0, ((1, 16),))
    value_upward = normal_values(arg_keys[8], (H, KVR, VDIM), (KVR // 16) ** -0.5, 1.0, ((0, 16),))
    out_proj = normal_values(arg_keys[9], (H, VDIM, D), (H * VDIM) ** -0.5, 0.046875, ((0, 16),))
    norm_gain = jnp.clip(1.0 + 0.18 * jax.random.normal(arg_keys[10], (D,), jnp.float32), 0.099609375, 1.8984375).astype(jnp.bfloat16)
    expert_ids = choose_distinct(part_splits[11], STEPS * ROWS, EXPERTS, TOPK, 8192).reshape((STEPS, ROWS, TOPK))
    expert_gates = jnp.clip(jnp.exp(math.log(0.6) - 1.7917595 * jax.random.uniform(part_splits[12], (STEPS, ROWS, TOPK), jnp.float32) ** shard_levels(part_splits[12], (STEPS, ROWS, TOPK), ((1, 16),), -0.2, 0.2)), 0.1, 0.6)
    gate_proj = normal_values(arg_keys[13], (N_EP * UNITS, D), D ** -0.5, 0.0625, ((0, 16),))
    up_proj = normal_values(arg_keys[14], (N_EP * UNITS, D), D ** -0.5, 0.0625, ((0, 16),))
    down_proj = normal_values(arg_keys[15], (N_EP * UNITS, D), MOE_FF ** -0.5, 0.1875, ((0, 16),))
    return dict(handoff_rows=handoff_rows, handoff_dest=handoff_dest, handoff_len=handoff_len, resident_cache=resident_cache, resident_len=resident_len, queries=queries, new_latent=new_latent, residual_in=residual_in, value_upward=value_upward, out_proj=out_proj, norm_gain=norm_gain, expert_ids=expert_ids, expert_gates=expert_gates, gate_proj=gate_proj, up_proj=up_proj, down_proj=down_proj)


softmax_scale = 192.0 ** (-0.5)
norm_epsilon = 1e-06
contract_last = (((1,), (1,)), ((), ()))

def expert_rows(rows, gate_rows, up_rows, down_rows):
    gate = lax.dot_general(rows, gate_rows, contract_last, preferred_element_type=jnp.float32)
    up_value = lax.dot_general(rows, up_rows, contract_last, preferred_element_type=jnp.float32)
    act = (jax.nn.silu(gate) * up_value).astype(jnp.bfloat16)
    return jnp.dot(act, down_rows, preferred_element_type=jnp.float32).astype(jnp.bfloat16)

def attend(query, key_rows, live_keys):
    scores = lax.dot_general(query, key_rows, contract_last, preferred_element_type=jnp.float32) * softmax_scale
    scores = jnp.where(live_keys[None, :], scores, -jnp.inf)
    probs = jax.nn.softmax(scores, axis=-1).astype(jnp.bfloat16)
    mixed = jnp.dot(probs, key_rows, preferred_element_type=jnp.float32)
    return mixed[:, :KVR].astype(jnp.bfloat16)

def reference(handoff_rows, handoff_dest, handoff_len, resident_cache, resident_len, queries, new_latent, residual_in, value_upward, out_proj, norm_gain, expert_ids, expert_gates, gate_proj, up_proj, down_proj):
    source_prompts = jnp.arange(N_EP, dtype=jnp.int32)
    same_dest = handoff_dest[:, None] == handoff_dest[None, :]
    earlier = source_prompts[None, :] < source_prompts[:, None]
    rank = lax.optimization_barrier(jnp.sum((same_dest & earlier).astype(jnp.int32), axis=1)).astype(jnp.int32)
    slot_pair = jnp.arange(2, dtype=jnp.int32)
    match = (handoff_dest[:, None, None] == source_prompts[None, :, None]) & (rank[:, None, None] == slot_pair[None, None, :])
    match_int = match.astype(jnp.int32)
    source_pick = lax.optimization_barrier(jnp.sum(match_int * source_prompts[:, None, None], axis=0)).astype(jnp.int32)
    length_pick = lax.optimization_barrier(jnp.sum(match_int * handoff_len[:, None, None], axis=0)).astype(jnp.int32)
    prompt_index = jnp.arange(PROMPT, dtype=jnp.int32)
    resident_live = jnp.arange(CACHE, dtype=jnp.int32)[None, :] < resident_len[:, None]
    gate_slices = gate_proj.reshape(N_EP, UNITS, D)
    up_slices = up_proj.reshape(N_EP, UNITS, D)
    down_slices = down_proj.reshape(N_EP, UNITS, D)
    layer_steps = []
    for step_index in range(STEPS):
        fresh_rows = jnp.transpose(new_latent[:step_index + 1].reshape(step_index + 1, N_EP, 2, LAT), (1, 2, 0, 3))
        step_queries = queries[step_index].reshape(N_EP, 2, H, LAT)
        fresh_live = jnp.ones((step_index + 1,), dtype=bool)

        def per_device(items):
            cache_rows, cache_live, pick_pair, length_pair, query_pair, fresh_pair = items
            arrived_rows = handoff_rows[pick_pair].reshape(2 * PROMPT, LAT)
            arrived_live = (prompt_index[None, :] < length_pair[:, None]).reshape(2 * PROMPT)
            first_out = attend(query_pair[0], jnp.concatenate([cache_rows, fresh_pair[0]], axis=0), jnp.concatenate([cache_live, fresh_live]))
            second_out = attend(query_pair[1], jnp.concatenate([arrived_rows, fresh_pair[1]], axis=0), jnp.concatenate([arrived_live, fresh_live]))
            return jnp.stack([first_out, second_out])
        latent_result = lax.map(per_device, (resident_cache, resident_live, source_pick, length_pick, step_queries, fresh_rows)).reshape(ROWS, H, KVR)
        value_rows = jnp.einsum('bqg,qgz->bqz', latent_result.astype(jnp.float32), value_upward.astype(jnp.float32)).astype(jnp.bfloat16)
        attention = jnp.dot(value_rows.reshape(ROWS, H * VDIM), out_proj.reshape(H * VDIM, D), preferred_element_type=jnp.float32)
        hidden = residual_in[step_index].astype(jnp.float32) + attention
        inverse_rms = lax.rsqrt(lax.optimization_barrier(jnp.mean(hidden * hidden, axis=-1, keepdims=True)) + norm_epsilon)
        normed = (hidden * inverse_rms * norm_gain.astype(jnp.float32)).astype(jnp.bfloat16)
        chosen = (expert_ids[step_index][:, :, None] == jnp.arange(EXPERTS, dtype=jnp.int32)[None, None, :]).astype(jnp.float32)
        weights = lax.optimization_barrier(jnp.sum(expert_gates[step_index][:, :, None] * chosen, axis=1))
        slice_weights = jnp.repeat(weights, SPLIT, axis=1)

        def add_slice(carry, items):
            gate_rows, up_rows, down_rows, slice_weight = items
            part_out = expert_rows(normed, gate_rows, up_rows, down_rows).astype(jnp.float32)
            return (carry + slice_weight[:, None] * part_out, None)
        moe_sum, _ = lax.scan(add_slice, jnp.zeros((ROWS, D), jnp.float32), (gate_slices, up_slices, down_slices, slice_weights.T))
        layer_steps.append((hidden + moe_sum).astype(jnp.bfloat16))
    return jnp.stack(layer_steps)
```

```python
import jax
import jax.numpy as jnp
from jax import lax
from jax.sharding import PartitionSpec as P

KVR = 512
MOE_FF = 1024
UNITS = 128


softmax_scale = 192.0 ** (-0.5)
norm_epsilon = 1e-06
contract_last = (((1,), (1,)), ((), ()))


def expert_rows(rows, gate_rows, up_rows, down_rows):
    flat_rows = rows.reshape(-1, rows.shape[-1])
    gate = lax.dot_general(flat_rows, gate_rows, contract_last, preferred_element_type=jnp.float32)
    up_value = lax.dot_general(
        flat_rows, up_rows, contract_last, preferred_element_type=jnp.float32
    )
    act = (jax.nn.silu(gate) * up_value).astype(jnp.bfloat16)
    produced = jnp.dot(act, down_rows, preferred_element_type=jnp.float32).astype(jnp.bfloat16)
    return produced.reshape(rows.shape)


def attend(query, key_rows, live_keys, fresh_rows):
    scores = (
        lax.dot_general(query, key_rows, contract_last, preferred_element_type=jnp.float32)
        * softmax_scale
    )
    scores = jnp.where(live_keys[None, :], scores, -jnp.inf)
    fresh_scores = (
        lax.dot_general(query, fresh_rows, contract_last, preferred_element_type=jnp.float32)
        * softmax_scale
    )
    peak_score = jnp.maximum(
        jnp.max(scores, axis=1, keepdims=True), jnp.max(fresh_scores, axis=1, keepdims=True)
    )
    cache_terms = jnp.exp(scores - peak_score)
    fresh_terms = jnp.exp(fresh_scores - peak_score)
    denominator = jnp.sum(cache_terms, axis=1, keepdims=True) + jnp.sum(
        fresh_terms, axis=1, keepdims=True
    )
    cache_probs = (cache_terms / denominator).astype(jnp.bfloat16)
    fresh_probs = (fresh_terms / denominator).astype(jnp.bfloat16)
    mixed = jnp.dot(cache_probs, key_rows, preferred_element_type=jnp.float32) + jnp.dot(
        fresh_probs, fresh_rows, preferred_element_type=jnp.float32
    )
    return mixed[:, :KVR].astype(jnp.bfloat16)


def shards(
    handoff_rows,
    handoff_dest,
    handoff_len,
    resident_cache,
    resident_len,
    queries,
    new_latent,
    residual_in,
    value_upward,
    out_proj,
    norm_gain,
    expert_ids,
    expert_gates,
    gate_proj,
    up_proj,
    down_proj,
):
    devices = lax.axis_size("ep")
    device = lax.axis_index("ep")
    slice_count = MOE_FF // UNITS
    expert_banks = devices // slice_count
    prompt_rows = handoff_rows.shape[1]
    width = handoff_rows.shape[2]
    per_peer = prompt_rows // devices
    spread_out = jnp.transpose(handoff_rows[0].reshape(per_peer, devices, width), (1, 0, 2))
    spread_in = lax.all_to_all(spread_out, "ep", split_axis=0, concat_axis=0, tiled=True)
    source_prompts = jnp.arange(devices, dtype=jnp.int32)
    same_dest = handoff_dest[:, None] == handoff_dest[None, :]
    earlier = source_prompts[None, :] < source_prompts[:, None]
    rank = jnp.sum((same_dest & earlier).astype(jnp.int32), axis=1)
    slot_of = handoff_dest * 2 + rank
    placing = (slot_of[None, :] == jnp.arange(2 * devices, dtype=jnp.int32)[:, None]).astype(
        jnp.bfloat16
    )
    outgoing = (
        jnp.dot(placing, spread_in.reshape(devices, -1), preferred_element_type=jnp.float32)
        .astype(jnp.bfloat16)
        .reshape(devices, 2, per_peer, width)
    )
    delivered = lax.all_to_all(outgoing, "ep", split_axis=0, concat_axis=0, tiled=True)
    new_keys = delivered.reshape(-1, width)
    own_match = slot_of[:, None] == (device * 2 + jnp.arange(2, dtype=jnp.int32))[None, :]
    slot_len = jnp.sum(jnp.where(own_match, handoff_len[:, None], 0), axis=0)
    peer_index = jnp.arange(devices, dtype=jnp.int32)[:, None, None]
    row_index = jnp.arange(per_peer, dtype=jnp.int32)[None, None, :]
    position = row_index * devices + peer_index
    new_live = (position < slot_len[None, :, None]).reshape(-1)
    cache_keys = resident_cache[0]
    cache_live = jnp.arange(cache_keys.shape[0], dtype=jnp.int32) < resident_len[0]
    resident_out = attend(queries[0, 0], cache_keys, cache_live, new_latent[:, 0])
    arrived_out = attend(queries[0, 1], new_keys, new_live, new_latent[:, 1])
    step_outputs = [jnp.stack([resident_out, arrived_out])]
    latent_result = jnp.stack(step_outputs)
    residual_rows = jnp.transpose(residual_in, (1, 0, 2))
    chosen_ids = jnp.transpose(expert_ids, (1, 0, 2))
    chosen_gates = jnp.transpose(expert_gates, (1, 0, 2))
    flat_weight = out_proj.reshape(-1, out_proj.shape[2])
    step_count = latent_result.shape[0]
    incoming_heads = lax.all_to_all(latent_result, "ep", split_axis=2, concat_axis=1, tiled=True)
    value_rows = jnp.einsum(
        "dfpl,pln->fdpn", incoming_heads, value_upward, preferred_element_type=jnp.float32
    ).astype(jnp.bfloat16)
    flat_values = value_rows.reshape(value_rows.shape[0] * step_count, -1)
    partial = jnp.dot(flat_values, flat_weight, preferred_element_type=jnp.float32).astype(
        jnp.bfloat16
    )
    partials = lax.all_to_all(
        partial.reshape(devices, -1, partial.shape[1]), "ep", split_axis=0, concat_axis=0, tiled=True
    )
    attention = jnp.sum(partials.astype(jnp.float32), axis=0).reshape(2, step_count, -1)
    hidden = residual_rows.astype(jnp.float32) + attention
    inverse_rms = lax.rsqrt(jnp.mean(hidden * hidden, axis=-1, keepdims=True) + norm_epsilon)
    normed = (hidden * inverse_rms * norm_gain.astype(jnp.float32)).astype(jnp.bfloat16)
    chosen = (chosen_ids[..., None] == jnp.arange(expert_banks, dtype=jnp.int32)).astype(
        jnp.float32
    )
    weights = jnp.sum(chosen_gates[..., None] * chosen, axis=2)
    slice_weights = jnp.repeat(weights, slice_count, axis=2)
    member = jnp.repeat(jnp.sum(chosen, axis=2), slice_count, axis=2)
    outgoing_rows = jnp.where(
        jnp.transpose(member, (2, 0, 1))[..., None] > 0.5, normed[None], jnp.zeros((), jnp.bfloat16)
    )
    produced = expert_rows(
        lax.all_to_all(outgoing_rows, "ep", split_axis=0, concat_axis=0, tiled=True),
        gate_proj,
        up_proj,
        down_proj,
    )
    returned = lax.all_to_all(produced, "ep", split_axis=0, concat_axis=0, tiled=True)
    mixed = jnp.einsum("bsq,qbsd->bsd", slice_weights, returned, preferred_element_type=jnp.float32)
    finished = (hidden + mixed).astype(jnp.bfloat16)
    return jnp.transpose(finished, (1, 0, 2))


def solution(mesh):
    placed = (
        P(("groups", "ep"), None, None),
        P("groups"),
        P("groups"),
        P(("groups", "ep"), None, None),
        P(("groups", "ep")),
        P(None, ("groups", "ep"), None, None),
        P(None, ("groups", "ep"), None),
        P(None, ("groups", "ep"), None),
        P("ep", None, None),
        P("ep", None, None),
        P(),
        P(None, ("groups", "ep"), None),
        P(None, ("groups", "ep"), None),
        P("ep", None),
        P("ep", None),
        P("ep", None),
    )
    return jax.shard_map(
        shards,
        mesh=mesh,
        in_specs=placed,
        out_specs=P(None, ("groups", "ep"), None),
        check_vma=False,
    )
```

```python
import functools

import jax
import jax.numpy as jnp
from jax import lax
from jax.experimental import pallas as pl
from jax.experimental.pallas import tpu as pltpu
from jax.sharding import PartitionSpec as P

KVR = 512
MOE_FF = 1024
UNITS = 128
LANES = 128

softmax_scale = 192.0 ** (-0.5)
norm_epsilon = 1e-06
contract_last = (((1,), (1,)), ((), ()))
f32 = jnp.float32
bf16 = jnp.bfloat16
whole = pl.BlockSpec(memory_space=pltpu.VMEM)
scalars = pl.BlockSpec(memory_space=pltpu.SMEM)


def attend(query, key_rows, live_keys, fresh_rows):
    scores = (
        lax.dot_general(query, key_rows, contract_last, preferred_element_type=f32) * softmax_scale
    )
    scores = jnp.where(live_keys[None, :], scores, -jnp.inf)
    fresh_scores = (
        lax.dot_general(query, fresh_rows, contract_last, preferred_element_type=f32)
        * softmax_scale
    )
    peak_score = jnp.maximum(
        jnp.max(scores, axis=1, keepdims=True), jnp.max(fresh_scores, axis=1, keepdims=True)
    )
    cache_terms = jnp.exp(scores - peak_score)
    fresh_terms = jnp.exp(fresh_scores - peak_score)
    denominator = jnp.sum(cache_terms, axis=1, keepdims=True) + jnp.sum(
        fresh_terms, axis=1, keepdims=True
    )
    cache_probs = (cache_terms / denominator).astype(bf16)
    fresh_probs = (fresh_terms / denominator).astype(bf16)
    mixed = jnp.dot(cache_probs, key_rows, preferred_element_type=f32) + jnp.dot(
        fresh_probs, fresh_rows, preferred_element_type=f32
    )
    return mixed[:, :KVR].astype(bf16)


def three_parts(value):
    first = value.astype(bf16).astype(f32)
    second = (value - first).astype(bf16).astype(f32)
    third = value - first - second
    return first, second, third


def pick_kernel(dest_ref, spread_ref, picked_ref):
    for prompt in range(spread_ref.shape[0]):
        picked_ref[prompt] = spread_ref[dest_ref[prompt]]


def prompt_kernel(
    length_ref, query_ref, key_ref, resident_ref, own_query_ref, fresh_ref, fresh_rows_ref, out_ref
):
    peers, rows, width = out_ref.shape
    per_peer = rows // 2
    heads = peers * per_peer
    query = query_ref[...].reshape(heads, query_ref.shape[2])
    keys = key_ref[...]
    scores = lax.dot_general(query, keys, contract_last, preferred_element_type=f32)
    position = lax.broadcasted_iota(jnp.int32, scores.shape, 1)
    scores = jnp.where(position < length_ref[0], scores * softmax_scale, -jnp.inf)
    peak = jnp.max(scores, axis=1, keepdims=True)
    terms = jnp.exp(scores - peak)
    total = jnp.sum(terms, axis=1, keepdims=True)
    mixed = jnp.dot(terms.astype(bf16), keys[:, :KVR], preferred_element_type=f32) / total
    log_sum = peak + jnp.log(total)
    fresh_score = softmax_scale * jnp.sum(
        own_query_ref[...].astype(f32) * fresh_ref[...].astype(f32), axis=1, keepdims=True
    )
    lane = lax.broadcasted_iota(jnp.int32, (heads, width - KVR), 1)
    stats = jnp.zeros((heads, width - KVR), f32)
    for at, column in enumerate(three_parts(log_sum) + three_parts(fresh_score)):
        stats = jnp.where(lane == at, column, stats)
    fold = lambda value: value.reshape(peers, per_peer, value.shape[1])
    out_ref[:, :, :KVR] = jnp.concatenate(
        [fold(mixed), fold(resident_ref[...].astype(f32))], axis=1
    ).astype(bf16)
    fresh_rows = jnp.broadcast_to(
        fresh_rows_ref[...].astype(f32)[None], (peers, per_peer, width - KVR)
    )
    out_ref[:, :, KVR:] = jnp.concatenate([fold(stats), fresh_rows], axis=1).astype(bf16)


def heads_kernel(row_ref, column_ref, rows_ref, upward_ref, proj_ref, keep_ref, send_ref):
    peers, rows, width = rows_ref.shape
    per_peer = rows // 2
    columns = peers * rows
    both = 2 * peers
    row_head, row_device, row_new = row_ref[:, 0:1], row_ref[:, 1:2], row_ref[:, 2:3]
    col_peer, col_row, col_dest = column_ref[0:1, :], column_ref[1:2, :], column_ref[2:3, :]
    stats = rows_ref[:, :, KVR : KVR + LANES].astype(f32).reshape(columns, LANES).T
    log_sum = stats[0:1] + stats[1:2] + stats[2:3]
    fresh_score = stats[3:4] + stats[4:5] + stats[5:6]
    same_head = col_row == row_head
    own = col_peer == row_device
    new_row = row_new == 1
    arrives = same_head & (col_dest == row_device) & new_row
    fresh = jnp.sum(jnp.where(same_head & own, fresh_score, 0.0), axis=1, keepdims=True)
    scored = jnp.where(arrives, log_sum, -jnp.inf)
    peak = jnp.maximum(jnp.max(scored, axis=1, keepdims=True), fresh)
    terms = jnp.exp(scored - peak)
    fresh_term = jnp.exp(fresh - peak)
    scale = 1.0 / (jnp.sum(terms, axis=1, keepdims=True) + fresh_term)
    resident = jnp.where(own & (col_row == row_head + per_peer), 1.0, 0.0)
    mixing = jnp.where(new_row, terms * scale, resident)
    peer = lax.broadcasted_iota(jnp.int32, (row_ref.shape[0], peers), 1)
    fresh_mixing = jnp.where((peer == row_device) & new_row, fresh_term * scale, 0.0)
    chunk = width - KVR
    fresh_rows = jnp.concatenate(
        [rows_ref[:, per_peer + at, KVR:] for at in range(KVR // chunk)], axis=1
    )
    latents = rows_ref[:, :, :KVR].reshape(columns, KVR)
    mixed = jnp.zeros((row_ref.shape[0], KVR), f32)
    for weights, values in ((mixing, latents), (fresh_mixing, fresh_rows)):
        high = weights.astype(bf16)
        low = (weights - high.astype(f32)).astype(bf16)
        mixed = mixed + jnp.dot(high, values, preferred_element_type=f32)
        mixed = mixed + jnp.dot(low, values, preferred_element_type=f32)
    mixed = mixed.astype(bf16)
    value_rows = jnp.concatenate(
        [
            jnp.dot(
                mixed[head * both : (head + 1) * both], upward_ref[head], preferred_element_type=f32
            ).astype(bf16)
            for head in range(per_peer)
        ],
        axis=1,
    )
    step = 1024
    for start in range(0, proj_ref.shape[1], step):
        part = jnp.dot(value_rows, proj_ref[:, start : start + step], preferred_element_type=f32)
        keep_ref[:, start : start + step] = part[:peers]
        send_ref[:, start : start + step] = part[peers:].astype(bf16)


def expert_kernel(own_ref, sibling_ref, gate_ref, up_ref, down_ref, keep_ref, send_ref):
    half = own_ref.shape[0]
    rows = jnp.concatenate([own_ref[...], sibling_ref[...]], axis=0)
    gate = lax.dot_general(rows, gate_ref[...], contract_last, preferred_element_type=f32)
    up_value = lax.dot_general(rows, up_ref[...], contract_last, preferred_element_type=f32)
    act = (gate / (1.0 + jnp.exp(-gate)) * up_value).astype(bf16)
    step = 1024
    for start in range(0, down_ref.shape[1], step):
        part = jnp.dot(act, down_ref[:, start : start + step], preferred_element_type=f32)
        keep_ref[:, start : start + step] = part[:half]
        send_ref[:, start : start + step] = part[half:].astype(bf16)


def call(kernel, shapes, specs, limit=32):
    return pl.pallas_call(
        kernel,
        out_shape=shapes,
        in_specs=specs,
        out_specs=jax.tree.map(lambda _: whole, shapes),
        compiler_params=pltpu.CompilerParams(vmem_limit_bytes=limit << 20),
    )


def shards(
    handoff_rows,
    handoff_dest,
    handoff_len,
    resident_cache,
    resident_len,
    queries,
    new_latent,
    residual_in,
    value_upward,
    out_proj,
    norm_gain,
    expert_ids,
    expert_gates,
    gate_proj,
    up_proj,
    down_proj,
):
    devices = lax.axis_size("ep")
    device = lax.axis_index("ep")
    core = device % 2
    chips = devices // 2
    siblings = [(i, i ^ 1) for i in range(devices)]
    same_core = [[2 * chip + k for chip in range(chips)] for k in range(2)]
    slice_count = MOE_FF // UNITS
    heads, width = queries.shape[2], queries.shape[3]
    per_peer = heads // devices
    model = residual_in.shape[2]

    exchange = functools.partial(
        lax.all_to_all, axis_name="ep", split_axis=0, concat_axis=0, tiled=True
    )
    exchange_core = functools.partial(exchange, axis_index_groups=same_core)

    spread = exchange(queries[0, 1].reshape(devices, per_peer, width))
    picked = call(
        pick_kernel,
        jax.ShapeDtypeStruct(spread.shape, bf16),
        [scalars, whole],
    )(handoff_dest, spread)
    arrived = exchange(picked)

    cache_keys = resident_cache[0]
    cache_live = jnp.arange(cache_keys.shape[0], dtype=jnp.int32) < resident_len[0]
    resident_out = attend(queries[0, 0], cache_keys, cache_live, new_latent[:, 0])

    chunk = max(LANES, KVR // per_peer)
    fresh_rows = new_latent[0, 1, :KVR].reshape(KVR // chunk, chunk)
    fresh_rows = jnp.pad(fresh_rows, ((0, per_peer - KVR // chunk), (0, 0)))
    own_len = lax.dynamic_slice(handoff_len, (device,), (1,))
    payload = call(
        prompt_kernel,
        jax.ShapeDtypeStruct((devices, 2 * per_peer, KVR + chunk), bf16),
        [scalars] + [whole] * 6,
    )(
        own_len,
        arrived,
        handoff_rows[0],
        resident_out,
        queries[0, 1],
        new_latent[0, 1:2],
        fresh_rows,
    )
    by_head = exchange(payload)

    row = jnp.arange(per_peer * 2 * devices, dtype=jnp.int32)
    row_core = (row // devices % 2) ^ core
    row_device = row // 2 % chips * 2 + row_core
    row_table = jnp.stack([row // (2 * devices), row_device, row % 2], axis=1)
    column = jnp.arange(devices * 2 * per_peer, dtype=jnp.int32)
    col_peer = column // (2 * per_peer)
    column_table = jnp.stack(
        [col_peer, column % (2 * per_peer), jnp.repeat(handoff_dest, 2 * per_peer)], axis=0
    )
    half_f32 = jax.ShapeDtypeStruct((devices, model), f32)
    half_bf16 = jax.ShapeDtypeStruct((devices, model), bf16)
    keep, send = call(heads_kernel, (half_f32, half_bf16), [whole] * 5, 48)(
        row_table,
        column_table,
        by_head,
        value_upward,
        out_proj.reshape(-1, model),
    )

    def reduce_rows(keep, send):
        other = lax.ppermute(send, "ep", siblings)
        pair = (keep + other.astype(f32)).astype(bf16).reshape(chips, 2, model)
        return exchange_core(pair)

    attention = jnp.sum(reduce_rows(keep, send).astype(f32), axis=0)
    hidden = residual_in[0].astype(f32) + attention
    inverse_rms = lax.rsqrt(jnp.mean(hidden * hidden, axis=-1, keepdims=True) + norm_epsilon)
    normed = (hidden * inverse_rms * norm_gain.astype(f32)).astype(bf16)

    own_rows = exchange_core(jnp.broadcast_to(normed[None], (chips, 2, model)))
    own_rows = own_rows.reshape(devices, model)
    sibling_rows = lax.ppermute(own_rows, "ep", siblings)
    keep, send = call(expert_kernel, (half_f32, half_bf16), [whole] * 5)(
        own_rows, sibling_rows, gate_proj, up_proj, down_proj
    )
    returned = reduce_rows(keep, send)

    chip_expert = jnp.arange(chips, dtype=jnp.int32) * 2 // slice_count
    chosen = (expert_ids[0][..., None] == chip_expert).astype(f32)
    weights = jnp.sum(expert_gates[0][..., None] * chosen, axis=1)
    mixed = jnp.sum(weights.T[..., None] * returned.astype(f32), axis=0)
    return (hidden + mixed).astype(bf16)[None]


def solution(mesh):
    placed = (
        P(("groups", "ep"), None, None),
        P("groups"),
        P("groups"),
        P(("groups", "ep"), None, None),
        P(("groups", "ep")),
        P(None, ("groups", "ep"), None, None),
        P(None, ("groups", "ep"), None),
        P(None, ("groups", "ep"), None),
        P("ep", None, None),
        P("ep", None, None),
        P(),
        P(None, ("groups", "ep"), None),
        P(None, ("groups", "ep"), None),
        P("ep", None),
        P("ep", None),
        P("ep", None),
    )
    return jax.shard_map(
        shards,
        mesh=mesh,
        in_specs=placed,
        out_specs=P(None, ("groups", "ep"), None),
        check_vma=False,
    )
```

```python
import functools

import jax
import jax.numpy as jnp
from jax import lax
from jax.experimental import pallas as pl
from jax.experimental.pallas import tpu as pltpu
from jax.sharding import PartitionSpec as P

KVR = 512
MOE_FF = 1024
UNITS = 128
LANES = 128
BLOCK = 1024

softmax_scale = 192.0 ** (-0.5)
norm_epsilon = 1e-06
contract_last = (((1,), (1,)), ((), ()))
f32 = jnp.float32
bf16 = jnp.bfloat16
whole = pl.BlockSpec(memory_space=pltpu.VMEM)
scalars = pl.BlockSpec(memory_space=pltpu.SMEM)


def attend(query, key_rows, live_keys, fresh_rows):
    scores = (
        lax.dot_general(query, key_rows, contract_last, preferred_element_type=f32) * softmax_scale
    )
    scores = jnp.where(live_keys[None, :], scores, -jnp.inf)
    fresh_scores = (
        lax.dot_general(query, fresh_rows, contract_last, preferred_element_type=f32)
        * softmax_scale
    )
    peak_score = jnp.maximum(
        jnp.max(scores, axis=1, keepdims=True), jnp.max(fresh_scores, axis=1, keepdims=True)
    )
    cache_terms = jnp.exp(scores - peak_score)
    fresh_terms = jnp.exp(fresh_scores - peak_score)
    denominator = jnp.sum(cache_terms, axis=1, keepdims=True) + jnp.sum(
        fresh_terms, axis=1, keepdims=True
    )
    cache_probs = (cache_terms / denominator).astype(bf16)
    fresh_probs = (fresh_terms / denominator).astype(bf16)
    mixed = jnp.dot(cache_probs, key_rows, preferred_element_type=f32) + jnp.dot(
        fresh_probs, fresh_rows, preferred_element_type=f32
    )
    return mixed[:, :KVR].astype(bf16)


def three_parts(value):
    first = value.astype(bf16).astype(f32)
    second = (value - first).astype(bf16).astype(f32)
    third = value - first - second
    return first, second, third


def spread_kernel(query_ref, spread_ref):
    peers, per_peer, width = spread_ref.shape
    rows = query_ref[0].astype(f32).T.reshape(peers, per_peer, width)
    spread_ref[...] = rows.astype(bf16)


def pick_kernel(dest_ref, spread_ref, picked_ref):
    for prompt in range(spread_ref.shape[0]):
        picked_ref[prompt] = spread_ref[dest_ref[prompt]]


def fresh_kernel(query_ref, fresh_ref, stats_ref):
    score = softmax_scale * jnp.sum(
        query_ref[...].astype(f32) * fresh_ref[...].astype(f32), axis=1, keepdims=True
    )
    lane = lax.broadcasted_iota(jnp.int32, stats_ref.shape, 1)
    stats = jnp.zeros(stats_ref.shape, f32)
    for at, column in enumerate(three_parts(score)):
        stats = jnp.where(lane == 3 + at, column, stats)
    stats_ref[...] = stats


def prompt_kernel(
    length_ref, query_ref, key_ref, resident_ref, stats_ref, fresh_rows_ref, out_ref
):
    peers, rows, width = out_ref.shape
    per_peer = rows // 2
    heads = peers * per_peer
    query = query_ref[...].reshape(heads, query_ref.shape[2])
    keys = key_ref[...]
    scores = lax.dot_general(query, keys, contract_last, preferred_element_type=f32)
    position = lax.broadcasted_iota(jnp.int32, scores.shape, 1)
    scores = jnp.where(position < length_ref[0], scores * softmax_scale, -jnp.inf)
    peak = jnp.max(scores, axis=1, keepdims=True)
    terms = jnp.exp(scores - peak)
    total = jnp.sum(terms, axis=1, keepdims=True)
    mixed = jnp.dot(terms.astype(bf16), keys[:, :KVR], preferred_element_type=f32) / total
    lane = lax.broadcasted_iota(jnp.int32, (heads, width - KVR), 1)
    stats = stats_ref[...]
    for at, column in enumerate(three_parts(peak + jnp.log(total))):
        stats = jnp.where(lane == at, column, stats)
    fold = lambda value: value.reshape(peers, per_peer, value.shape[1])
    out_ref[:, :, :KVR] = jnp.concatenate(
        [fold(mixed), fold(resident_ref[...].astype(f32))], axis=1
    ).astype(bf16)
    fresh_rows = jnp.broadcast_to(
        fresh_rows_ref[...].astype(f32)[None], (peers, per_peer, width - KVR)
    )
    out_ref[:, :, KVR:] = jnp.concatenate([fold(stats), fresh_rows], axis=1).astype(bf16)


def pair_kernel(keep_ref, other_ref, pair_ref):
    total = keep_ref[...] + other_ref[...].astype(f32)
    pair_ref[...] = total.reshape(pair_ref.shape).astype(bf16)


def heads_kernel(
    row_ref,
    column_ref,
    rows_ref,
    upward_hbm,
    proj_hbm,
    keep_ref,
    send_ref,
    upward_ref,
    proj_ref,
    arrived,
):
    upward_copy = pltpu.make_async_copy(upward_hbm, upward_ref, arrived.at[0])
    upward_copy.start()
    blocks = range(0, proj_ref.shape[1], BLOCK)
    proj_copies = [
        pltpu.make_async_copy(
            proj_hbm.at[:, start : start + BLOCK],
            proj_ref.at[:, start : start + BLOCK],
            arrived.at[1 + at],
        )
        for at, start in enumerate(blocks)
    ]
    for copy in proj_copies:
        copy.start()
    peers, rows, width = rows_ref.shape
    per_peer = rows // 2
    columns = peers * rows
    both = 2 * peers
    row_head, row_device, row_new = row_ref[:, 0:1], row_ref[:, 1:2], row_ref[:, 2:3]
    col_peer, col_row, col_dest = column_ref[0:1, :], column_ref[1:2, :], column_ref[2:3, :]
    stats = rows_ref[:, :, KVR : KVR + LANES].astype(f32).reshape(columns, LANES).T
    log_sum = stats[0:1] + stats[1:2] + stats[2:3]
    fresh_score = stats[3:4] + stats[4:5] + stats[5:6]
    same_head = col_row == row_head
    own = col_peer == row_device
    new_row = row_new == 1
    arrives = same_head & (col_dest == row_device) & new_row
    fresh = jnp.sum(jnp.where(same_head & own, fresh_score, 0.0), axis=1, keepdims=True)
    scored = jnp.where(arrives, log_sum, -jnp.inf)
    peak = jnp.maximum(jnp.max(scored, axis=1, keepdims=True), fresh)
    terms = jnp.exp(scored - peak)
    fresh_term = jnp.exp(fresh - peak)
    scale = 1.0 / (jnp.sum(terms, axis=1, keepdims=True) + fresh_term)
    resident = jnp.where(own & (col_row == row_head + per_peer), 1.0, 0.0)
    mixing = jnp.where(new_row, terms * scale, resident)
    peer = lax.broadcasted_iota(jnp.int32, (row_ref.shape[0], peers), 1)
    fresh_mixing = jnp.where((peer == row_device) & new_row, fresh_term * scale, 0.0)
    chunk = width - KVR
    fresh_rows = jnp.concatenate(
        [rows_ref[:, per_peer + at, KVR:] for at in range(KVR // chunk)], axis=1
    )
    latents = rows_ref[:, :, :KVR].reshape(columns, KVR)
    mixed = jnp.zeros((row_ref.shape[0], KVR), f32)
    for weights, values in ((mixing, latents), (fresh_mixing, fresh_rows)):
        high = weights.astype(bf16)
        low = (weights - high.astype(f32)).astype(bf16)
        mixed = mixed + jnp.dot(high, values, preferred_element_type=f32)
        mixed = mixed + jnp.dot(low, values, preferred_element_type=f32)
    mixed = mixed.astype(bf16)
    upward_copy.wait()
    value_rows = jnp.concatenate(
        [
            jnp.dot(
                mixed[head * both : (head + 1) * both], upward_ref[head], preferred_element_type=f32
            ).astype(bf16)
            for head in range(per_peer)
        ],
        axis=1,
    )
    for copy, start in zip(proj_copies, blocks):
        copy.wait()
        part = jnp.dot(value_rows, proj_ref[:, start : start + BLOCK], preferred_element_type=f32)
        keep_ref[:, start : start + BLOCK] = part[:peers]
        send_ref[:, start : start + BLOCK] = part[peers:].astype(bf16)


def expert_kernel(rows_ref, *refs):
    out_ref, arrived = refs[6], refs[10]
    units = refs[0].shape[0]
    copies = [
        pltpu.make_async_copy(
            refs[at], refs[7 + at // 2].at[pl.ds(at % 2 * units, units)], arrived.at[at]
        )
        for at in range(6)
    ]
    for copy in copies:
        copy.start()
    gate_ref, up_ref, down_ref = refs[7:10]
    rows = rows_ref[...]
    copies[0].wait()
    copies[1].wait()
    gate = lax.dot_general(rows, gate_ref[...], contract_last, preferred_element_type=f32)
    copies[2].wait()
    copies[3].wait()
    up_value = lax.dot_general(rows, up_ref[...], contract_last, preferred_element_type=f32)
    act = (gate / (1.0 + jnp.exp(-gate)) * up_value).astype(bf16)
    copies[4].wait()
    copies[5].wait()
    chips, pair = out_ref.shape[:2]
    for start in range(0, down_ref.shape[1], BLOCK):
        part = jnp.dot(act, down_ref[:, start : start + BLOCK], preferred_element_type=f32)
        out_ref[:, :, start : start + BLOCK] = part.reshape(chips, pair, BLOCK).astype(bf16)


def near(value):
    return pltpu.with_memory_space_constraint(value, pltpu.VMEM)


def call(kernel, outputs, operands, far=(), scratch=()):
    specs = [scalars if operand.ndim == 1 else whole for operand in operands]
    return pl.pallas_call(
        kernel,
        out_shape=[pltpu.VMEM(shape, dtype) for shape, dtype in outputs],
        in_specs=specs + [pl.BlockSpec(memory_space=pl.ANY)] * len(far),
        out_specs=[whole] * len(outputs),
        scratch_shapes=scratch,
        compiler_params=pltpu.CompilerParams(vmem_limit_bytes=32 << 20),
    )(
        *[operand if operand.ndim == 1 else near(operand) for operand in operands],
        *[pltpu.with_memory_space_constraint(operand, pltpu.HBM) for operand in far],
    )


def shards(
    handoff_rows,
    handoff_dest,
    handoff_len,
    resident_cache,
    resident_len,
    queries,
    new_latent,
    residual_in,
    value_upward,
    out_proj,
    norm_gain,
    expert_ids,
    expert_gates,
    gate_proj,
    up_proj,
    down_proj,
):
    devices = lax.axis_size("ep")
    device = lax.axis_index("ep")
    core = device % 2
    chips = devices // 2
    siblings = [(i, i ^ 1) for i in range(devices)]
    same_core = [[2 * chip + k for chip in range(chips)] for k in range(2)]
    slice_count = MOE_FF // UNITS
    heads, width = queries.shape[2], queries.shape[3]
    per_peer = heads // devices
    model = residual_in.shape[2]

    exchange = functools.partial(
        lax.all_to_all, axis_name="ep", split_axis=0, concat_axis=0, tiled=True
    )
    exchange_core = functools.partial(exchange, axis_index_groups=same_core)

    flipped = jnp.swapaxes(queries[0], 1, 2)
    spread_rows = pl.pallas_call(
        spread_kernel,
        out_shape=pltpu.VMEM((devices, per_peer, width), bf16),
        grid=(1,),
        in_specs=[pl.BlockSpec((1, width, heads), lambda step: (1, 0, 0))],
        out_specs=pl.BlockSpec((devices, per_peer, width), lambda step: (0, 0, 0)),
        compiler_params=pltpu.CompilerParams(vmem_limit_bytes=16 << 20),
    )(pltpu.with_memory_space_constraint(flipped, pltpu.HBM))
    spread = exchange(spread_rows)
    (picked,) = call(pick_kernel, [(spread.shape, bf16)], [handoff_dest, spread])
    arrived = exchange(picked)

    cache_keys = resident_cache[0]
    cache_live = jnp.arange(cache_keys.shape[0], dtype=jnp.int32) < resident_len[0]
    resident_out = attend(queries[0, 0], cache_keys, cache_live, new_latent[:, 0])

    chunk = max(LANES, KVR // per_peer)
    fresh_rows = new_latent[0, 1, :KVR].reshape(KVR // chunk, chunk)
    fresh_rows = jnp.pad(fresh_rows, ((0, per_peer - KVR // chunk), (0, 0)))
    own_len = lax.dynamic_slice(handoff_len, (device,), (1,))
    (stats,) = call(fresh_kernel, [((heads, chunk), f32)], [queries[0, 1], new_latent[0, 1:2]])
    (payload,) = call(
        prompt_kernel,
        [((devices, 2 * per_peer, KVR + chunk), bf16)],
        [own_len, arrived, handoff_rows[0], resident_out, stats, fresh_rows],
    )
    by_head = exchange(payload)

    row = jnp.arange(per_peer * 2 * devices, dtype=jnp.int32)
    row_core = (row // devices % 2) ^ core
    row_device = row // 2 % chips * 2 + row_core
    row_table = jnp.stack([row // (2 * devices), row_device, row % 2], axis=1)
    column = jnp.arange(devices * 2 * per_peer, dtype=jnp.int32)
    col_peer = column // (2 * per_peer)
    column_table = jnp.stack(
        [col_peer, column % (2 * per_peer), jnp.repeat(handoff_dest, 2 * per_peer)], axis=0
    )
    projection = out_proj.reshape(-1, model)
    keep, send = call(
        heads_kernel,
        [((devices, model), f32), ((devices, model), bf16)],
        [row_table, column_table, by_head],
        [value_upward, projection],
        [
            pltpu.VMEM(value_upward.shape, bf16),
            pltpu.VMEM(projection.shape, bf16),
            pltpu.SemaphoreType.DMA((1 + model // BLOCK,)),
        ],
    )

    other = lax.ppermute(send, "ep", siblings)
    (pair,) = call(pair_kernel, [((chips, 2, model), bf16)], [keep, other])
    attention = jnp.sum(exchange_core(pair).astype(f32), axis=0)
    hidden = residual_in[0].astype(f32) + attention
    inverse_rms = lax.rsqrt(jnp.mean(hidden * hidden, axis=-1, keepdims=True) + norm_epsilon)
    normed = (hidden * inverse_rms * norm_gain.astype(f32)).astype(bf16)

    own_rows = exchange_core(jnp.broadcast_to(normed[None], (chips, 2, model)))
    experts = []
    for matrix in (gate_proj, up_proj, down_proj):
        experts += [matrix, lax.ppermute(matrix, "ep", siblings)]
    (part,) = call(
        expert_kernel,
        [((chips, 2, model), bf16)],
        [own_rows.reshape(devices, model)],
        experts,
        [pltpu.VMEM((2 * gate_proj.shape[0], model), bf16)] * 3
        + [pltpu.SemaphoreType.DMA((6,))],
    )
    returned = exchange_core(part)

    chip_expert = jnp.arange(chips, dtype=jnp.int32) * 2 // slice_count
    chosen = (expert_ids[0][..., None] == chip_expert).astype(f32)
    weights = jnp.sum(expert_gates[0][..., None] * chosen, axis=1)
    mixed = jnp.sum(weights.T[..., None] * returned.astype(f32), axis=0)
    return (hidden + mixed).astype(bf16)[None]


def solution(mesh):
    placed = (
        P(("groups", "ep"), None, None),
        P("groups"),
        P("groups"),
        P(("groups", "ep"), None, None),
        P(("groups", "ep")),
        P(None, ("groups", "ep"), None, None),
        P(None, ("groups", "ep"), None),
        P(None, ("groups", "ep"), None),
        P("ep", None, None),
        P("ep", None, None),
        P(),
        P(None, ("groups", "ep"), None),
        P(None, ("groups", "ep"), None),
        P("ep", None),
        P("ep", None),
        P("ep", None),
    )
    return jax.shard_map(
        shards,
        mesh=mesh,
        in_specs=placed,
        out_specs=P(None, ("groups", "ep"), None),
        check_vma=False,
    )
```

```python
import functools

import jax
import jax.numpy as jnp
from jax import lax
from jax.experimental import pallas as pl
from jax.experimental.pallas import tpu as pltpu
from jax.sharding import PartitionSpec as P

KVR = 512
MOE_FF = 1024
UNITS = 128
LANES = 128
BLOCK = 1024
PLANE = 4
FRESH_ROWS = 16

softmax_scale = 192.0 ** (-0.5)
norm_epsilon = 1e-06
contract_last = (((1,), (1,)), ((), ()))
f32 = jnp.float32
bf16 = jnp.bfloat16
whole = pl.BlockSpec(memory_space=pltpu.VMEM)
scalars = pl.BlockSpec(memory_space=pltpu.SMEM)


def attend(query, key_rows, live_keys, fresh_rows):
    scores = (
        lax.dot_general(query, key_rows, contract_last, preferred_element_type=f32) * softmax_scale
    )
    scores = jnp.where(live_keys[None, :], scores, -jnp.inf)
    fresh_scores = (
        lax.dot_general(query, fresh_rows, contract_last, preferred_element_type=f32)
        * softmax_scale
    )
    peak_score = jnp.maximum(
        jnp.max(scores, axis=1, keepdims=True), jnp.max(fresh_scores, axis=1, keepdims=True)
    )
    cache_terms = jnp.exp(scores - peak_score)
    fresh_terms = jnp.exp(fresh_scores - peak_score)
    denominator = jnp.sum(cache_terms, axis=1, keepdims=True) + jnp.sum(
        fresh_terms, axis=1, keepdims=True
    )
    cache_probs = (cache_terms / denominator).astype(bf16)
    fresh_probs = (fresh_terms / denominator).astype(bf16)
    mixed = jnp.dot(cache_probs, key_rows, preferred_element_type=f32) + jnp.dot(
        fresh_probs, fresh_rows, preferred_element_type=f32
    )
    return mixed[:, :KVR]


def three_parts(value):
    first = value.astype(bf16).astype(f32)
    second = (value - first).astype(bf16).astype(f32)
    third = value - first - second
    return first, second, third


def spread_kernel(query_ref, spread_ref):
    peers, rows, width = spread_ref.shape
    planes = peers // PLANE
    by_peer = query_ref[0].astype(f32).T.reshape(planes, PLANE, rows // planes, width)
    for column in range(PLANE):
        block = by_peer[:, column].reshape(rows, width).astype(bf16)
        for plane in range(planes):
            spread_ref[plane * PLANE + column] = block


def column_kernel(device_ref, resident_ref, fresh_ref, *message_refs):
    planes, _, per_peer, latent = resident_ref.shape
    rows = planes * per_peer
    column = device_ref[0] % PLANE
    for at, message_ref in enumerate(message_refs):
        message_ref[:rows, :latent] = resident_ref[:, column ^ at].reshape(rows, latent).astype(bf16)
        message_ref[rows:] = jnp.broadcast_to(fresh_ref[...], message_ref[rows:].shape)


def prompt_kernel(device_ref, dest_ref, length_ref, query_ref, *refs):
    key_refs, message_refs = refs[:PLANE], refs[PLANE : 2 * PLANE]
    out_refs, stage_ref = refs[2 * PLANE : -1], refs[-1]
    planes, _, rows, width = stage_ref.shape
    per_peer, chunk = rows // 2, width - KVR
    heads = planes * per_peer
    device = device_ref[0]
    scores = []
    for at in range(PLANE):
        prompt = device ^ at
        query = query_ref[dest_ref[prompt]]
        score = jnp.dot(query, key_refs[at][...], preferred_element_type=f32) * softmax_scale
        position = lax.broadcasted_iota(jnp.int32, score.shape, 1)
        scores.append(jnp.where(position < length_ref[prompt], score, -jnp.inf))
    scores = jnp.concatenate(scores, axis=0)
    peak = jnp.max(scores, axis=1, keepdims=True)
    terms = jnp.exp(scores - peak)
    total = jnp.sum(terms, axis=1, keepdims=True)
    log_sum = peak + jnp.log(total)
    scale = 1.0 / total
    terms = terms.astype(bf16)
    lane = lax.broadcasted_iota(jnp.int32, (heads, chunk), 1)
    fold = lambda value: value.reshape(planes, per_peer, value.shape[1])
    for at in range(PLANE):
        part = slice(at * heads, (at + 1) * heads)
        mixed = lax.dot_general(
            terms[part], key_refs[at][:KVR], contract_last, preferred_element_type=f32
        )
        resident = message_refs[at][:heads, :KVR].astype(f32)
        stage_ref[:, at, :, :KVR] = jnp.concatenate(
            [fold(mixed * scale[part]), fold(resident)], axis=1
        ).astype(bf16)
        fresh = message_refs[at][heads : heads + FRESH_ROWS].astype(f32)[:1]
        fresh_score = softmax_scale * jnp.sum(
            query_ref[device ^ at].astype(f32) * fresh, axis=1, keepdims=True
        )
        stats = jnp.zeros((heads, chunk), f32)
        for lane_at, value in enumerate(three_parts(log_sum[part]) + three_parts(fresh_score)):
            stats = jnp.where(lane == lane_at, value, stats)
        fresh_rows = [fresh[:, start : start + chunk] for start in range(0, KVR, chunk)]
        if len(fresh_rows) < per_peer:
            fresh_rows.append(jnp.zeros((per_peer - len(fresh_rows), chunk), f32))
        fresh_rows = jnp.concatenate(fresh_rows, axis=0)[None]
        stage_ref[:, at, :, KVR:] = jnp.concatenate(
            [fold(stats), jnp.broadcast_to(fresh_rows, (planes, per_peer, chunk))], axis=1
        ).astype(bf16)
    for at, out_ref in enumerate(out_refs):
        out_ref[...] = stage_ref[(device // PLANE) ^ at]


def pair_kernel(keep_ref, other_ref, pair_ref):
    total = keep_ref[...] + other_ref[...].astype(f32)
    pair_ref[...] = total.reshape(pair_ref.shape).astype(bf16)


def heads_kernel(row_ref, column_ref, peer_ref, *refs):
    payload_refs, rows_ref, arrived = refs[:-8], refs[-2], refs[-1]
    upward_hbm, proj_hbm, keep_ref, send_ref, upward_ref, proj_ref = refs[-8:-2]
    upward_copy = pltpu.make_async_copy(upward_hbm, upward_ref, arrived.at[0])
    upward_copy.start()
    blocks = range(0, proj_ref.shape[1], BLOCK)
    proj_copies = [
        pltpu.make_async_copy(
            proj_hbm.at[:, start : start + BLOCK],
            proj_ref.at[:, start : start + BLOCK],
            arrived.at[1 + at],
        )
        for at, start in enumerate(blocks)
    ]
    for copy in proj_copies:
        copy.start()
    for at, payload_ref in enumerate(payload_refs):
        rows_ref[at * PLANE : (at + 1) * PLANE] = payload_ref[...]
    peers, rows, width = rows_ref.shape
    per_peer = rows // 2
    columns = peers * rows
    both = 2 * peers
    row_head, row_device, row_new = row_ref[:, 0:1], row_ref[:, 1:2], row_ref[:, 2:3]
    col_peer, col_row, col_dest = column_ref[0:1, :], column_ref[1:2, :], column_ref[2:3, :]
    stats = rows_ref[:, :, KVR : KVR + LANES].astype(f32).reshape(columns, LANES).T
    log_sum = stats[0:1] + stats[1:2] + stats[2:3]
    fresh_score = stats[3:4] + stats[4:5] + stats[5:6]
    same_head = col_row == row_head
    own = col_peer == row_device
    new_row = row_new == 1
    arrives = same_head & (col_dest == row_device) & new_row
    fresh = jnp.sum(jnp.where(same_head & own, fresh_score, 0.0), axis=1, keepdims=True)
    scored = jnp.where(arrives, log_sum, -jnp.inf)
    peak = jnp.maximum(jnp.max(scored, axis=1, keepdims=True), fresh)
    terms = jnp.exp(scored - peak)
    fresh_term = jnp.exp(fresh - peak)
    scale = 1.0 / (jnp.sum(terms, axis=1, keepdims=True) + fresh_term)
    resident = jnp.where(own & (col_row == row_head + per_peer), 1.0, 0.0)
    mixing = jnp.where(new_row, terms * scale, resident)
    fresh_mixing = jnp.where((peer_ref[...] == row_device) & new_row, fresh_term * scale, 0.0)
    chunk = width - KVR
    fresh_rows = jnp.concatenate(
        [rows_ref[:, per_peer + at, KVR:] for at in range(KVR // chunk)], axis=1
    )
    latents = rows_ref[:, :, :KVR].reshape(columns, KVR)
    mixed = jnp.zeros((row_ref.shape[0], KVR), f32)
    for weights, values in ((mixing, latents), (fresh_mixing, fresh_rows)):
        high = weights.astype(bf16)
        low = (weights - high.astype(f32)).astype(bf16)
        mixed = mixed + jnp.dot(high, values, preferred_element_type=f32)
        mixed = mixed + jnp.dot(low, values, preferred_element_type=f32)
    mixed = mixed.astype(bf16)
    upward_copy.wait()
    value_rows = jnp.concatenate(
        [
            jnp.dot(
                mixed[head * both : (head + 1) * both], upward_ref[head], preferred_element_type=f32
            ).astype(bf16)
            for head in range(per_peer)
        ],
        axis=1,
    )
    for copy, start in zip(proj_copies, blocks):
        copy.wait()
        part = jnp.dot(value_rows, proj_ref[:, start : start + BLOCK], preferred_element_type=f32)
        keep_ref[:, start : start + BLOCK] = part[:peers]
        send_ref[:, start : start + BLOCK] = part[peers:].astype(bf16)


def expert_kernel(rows_ref, *refs):
    out_ref, arrived = refs[6], refs[10]
    units = refs[0].shape[0]
    copies = [
        pltpu.make_async_copy(
            refs[at], refs[7 + at // 2].at[pl.ds(at % 2 * units, units)], arrived.at[at]
        )
        for at in range(6)
    ]
    for copy in copies:
        copy.start()
    gate_ref, up_ref, down_ref = refs[7:10]
    rows = rows_ref[...]
    copies[0].wait()
    copies[1].wait()
    gate = lax.dot_general(rows, gate_ref[...], contract_last, preferred_element_type=f32)
    copies[2].wait()
    copies[3].wait()
    up_value = lax.dot_general(rows, up_ref[...], contract_last, preferred_element_type=f32)
    act = (gate / (1.0 + jnp.exp(-gate)) * up_value).astype(bf16)
    copies[4].wait()
    copies[5].wait()
    chips, pair = out_ref.shape[:2]
    for start in range(0, down_ref.shape[1], BLOCK):
        part = jnp.dot(act, down_ref[:, start : start + BLOCK], preferred_element_type=f32)
        out_ref[:, :, start : start + BLOCK] = part.reshape(chips, pair, BLOCK).astype(bf16)


def near(value):
    return pltpu.with_memory_space_constraint(value, pltpu.VMEM)


def call(kernel, outputs, operands, far=(), scratch=()):
    specs = [scalars if operand.ndim == 1 else whole for operand in operands]
    return pl.pallas_call(
        kernel,
        out_shape=[pltpu.VMEM(shape, dtype) for shape, dtype in outputs],
        in_specs=specs + [pl.BlockSpec(memory_space=pl.ANY)] * len(far),
        out_specs=[whole] * len(outputs),
        scratch_shapes=scratch,
        compiler_params=pltpu.CompilerParams(vmem_limit_bytes=32 << 20),
    )(
        *[operand if operand.ndim == 1 else near(operand) for operand in operands],
        *[pltpu.with_memory_space_constraint(operand, pltpu.HBM) for operand in far],
    )


def shards(
    handoff_rows,
    handoff_dest,
    handoff_len,
    resident_cache,
    resident_len,
    queries,
    new_latent,
    residual_in,
    value_upward,
    out_proj,
    norm_gain,
    expert_ids,
    expert_gates,
    gate_proj,
    up_proj,
    down_proj,
):
    devices = lax.axis_size("ep")
    device = lax.axis_index("ep")
    core = device % 2
    chips = devices // 2
    siblings = [(i, i ^ 1) for i in range(devices)]
    same_core = [[2 * chip + k for chip in range(chips)] for k in range(2)]
    slice_count = MOE_FF // UNITS
    heads, width = queries.shape[2], queries.shape[3]
    per_peer = heads // devices
    model = residual_in.shape[2]

    exchange = functools.partial(
        lax.all_to_all, axis_name="ep", split_axis=0, concat_axis=0, tiled=True
    )
    exchange_core = functools.partial(exchange, axis_index_groups=same_core)

    planes = devices // PLANE
    toward = lambda value, bits: (
        lax.ppermute(value, "ep", [(i, i ^ bits) for i in range(devices)]) if bits else value
    )
    own_device = device.astype(jnp.int32)[None]

    flipped = jnp.swapaxes(queries[0], 1, 2)
    spread_shape = (devices, planes * per_peer, width)
    spread_rows = pl.pallas_call(
        spread_kernel,
        out_shape=pltpu.VMEM(spread_shape, bf16),
        grid=(1,),
        in_specs=[pl.BlockSpec((1, width, heads), lambda step: (1, 0, 0))],
        out_specs=pl.BlockSpec(spread_shape, lambda step: (0, 0, 0)),
        compiler_params=pltpu.CompilerParams(vmem_limit_bytes=32 << 20),
    )(pltpu.with_memory_space_constraint(flipped, pltpu.HBM))
    spread = exchange(spread_rows)

    flipped_keys = jnp.swapaxes(handoff_rows[0], 0, 1)
    plane_keys = [toward(flipped_keys, at) for at in range(PLANE)]
    cache_keys = resident_cache[0]
    cache_live = jnp.arange(cache_keys.shape[0], dtype=jnp.int32) < resident_len[0]
    resident_out = attend(queries[0, 0], cache_keys, cache_live, new_latent[:, 0])
    messages = call(
        column_kernel,
        [((planes * per_peer + FRESH_ROWS, width), bf16)] * PLANE,
        [
            own_device,
            resident_out.reshape(planes, PLANE, per_peer, KVR),
            new_latent[0, 1:2],
        ],
    )
    messages = [toward(message, at) for at, message in enumerate(messages)]

    chunk = max(LANES, KVR // per_peer)
    payloads = call(
        prompt_kernel,
        [((PLANE, 2 * per_peer, KVR + chunk), bf16)] * planes,
        [own_device, handoff_dest, handoff_len, spread, *plane_keys, *messages],
        scratch=[pltpu.VMEM((planes, PLANE, 2 * per_peer, KVR + chunk), bf16)],
    )
    payloads = [toward(payload, at * PLANE) for at, payload in enumerate(payloads)]

    row = jnp.arange(per_peer * 2 * devices, dtype=jnp.int32)
    row_core = (row // devices % 2) ^ core
    row_device = row // 2 % chips * 2 + row_core
    row_table = jnp.stack([row // (2 * devices), row_device, row % 2], axis=1)
    peers = device.astype(jnp.int32) ^ jnp.arange(devices, dtype=jnp.int32)
    is_peer = peers[:, None] == jnp.arange(devices, dtype=jnp.int32)[None, :]
    peer_dest = jnp.sum(jnp.where(is_peer, handoff_dest[None, :], 0), axis=1)
    column = jnp.arange(devices * 2 * per_peer, dtype=jnp.int32)
    column_table = jnp.stack(
        [
            jnp.repeat(peers, 2 * per_peer),
            column % (2 * per_peer),
            jnp.repeat(peer_dest, 2 * per_peer),
        ],
        axis=0,
    )
    projection = out_proj.reshape(-1, model)
    keep, send = call(
        heads_kernel,
        [((devices, model), f32), ((devices, model), bf16)],
        [row_table, column_table, peers[None], *payloads],
        [value_upward, projection],
        [
            pltpu.VMEM(value_upward.shape, bf16),
            pltpu.VMEM(projection.shape, bf16),
            pltpu.VMEM((devices, 2 * per_peer, KVR + chunk), bf16),
            pltpu.SemaphoreType.DMA((1 + model // BLOCK,)),
        ],
    )

    other = lax.ppermute(send, "ep", siblings)
    (pair,) = call(pair_kernel, [((chips, 2, model), bf16)], [keep, other])
    attention = jnp.sum(exchange_core(pair).astype(f32), axis=0)
    hidden = residual_in[0].astype(f32) + attention
    inverse_rms = lax.rsqrt(jnp.mean(hidden * hidden, axis=-1, keepdims=True) + norm_epsilon)
    normed = (hidden * inverse_rms * norm_gain.astype(f32)).astype(bf16)

    own_rows = exchange_core(jnp.broadcast_to(normed[None], (chips, 2, model)))
    experts = []
    for matrix in (gate_proj, up_proj, down_proj):
        experts += [matrix, lax.ppermute(matrix, "ep", siblings)]
    (part,) = call(
        expert_kernel,
        [((chips, 2, model), bf16)],
        [own_rows.reshape(devices, model)],
        experts,
        [pltpu.VMEM((2 * gate_proj.shape[0], model), bf16)] * 3
        + [pltpu.SemaphoreType.DMA((6,))],
    )
    returned = exchange_core(part)

    chip_expert = jnp.arange(chips, dtype=jnp.int32) * 2 // slice_count
    chosen = (expert_ids[0][..., None] == chip_expert).astype(f32)
    weights = jnp.sum(expert_gates[0][..., None] * chosen, axis=1)
    mixed = jnp.sum(weights.T[..., None] * returned.astype(f32), axis=0)
    return (hidden + mixed).astype(bf16)[None]


def solution(mesh):
    placed = (
        P(("groups", "ep"), None, None),
        P("groups"),
        P("groups"),
        P(("groups", "ep"), None, None),
        P(("groups", "ep")),
        P(None, ("groups", "ep"), None, None),
        P(None, ("groups", "ep"), None),
        P(None, ("groups", "ep"), None),
        P("ep", None, None),
        P("ep", None, None),
        P(),
        P(None, ("groups", "ep"), None),
        P(None, ("groups", "ep"), None),
        P("ep", None),
        P("ep", None),
        P("ep", None),
    )
    return jax.shard_map(
        shards,
        mesh=mesh,
        in_specs=placed,
        out_specs=P(None, ("groups", "ep"), None),
        check_vma=False,
    )
```

```python
import functools

import jax
import jax.numpy as jnp
from jax import lax
from jax.experimental import pallas as pl
from jax.experimental.pallas import tpu as pltpu
from jax.sharding import PartitionSpec as P

KVR = 512
MOE_FF = 1024
UNITS = 128
LANES = 128
BLOCK = 1024
PLANE = 4
FRESH_ROWS = 16

softmax_scale = 192.0 ** (-0.5)
norm_epsilon = 1e-06
contract_last = (((1,), (1,)), ((), ()))
f32 = jnp.float32
bf16 = jnp.bfloat16
whole = pl.BlockSpec(memory_space=pltpu.VMEM)
scalars = pl.BlockSpec(memory_space=pltpu.SMEM)


def three_parts(value):
    first = value.astype(bf16).astype(f32)
    second = (value - first).astype(bf16).astype(f32)
    third = value - first - second
    return first, second, third


def spread_kernel(query_hbm, spread_hbm, query_ref, blocks_ref, sems):
    peers, rows, width = spread_hbm.shape
    planes = peers // PLANE
    load = pltpu.make_async_copy(query_hbm.at[1], query_ref, sems.at[0])
    load.start()
    load.wait()
    by_peer = query_ref[...].astype(f32).T.reshape(planes, PLANE, rows // planes, width)
    copies = []
    for column in range(PLANE):
        blocks_ref[column] = by_peer[:, column].reshape(rows, width).astype(bf16)
        for plane in range(planes):
            peer = plane * PLANE + column
            copies.append(
                pltpu.make_async_copy(blocks_ref.at[column], spread_hbm.at[peer], sems.at[1 + peer])
            )
            copies[-1].start()
    for copy in copies:
        copy.wait()


def stage_kernel(after_ref, keys_hbm, staged_hbm, sem):
    del after_ref
    copy = pltpu.make_async_copy(keys_hbm, staged_hbm, sem)
    copy.start()
    copy.wait()


def prefetch_kernel(after_ref, *refs):
    del after_ref
    count = (len(refs) - 1) // 2
    copies = [
        pltpu.make_async_copy(refs[at], refs[count + at], refs[-1].at[at]) for at in range(count)
    ]
    for copy in copies:
        copy.start()
    for copy in copies:
        copy.wait()


def resident_kernel(device_ref, length_ref, fresh_ref, after_ref, query_hbm, cache_hbm, *refs):
    message_refs, (query_ref, cache_ref, mixed_ref, sems) = refs[:-4], refs[-4:]
    del after_ref
    loads = [
        pltpu.make_async_copy(query_hbm.at[0], query_ref, sems.at[0]),
        pltpu.make_async_copy(cache_hbm, cache_ref, sems.at[1]),
    ]
    for load in loads:
        load.start()
    for load in loads:
        load.wait()
    query = query_ref[...].astype(f32).T
    fresh = fresh_ref[0:1].astype(f32)
    scores = jnp.dot(query.astype(bf16), cache_ref[...], preferred_element_type=f32)
    position = lax.broadcasted_iota(jnp.int32, scores.shape, 1)
    scores = jnp.where(position < length_ref[0], scores * softmax_scale, -jnp.inf)
    fresh_score = softmax_scale * jnp.sum(query * fresh, axis=1, keepdims=True)
    peak = jnp.maximum(jnp.max(scores, axis=1, keepdims=True), fresh_score)
    terms = jnp.exp(scores - peak)
    fresh_term = jnp.exp(fresh_score - peak)
    scale = 1.0 / (jnp.sum(terms, axis=1, keepdims=True) + fresh_term)
    mixed = lax.dot_general(
        (terms * scale).astype(bf16), cache_ref[:KVR], contract_last, preferred_element_type=f32
    )
    mixed_ref[...] = (mixed + fresh_term * scale * fresh[:, :KVR]).reshape(mixed_ref.shape)
    planes, _, per_peer, latent = mixed_ref.shape
    rows = planes * per_peer
    column = device_ref[0] % PLANE
    for at, message_ref in enumerate(message_refs):
        message_ref[:rows, :latent] = mixed_ref[:, column ^ at].reshape(rows, latent).astype(bf16)
        message_ref[rows:] = jnp.broadcast_to(fresh_ref[1:2], message_ref[rows:].shape)


def prompt_kernel(device_ref, dest_ref, length_ref, *refs):
    key_refs, message_refs, query_hbm = refs[:PLANE], refs[PLANE : 2 * PLANE], refs[2 * PLANE]
    out_refs, (stage_ref, query_ref, sems) = refs[2 * PLANE + 1 : -3], refs[-3:]
    planes, _, rows, width = stage_ref.shape
    per_peer, chunk = rows // 2, width - KVR
    heads = planes * per_peer
    device = device_ref[0]
    sources = [dest_ref[device ^ at] for at in range(PLANE)] + [device ^ at for at in range(PLANE)]
    loads = [
        pltpu.make_async_copy(query_hbm.at[source], query_ref.at[at], sems.at[at])
        for at, source in enumerate(sources)
    ]
    for load in loads:
        load.start()
    for load in loads:
        load.wait()
    scores = []
    for at in range(PLANE):
        prompt = device ^ at
        query = query_ref[at]
        score = jnp.dot(query, key_refs[at][...], preferred_element_type=f32) * softmax_scale
        position = lax.broadcasted_iota(jnp.int32, score.shape, 1)
        scores.append(jnp.where(position < length_ref[prompt], score, -jnp.inf))
    scores = jnp.concatenate(scores, axis=0)
    peak = jnp.max(scores, axis=1, keepdims=True)
    terms = jnp.exp(scores - peak)
    total = jnp.sum(terms, axis=1, keepdims=True)
    log_sum = peak + jnp.log(total)
    scale = 1.0 / total
    terms = terms.astype(bf16)
    lane = lax.broadcasted_iota(jnp.int32, (heads, chunk), 1)
    fold = lambda value: value.reshape(planes, per_peer, value.shape[1])
    for at in range(PLANE):
        part = slice(at * heads, (at + 1) * heads)
        mixed = lax.dot_general(
            terms[part], key_refs[at][:KVR], contract_last, preferred_element_type=f32
        )
        resident = message_refs[at][:heads, :KVR].astype(f32)
        stage_ref[:, at, :, :KVR] = jnp.concatenate(
            [fold(mixed * scale[part]), fold(resident)], axis=1
        ).astype(bf16)
        fresh = message_refs[at][heads : heads + FRESH_ROWS].astype(f32)[:1]
        fresh_score = softmax_scale * jnp.sum(
            query_ref[PLANE + at].astype(f32) * fresh, axis=1, keepdims=True
        )
        stats = jnp.zeros((heads, chunk), f32)
        for lane_at, value in enumerate(three_parts(log_sum[part]) + three_parts(fresh_score)):
            stats = jnp.where(lane == lane_at, value, stats)
        fresh_rows = [fresh[:, start : start + chunk] for start in range(0, KVR, chunk)]
        if len(fresh_rows) < per_peer:
            fresh_rows.append(jnp.zeros((per_peer - len(fresh_rows), chunk), f32))
        fresh_rows = jnp.concatenate(fresh_rows, axis=0)[None]
        stage_ref[:, at, :, KVR:] = jnp.concatenate(
            [fold(stats), jnp.broadcast_to(fresh_rows, (planes, per_peer, chunk))], axis=1
        ).astype(bf16)
    for at, out_ref in enumerate(out_refs):
        out_ref[...] = stage_ref[(device // PLANE) ^ at]


def pair_kernel(keep_ref, other_ref, pair_ref):
    total = keep_ref[...] + other_ref[...].astype(f32)
    pair_ref[...] = total.reshape(pair_ref.shape).astype(bf16)


def heads_kernel(row_ref, column_ref, peer_ref, upward_ref, proj_ref, *refs):
    payload_refs, (keep_ref, send_ref, rows_ref) = refs[:-3], refs[-3:]
    for at, payload_ref in enumerate(payload_refs):
        rows_ref[at * PLANE : (at + 1) * PLANE] = payload_ref[...]
    peers, rows, width = rows_ref.shape
    per_peer = rows // 2
    columns = peers * rows
    both = 2 * peers
    row_head, row_device, row_new = row_ref[:, 0:1], row_ref[:, 1:2], row_ref[:, 2:3]
    col_peer, col_row, col_dest = column_ref[0:1, :], column_ref[1:2, :], column_ref[2:3, :]
    stats = rows_ref[:, :, KVR : KVR + LANES].astype(f32).reshape(columns, LANES).T
    log_sum = stats[0:1] + stats[1:2] + stats[2:3]
    fresh_score = stats[3:4] + stats[4:5] + stats[5:6]
    same_head = col_row == row_head
    own = col_peer == row_device
    new_row = row_new == 1
    arrives = same_head & (col_dest == row_device) & new_row
    fresh = jnp.sum(jnp.where(same_head & own, fresh_score, 0.0), axis=1, keepdims=True)
    scored = jnp.where(arrives, log_sum, -jnp.inf)
    peak = jnp.maximum(jnp.max(scored, axis=1, keepdims=True), fresh)
    terms = jnp.exp(scored - peak)
    fresh_term = jnp.exp(fresh - peak)
    scale = 1.0 / (jnp.sum(terms, axis=1, keepdims=True) + fresh_term)
    resident = jnp.where(own & (col_row == row_head + per_peer), 1.0, 0.0)
    mixing = jnp.where(new_row, terms * scale, resident)
    fresh_mixing = jnp.where((peer_ref[...] == row_device) & new_row, fresh_term * scale, 0.0)
    chunk = width - KVR
    fresh_rows = jnp.concatenate(
        [rows_ref[:, per_peer + at, KVR:] for at in range(KVR // chunk)], axis=1
    )
    latents = rows_ref[:, :, :KVR].reshape(columns, KVR)
    mixed = jnp.zeros((row_ref.shape[0], KVR), f32)
    for weights, values in ((mixing, latents), (fresh_mixing, fresh_rows)):
        high = weights.astype(bf16)
        low = (weights - high.astype(f32)).astype(bf16)
        mixed = mixed + jnp.dot(high, values, preferred_element_type=f32)
        mixed = mixed + jnp.dot(low, values, preferred_element_type=f32)
    mixed = mixed.astype(bf16)
    value_rows = jnp.concatenate(
        [
            jnp.dot(
                mixed[head * both : (head + 1) * both], upward_ref[head], preferred_element_type=f32
            ).astype(bf16)
            for head in range(per_peer)
        ],
        axis=1,
    )
    for start in range(0, proj_ref.shape[1], BLOCK):
        part = jnp.dot(value_rows, proj_ref[:, start : start + BLOCK], preferred_element_type=f32)
        keep_ref[:, start : start + BLOCK] = part[:peers]
        send_ref[:, start : start + BLOCK] = part[peers:].astype(bf16)


def expert_kernel(rows_ref, *refs):
    out_ref, arrived = refs[6], refs[10]
    gate_ref, up_ref, down_ref = refs[7:10]
    units, model = refs[0].shape
    chips, pair = out_ref.shape[:2]
    first, second = model // 4, model // 2
    steps = [(range(4), start, first) for start in range(0, model, first)]
    steps += [(range(4, 6), start, second) for start in range(0, model, second)]
    copies = []
    for matrices, start, size in steps:
        copies.append([])
        for at in matrices:
            place = refs[7 + at // 2].at[pl.ds(at % 2 * units, units), pl.ds(start, size)]
            sem = arrived.at[sum(map(len, copies))]
            copies[-1].append(
                pltpu.make_async_copy(refs[at].at[:, pl.ds(start, size)], place, sem)
            )
            copies[-1][-1].start()
    gate = up_value = jnp.zeros((rows_ref.shape[0], 2 * units), f32)
    for step, (matrices, start, size) in enumerate(steps):
        for copy in copies[step]:
            copy.wait()
        columns = slice(start, start + size)
        if size == first:
            rows = rows_ref[:, columns]
            gate += lax.dot_general(
                rows, gate_ref[:, columns], contract_last, preferred_element_type=f32
            )
            up_value += lax.dot_general(
                rows, up_ref[:, columns], contract_last, preferred_element_type=f32
            )
        else:
            act = (gate / (1.0 + jnp.exp(-gate)) * up_value).astype(bf16)
            part = jnp.dot(act, down_ref[:, columns], preferred_element_type=f32)
            out_ref[:, :, columns] = part.reshape(chips, pair, size).astype(bf16)


def near(value):
    return pltpu.with_memory_space_constraint(value, pltpu.VMEM)


def call(kernel, outputs, operands, far=(), scratch=(), cost=None):
    specs = [scalars if operand.ndim == 1 else whole for operand in operands]
    return pl.pallas_call(
        kernel,
        out_shape=[pltpu.VMEM(shape, dtype) for shape, dtype in outputs],
        in_specs=specs + [pl.BlockSpec(memory_space=pl.ANY)] * len(far),
        out_specs=[whole] * len(outputs),
        scratch_shapes=scratch,
        compiler_params=pltpu.CompilerParams(vmem_limit_bytes=32 << 20),
        cost_estimate=cost,
    )(
        *[operand if operand.ndim == 1 else near(operand) for operand in operands],
        *[pltpu.with_memory_space_constraint(operand, pltpu.HBM) for operand in far],
    )


def call_far(kernel, shapes, operands, scratch, cost=None):
    far = pl.BlockSpec(memory_space=pltpu.HBM)
    return pl.pallas_call(
        kernel,
        out_shape=shapes,
        in_specs=[far] * len(operands),
        out_specs=jax.tree.map(lambda _: far, shapes),
        scratch_shapes=scratch,
        compiler_params=pltpu.CompilerParams(vmem_limit_bytes=16 << 20),
        cost_estimate=cost,
    )(*operands)


def prefetch(after, weights):
    return pl.pallas_call(
        prefetch_kernel,
        out_shape=[pltpu.VMEM(weight.shape, weight.dtype) for weight in weights],
        in_specs=[pl.BlockSpec(memory_space=pl.ANY)] * (1 + len(weights)),
        out_specs=[whole] * len(weights),
        scratch_shapes=[pltpu.SemaphoreType.DMA((len(weights),))],
        compiler_params=pltpu.CompilerParams(vmem_limit_bytes=16 << 20),
    )(after, *[pltpu.with_memory_space_constraint(weight, pltpu.HBM) for weight in weights])


def shards(
    handoff_rows,
    handoff_dest,
    handoff_len,
    resident_cache,
    resident_len,
    queries,
    new_latent,
    residual_in,
    value_upward,
    out_proj,
    norm_gain,
    expert_ids,
    expert_gates,
    gate_proj,
    up_proj,
    down_proj,
):
    devices = lax.axis_size("ep")
    device = lax.axis_index("ep")
    core = device % 2
    chips = devices // 2
    siblings = [(i, i ^ 1) for i in range(devices)]
    same_core = [[2 * chip + k for chip in range(chips)] for k in range(2)]
    slice_count = MOE_FF // UNITS
    heads, width = queries.shape[2], queries.shape[3]
    per_peer = heads // devices
    model = residual_in.shape[2]

    exchange = functools.partial(
        lax.all_to_all, axis_name="ep", split_axis=0, concat_axis=0, tiled=True
    )
    exchange_core = functools.partial(exchange, axis_index_groups=same_core)

    planes = devices // PLANE
    toward = lambda value, bits: (
        lax.ppermute(value, "ep", [(i, i ^ bits) for i in range(devices)]) if bits else value
    )
    own_device = device.astype(jnp.int32)[None]

    flipped = jnp.swapaxes(queries[0], 1, 2)
    spread_shape = (devices, planes * per_peer, width)
    spread_rows = call_far(
        spread_kernel,
        jax.ShapeDtypeStruct(spread_shape, bf16),
        [flipped],
        [
            pltpu.VMEM((width, heads), bf16),
            pltpu.VMEM((PLANE, *spread_shape[1:]), bf16),
            pltpu.SemaphoreType.DMA((1 + devices,)),
        ],
    )
    spread = exchange(spread_rows)

    short = pl.CostEstimate(flops=1, bytes_accessed=1, transcendentals=0)
    flipped_keys = jnp.swapaxes(handoff_rows[0], 0, 1)
    staged_keys = call_far(
        stage_kernel,
        jax.ShapeDtypeStruct(flipped_keys.shape, bf16),
        [spread_rows, flipped_keys],
        [pltpu.SemaphoreType.DMA],
        short,
    )
    plane_keys = [staged_keys]
    bit = PLANE // 2
    while bit:
        crossing = [toward(keys, bit) for keys in plane_keys]
        plane_keys = [keys for pair in zip(plane_keys, crossing) for keys in pair]
        bit //= 2
    flipped_cache = jnp.swapaxes(resident_cache[0], 0, 1)
    messages = call(
        resident_kernel,
        [((planes * per_peer + FRESH_ROWS, width), bf16)] * PLANE,
        [own_device, resident_len, new_latent[0]],
        [spread_rows, flipped, flipped_cache],
        [
            pltpu.VMEM((width, heads), bf16),
            pltpu.VMEM(flipped_cache.shape, bf16),
            pltpu.VMEM((planes, PLANE, per_peer, KVR), f32),
            pltpu.SemaphoreType.DMA((2,)),
        ],
        short,
    )
    messages = [toward(message, at) for at, message in enumerate(messages)]

    chunk = max(LANES, KVR // per_peer)
    payloads = call(
        prompt_kernel,
        [((PLANE, 2 * per_peer, KVR + chunk), bf16)] * planes,
        [own_device, handoff_dest, handoff_len, *plane_keys, *messages],
        [spread],
        [
            pltpu.VMEM((planes, PLANE, 2 * per_peer, KVR + chunk), bf16),
            pltpu.VMEM((2 * PLANE, *spread_shape[1:]), bf16),
            pltpu.SemaphoreType.DMA((2 * PLANE,)),
        ],
    )
    upward, projection = prefetch(payloads[0], [value_upward, out_proj.reshape(-1, model)])
    payloads = [toward(payload, at * PLANE) for at, payload in enumerate(payloads)]

    row = jnp.arange(per_peer * 2 * devices, dtype=jnp.int32)
    row_core = (row // devices % 2) ^ core
    row_device = row // 2 % chips * 2 + row_core
    row_table = jnp.stack([row // (2 * devices), row_device, row % 2], axis=1)
    peers = device.astype(jnp.int32) ^ jnp.arange(devices, dtype=jnp.int32)
    is_peer = peers[:, None] == jnp.arange(devices, dtype=jnp.int32)[None, :]
    peer_dest = jnp.sum(jnp.where(is_peer, handoff_dest[None, :], 0), axis=1)
    column = jnp.arange(devices * 2 * per_peer, dtype=jnp.int32)
    column_table = jnp.stack(
        [
            jnp.repeat(peers, 2 * per_peer),
            column % (2 * per_peer),
            jnp.repeat(peer_dest, 2 * per_peer),
        ],
        axis=0,
    )
    keep, send = call(
        heads_kernel,
        [((devices, model), f32), ((devices, model), bf16)],
        [row_table, column_table, peers[None], upward, projection, *payloads],
        scratch=[pltpu.VMEM((devices, 2 * per_peer, KVR + chunk), bf16)],
    )

    other = lax.ppermute(send, "ep", siblings)
    (pair,) = call(pair_kernel, [((chips, 2, model), bf16)], [keep, other])
    attention = jnp.sum(exchange_core(pair).astype(f32), axis=0)
    hidden = residual_in[0].astype(f32) + attention
    inverse_rms = lax.rsqrt(jnp.mean(hidden * hidden, axis=-1, keepdims=True) + norm_epsilon)
    normed = (hidden * inverse_rms * norm_gain.astype(f32)).astype(bf16)

    own_rows = exchange_core(jnp.broadcast_to(normed[None], (chips, 2, model)))
    experts = []
    for matrix in (gate_proj, up_proj, down_proj):
        experts += [matrix, lax.ppermute(matrix, "ep", siblings)]
    (part,) = call(
        expert_kernel,
        [((chips, 2, model), bf16)],
        [own_rows.reshape(devices, model)],
        experts,
        [pltpu.VMEM((2 * gate_proj.shape[0], model), bf16)] * 3
        + [pltpu.SemaphoreType.DMA((20,))],
    )
    returned = exchange_core(part)

    chip_expert = jnp.arange(chips, dtype=jnp.int32) * 2 // slice_count
    chosen = (expert_ids[0][..., None] == chip_expert).astype(f32)
    weights = jnp.sum(expert_gates[0][..., None] * chosen, axis=1)
    mixed = jnp.sum(weights.T[..., None] * returned.astype(f32), axis=0)
    return (hidden + mixed).astype(bf16)[None]


def solution(mesh):
    placed = (
        P(("groups", "ep"), None, None),
        P("groups"),
        P("groups"),
        P(("groups", "ep"), None, None),
        P(("groups", "ep")),
        P(None, ("groups", "ep"), None, None),
        P(None, ("groups", "ep"), None),
        P(None, ("groups", "ep"), None),
        P("ep", None, None),
        P("ep", None, None),
        P(),
        P(None, ("groups", "ep"), None),
        P(None, ("groups", "ep"), None),
        P("ep", None),
        P("ep", None),
        P("ep", None),
    )
    return jax.shard_map(
        shards,
        mesh=mesh,
        in_specs=placed,
        out_specs=P(None, ("groups", "ep"), None),
        check_vma=False,
    )
```

```python
import functools

import jax
import jax.numpy as jnp
from jax import lax
from jax.experimental import pallas as pl
from jax.experimental.pallas import tpu as pltpu
from jax.sharding import PartitionSpec as P

KVR = 512
MOE_FF = 1024
UNITS = 128
LANES = 128
BLOCK = 1024
PLANE = 4
FRESH_ROWS = 16

softmax_scale = 192.0 ** (-0.5)
norm_epsilon = 1e-06
contract_last = (((1,), (1,)), ((), ()))
f32 = jnp.float32
bf16 = jnp.bfloat16
whole = pl.BlockSpec(memory_space=pltpu.VMEM)
scalars = pl.BlockSpec(memory_space=pltpu.SMEM)


def three_parts(value):
    first = value.astype(bf16).astype(f32)
    second = (value - first).astype(bf16).astype(f32)
    third = value - first - second
    return first, second, third


def pack(rows):
    heads, width = rows.shape
    tail = width - KVR
    beside = LANES // tail
    high = heads // beside
    pieces = [rows[:, start : start + LANES] for start in range(0, KVR, LANES)]
    pieces.append(
        jnp.concatenate([rows[at * high : (at + 1) * high, KVR:] for at in range(beside)], axis=1)
    )
    return jnp.concatenate(pieces, axis=0)


def unpack(packed, heads, tail):
    pieces = [packed[at * heads : (at + 1) * heads] for at in range(KVR // LANES)]
    rest = packed[heads * (KVR // LANES) :]
    tails = [rest[:, start : start + tail] for start in range(0, LANES, tail)]
    return jnp.concatenate(pieces, axis=1), jnp.concatenate(tails, axis=0)


def spread_kernel(query_hbm, spread_hbm, query_ref, blocks_ref, sems):
    peers = spread_hbm.shape[0]
    planes = peers // PLANE
    width, heads = query_ref.shape
    load = pltpu.make_async_copy(query_hbm.at[1], query_ref, sems.at[0])
    load.start()
    load.wait()
    by_peer = query_ref[...].astype(f32).T.reshape(planes, PLANE, heads // peers, width)
    copies = []
    for column in range(PLANE):
        rows = by_peer[:, column].reshape(heads // PLANE, width)
        blocks_ref[column] = pack(rows).astype(bf16)
        for plane in range(planes):
            peer = plane * PLANE + column
            copies.append(
                pltpu.make_async_copy(blocks_ref.at[column], spread_hbm.at[peer], sems.at[1 + peer])
            )
            copies[-1].start()
    for copy in copies:
        copy.wait()


def prefetch_kernel(after_ref, *refs):
    del after_ref
    count = (len(refs) - 1) // 2
    copies = [
        pltpu.make_async_copy(refs[at], refs[count + at], refs[-1].at[at]) for at in range(count)
    ]
    for copy in copies:
        copy.start()
    for copy in copies:
        copy.wait()


def resident_kernel(device_ref, length_ref, fresh_ref, after_ref, query_hbm, cache_hbm, *refs):
    message_refs, (query_ref, cache_ref, mixed_ref, sems) = refs[:-4], refs[-4:]
    del after_ref
    loads = [
        pltpu.make_async_copy(query_hbm.at[0], query_ref, sems.at[0]),
        pltpu.make_async_copy(cache_hbm, cache_ref, sems.at[1]),
    ]
    for load in loads:
        load.start()
    for load in loads:
        load.wait()
    query = query_ref[...].astype(f32).T
    fresh = fresh_ref[0:1].astype(f32)
    scores = jnp.dot(query.astype(bf16), cache_ref[...], preferred_element_type=f32)
    position = lax.broadcasted_iota(jnp.int32, scores.shape, 1)
    scores = jnp.where(position < length_ref[0], scores * softmax_scale, -jnp.inf)
    fresh_score = softmax_scale * jnp.sum(query * fresh, axis=1, keepdims=True)
    peak = jnp.maximum(jnp.max(scores, axis=1, keepdims=True), fresh_score)
    terms = jnp.exp(scores - peak)
    fresh_term = jnp.exp(fresh_score - peak)
    scale = 1.0 / (jnp.sum(terms, axis=1, keepdims=True) + fresh_term)
    mixed = lax.dot_general(
        (terms * scale).astype(bf16), cache_ref[:KVR], contract_last, preferred_element_type=f32
    )
    mixed_ref[...] = (mixed + fresh_term * scale * fresh[:, :KVR]).reshape(mixed_ref.shape)
    planes, _, per_peer, latent = mixed_ref.shape
    rows = planes * per_peer
    column = device_ref[0] % PLANE
    new_key = fresh_ref[1:2].astype(f32)
    rest = jnp.concatenate(
        [new_key[:, KVR:], jnp.zeros((1, 2 * KVR - new_key.shape[1]), f32)], axis=1
    )
    line = lax.broadcasted_iota(jnp.int32, (FRESH_ROWS, KVR), 0)
    key_rows = jnp.where(line == 0, new_key[:, :KVR], jnp.where(line == 1, rest, 0.0)).astype(bf16)
    for at, message_ref in enumerate(message_refs):
        message_ref[:rows] = mixed_ref[:, column ^ at].reshape(rows, latent).astype(bf16)
        message_ref[rows:] = key_rows


def prompt_kernel(device_ref, dest_ref, length_ref, *refs):
    key_refs, message_refs, query_hbm = refs[:PLANE], refs[PLANE : 2 * PLANE], refs[2 * PLANE]
    out_refs, (stage_ref, query_ref, sems) = refs[2 * PLANE + 1 : -3], refs[-3:]
    planes, _, rows, width = stage_ref.shape
    per_peer, chunk = rows // 2, width - KVR
    heads = planes * per_peer
    tail = key_refs[0].shape[0] - KVR
    device = device_ref[0]
    sources = [dest_ref[device ^ at] for at in range(PLANE)] + [device ^ at for at in range(PLANE)]
    loads = [
        pltpu.make_async_copy(query_hbm.at[source], query_ref.at[at], sems.at[at])
        for at, source in enumerate(sources)
    ]
    for load in loads:
        load.start()
    for load in loads:
        load.wait()
    scores = []
    for at in range(PLANE):
        prompt = device ^ at
        latent, rest = unpack(query_ref[at], heads, tail)
        score = jnp.dot(latent, key_refs[at][:KVR], preferred_element_type=f32)
        score += jnp.dot(rest, key_refs[at][KVR:], preferred_element_type=f32)
        score *= softmax_scale
        position = lax.broadcasted_iota(jnp.int32, score.shape, 1)
        scores.append(jnp.where(position < length_ref[prompt], score, -jnp.inf))
    scores = jnp.concatenate(scores, axis=0)
    peak = jnp.max(scores, axis=1, keepdims=True)
    terms = jnp.exp(scores - peak)
    total = jnp.sum(terms, axis=1, keepdims=True)
    log_sum = peak + jnp.log(total)
    scale = 1.0 / total
    terms = terms.astype(bf16)
    lane = lax.broadcasted_iota(jnp.int32, (heads, chunk), 1)
    fold = lambda value: value.reshape(planes, per_peer, value.shape[1])
    for at in range(PLANE):
        part = slice(at * heads, (at + 1) * heads)
        mixed = lax.dot_general(
            terms[part], key_refs[at][:KVR], contract_last, preferred_element_type=f32
        )
        resident = message_refs[at][:heads, :KVR].astype(f32)
        stage_ref[:, at, :, :KVR] = jnp.concatenate(
            [fold(mixed * scale[part]), fold(resident)], axis=1
        ).astype(bf16)
        fresh = message_refs[at][heads : heads + FRESH_ROWS].astype(f32)
        fresh, fresh_rest = fresh[0:1], fresh[1:2, :tail]
        latent, rest = unpack(query_ref[PLANE + at], heads, tail)
        fresh_score = softmax_scale * (
            jnp.sum(latent.astype(f32) * fresh, axis=1, keepdims=True)
            + jnp.sum(rest.astype(f32) * fresh_rest, axis=1, keepdims=True)
        )
        stats = jnp.zeros((heads, chunk), f32)
        for lane_at, value in enumerate(three_parts(log_sum[part]) + three_parts(fresh_score)):
            stats = jnp.where(lane == lane_at, value, stats)
        fresh_rows = [fresh[:, start : start + chunk] for start in range(0, KVR, chunk)]
        if len(fresh_rows) < per_peer:
            fresh_rows.append(jnp.zeros((per_peer - len(fresh_rows), chunk), f32))
        fresh_rows = jnp.concatenate(fresh_rows, axis=0)[None]
        stage_ref[:, at, :, KVR:] = jnp.concatenate(
            [fold(stats), jnp.broadcast_to(fresh_rows, (planes, per_peer, chunk))], axis=1
        ).astype(bf16)
    for at, out_ref in enumerate(out_refs):
        out_ref[...] = stage_ref[(device // PLANE) ^ at]


def pair_kernel(keep_ref, other_ref, pair_ref):
    pair_ref[...] = (keep_ref[...] + other_ref[...].astype(f32)).astype(bf16)


def heads_kernel(row_ref, column_ref, peer_ref, upward_ref, proj_ref, *refs):
    payload_refs, (keep_ref, send_ref, rows_ref) = refs[:-3], refs[-3:]
    for at, payload_ref in enumerate(payload_refs):
        rows_ref[at * PLANE : (at + 1) * PLANE] = payload_ref[...]
    peers, rows, width = rows_ref.shape
    per_peer = rows // 2
    columns = peers * rows
    both = 2 * peers
    row_head, row_device, row_new = row_ref[:, 0:1], row_ref[:, 1:2], row_ref[:, 2:3]
    col_peer, col_row, col_dest = column_ref[0:1, :], column_ref[1:2, :], column_ref[2:3, :]
    stats = rows_ref[:, :, KVR : KVR + LANES].astype(f32).reshape(columns, LANES).T
    log_sum = stats[0:1] + stats[1:2] + stats[2:3]
    fresh_score = stats[3:4] + stats[4:5] + stats[5:6]
    same_head = col_row == row_head
    own = col_peer == row_device
    new_row = row_new == 1
    arrives = same_head & (col_dest == row_device) & new_row
    fresh = jnp.sum(jnp.where(same_head & own, fresh_score, 0.0), axis=1, keepdims=True)
    scored = jnp.where(arrives, log_sum, -jnp.inf)
    peak = jnp.maximum(jnp.max(scored, axis=1, keepdims=True), fresh)
    terms = jnp.exp(scored - peak)
    fresh_term = jnp.exp(fresh - peak)
    scale = 1.0 / (jnp.sum(terms, axis=1, keepdims=True) + fresh_term)
    resident = jnp.where(own & (col_row == row_head + per_peer), 1.0, 0.0)
    mixing = jnp.where(new_row, terms * scale, resident)
    fresh_mixing = jnp.where((peer_ref[...] == row_device) & new_row, fresh_term * scale, 0.0)
    chunk = width - KVR
    fresh_rows = jnp.concatenate(
        [rows_ref[:, per_peer + at, KVR:] for at in range(KVR // chunk)], axis=1
    )
    latents = rows_ref[:, :, :KVR].reshape(columns, KVR)
    mixed = jnp.zeros((row_ref.shape[0], KVR), f32)
    for weights, values in ((mixing, latents), (fresh_mixing, fresh_rows)):
        high = weights.astype(bf16)
        low = (weights - high.astype(f32)).astype(bf16)
        mixed = mixed + jnp.dot(high, values, preferred_element_type=f32)
        mixed = mixed + jnp.dot(low, values, preferred_element_type=f32)
    mixed = mixed.astype(bf16)
    value_rows = jnp.concatenate(
        [
            jnp.dot(
                mixed[head * both : (head + 1) * both], upward_ref[head], preferred_element_type=f32
            ).astype(bf16)
            for head in range(per_peer)
        ],
        axis=1,
    )
    for start in range(0, proj_ref.shape[1], BLOCK):
        part = jnp.dot(value_rows, proj_ref[:, start : start + BLOCK], preferred_element_type=f32)
        columns = slice(start, start + BLOCK)
        keep_ref[:, :, columns] = part[:peers].reshape(peers // 2, 2, BLOCK)
        send_ref[:, :, columns] = part[peers:].reshape(peers // 2, 2, BLOCK).astype(bf16)


def expert_kernel(rows_ref, *refs):
    out_ref, arrived = refs[6], refs[10]
    gate_ref, up_ref, down_ref = refs[7:10]
    units, model = refs[0].shape
    chips, pair = out_ref.shape[:2]
    first, second = model // 4, model // 2
    steps = [(range(4), start, first) for start in range(0, model, first)]
    steps += [(range(4, 6), start, second) for start in range(0, model, second)]
    copies = []
    for matrices, start, size in steps:
        copies.append([])
        for at in matrices:
            place = refs[7 + at // 2].at[pl.ds(at % 2 * units, units), pl.ds(start, size)]
            sem = arrived.at[sum(map(len, copies))]
            copies[-1].append(
                pltpu.make_async_copy(refs[at].at[:, pl.ds(start, size)], place, sem)
            )
            copies[-1][-1].start()
    gate = up_value = jnp.zeros((rows_ref.shape[0], 2 * units), f32)
    for step, (matrices, start, size) in enumerate(steps):
        for copy in copies[step]:
            copy.wait()
        columns = slice(start, start + size)
        if size == first:
            rows = rows_ref[:, columns]
            gate += lax.dot_general(
                rows, gate_ref[:, columns], contract_last, preferred_element_type=f32
            )
            up_value += lax.dot_general(
                rows, up_ref[:, columns], contract_last, preferred_element_type=f32
            )
        else:
            act = (gate / (1.0 + jnp.exp(-gate)) * up_value).astype(bf16)
            part = jnp.dot(act, down_ref[:, columns], preferred_element_type=f32)
            out_ref[:, :, columns] = part.reshape(chips, pair, size).astype(bf16)


def near(value):
    return pltpu.with_memory_space_constraint(value, pltpu.VMEM)


def distant(value):
    return pltpu.with_memory_space_constraint(value, pltpu.HBM)


def call(kernel, outputs, operands, far=(), scratch=(), cost=None):
    specs = [scalars if operand.ndim == 1 else whole for operand in operands]
    return pl.pallas_call(
        kernel,
        out_shape=[pltpu.VMEM(shape, dtype) for shape, dtype in outputs],
        in_specs=specs + [pl.BlockSpec(memory_space=pl.ANY)] * len(far),
        out_specs=[whole] * len(outputs),
        scratch_shapes=scratch,
        compiler_params=pltpu.CompilerParams(vmem_limit_bytes=32 << 20),
        cost_estimate=cost,
    )(
        *[operand if operand.ndim == 1 else near(operand) for operand in operands],
        *far,
    )


def call_far(kernel, shapes, operands, scratch, cost=None):
    far = pl.BlockSpec(memory_space=pltpu.HBM)
    return pl.pallas_call(
        kernel,
        out_shape=shapes,
        in_specs=[far] * len(operands),
        out_specs=jax.tree.map(lambda _: far, shapes),
        scratch_shapes=scratch,
        compiler_params=pltpu.CompilerParams(vmem_limit_bytes=16 << 20),
        cost_estimate=cost,
    )(*map(distant, operands))


def prefetch(after, weights):
    return pl.pallas_call(
        prefetch_kernel,
        out_shape=[pltpu.VMEM(weight.shape, weight.dtype) for weight in weights],
        in_specs=[pl.BlockSpec(memory_space=pl.ANY)] * (1 + len(weights)),
        out_specs=[whole] * len(weights),
        scratch_shapes=[pltpu.SemaphoreType.DMA((len(weights),))],
        compiler_params=pltpu.CompilerParams(vmem_limit_bytes=16 << 20),
    )(after, *map(distant, weights))


def shards(
    handoff_rows,
    handoff_dest,
    handoff_len,
    resident_cache,
    resident_len,
    queries,
    new_latent,
    residual_in,
    value_upward,
    out_proj,
    norm_gain,
    expert_ids,
    expert_gates,
    gate_proj,
    up_proj,
    down_proj,
):
    devices = lax.axis_size("ep")
    device = lax.axis_index("ep")
    core = device % 2
    chips = devices // 2
    siblings = [(i, i ^ 1) for i in range(devices)]
    same_core = [[2 * chip + k for chip in range(chips)] for k in range(2)]
    slice_count = MOE_FF // UNITS
    heads, width = queries.shape[2], queries.shape[3]
    per_peer = heads // devices
    model = residual_in.shape[2]

    exchange = functools.partial(
        lax.all_to_all, axis_name="ep", split_axis=0, concat_axis=0, tiled=True
    )
    exchange_core = functools.partial(exchange, axis_index_groups=same_core)

    planes = devices // PLANE
    toward = lambda value, bits: (
        lax.ppermute(value, "ep", [(i, i ^ bits) for i in range(devices)]) if bits else value
    )
    own_device = device.astype(jnp.int32)[None]

    flipped = jnp.swapaxes(queries[0], 1, 2)
    spread_shape = (devices, heads // PLANE * width // LANES, LANES)
    spread_rows = call_far(
        spread_kernel,
        jax.ShapeDtypeStruct(spread_shape, bf16),
        [flipped],
        [
            pltpu.VMEM((width, heads), bf16),
            pltpu.VMEM((PLANE, *spread_shape[1:]), bf16),
            pltpu.SemaphoreType.DMA((1 + devices,)),
        ],
    )
    spread = exchange(spread_rows)

    short = pl.CostEstimate(flops=1, bytes_accessed=1, transcendentals=0)
    flipped_keys = jnp.swapaxes(handoff_rows[0], 0, 1)
    plane_keys = [flipped_keys]
    bit = PLANE // 2
    while bit:
        crossing = [toward(keys, bit) for keys in plane_keys]
        plane_keys = [keys for pair in zip(plane_keys, crossing) for keys in pair]
        bit //= 2
    flipped_cache = jnp.swapaxes(resident_cache[0], 0, 1)
    messages = call(
        resident_kernel,
        [((planes * per_peer + FRESH_ROWS, KVR), bf16)] * PLANE,
        [own_device, resident_len, new_latent[0]],
        [spread_rows, distant(flipped), distant(flipped_cache)],
        [
            pltpu.VMEM((width, heads), bf16),
            pltpu.VMEM(flipped_cache.shape, bf16),
            pltpu.VMEM((planes, PLANE, per_peer, KVR), f32),
            pltpu.SemaphoreType.DMA((2,)),
        ],
        short,
    )
    messages = [toward(message, at) for at, message in enumerate(messages)]

    chunk = max(LANES, KVR // per_peer)
    payloads = call(
        prompt_kernel,
        [((PLANE, 2 * per_peer, KVR + chunk), bf16)] * planes,
        [own_device, handoff_dest, handoff_len, *plane_keys, *messages],
        [spread],
        [
            pltpu.VMEM((planes, PLANE, 2 * per_peer, KVR + chunk), bf16),
            pltpu.VMEM((2 * PLANE, *spread_shape[1:]), bf16),
            pltpu.SemaphoreType.DMA((2 * PLANE,)),
        ],
    )
    upward, projection = prefetch(payloads[0], [value_upward, out_proj.reshape(-1, model)])
    payloads = [toward(payload, at * PLANE) for at, payload in enumerate(payloads)]

    row = jnp.arange(per_peer * 2 * devices, dtype=jnp.int32)
    row_core = (row // devices % 2) ^ core
    row_device = row // 2 % chips * 2 + row_core
    row_table = jnp.stack([row // (2 * devices), row_device, row % 2], axis=1)
    peers = device.astype(jnp.int32) ^ jnp.arange(devices, dtype=jnp.int32)
    is_peer = peers[:, None] == jnp.arange(devices, dtype=jnp.int32)[None, :]
    peer_dest = jnp.sum(jnp.where(is_peer, handoff_dest[None, :], 0), axis=1)
    column = jnp.arange(devices * 2 * per_peer, dtype=jnp.int32)
    column_table = jnp.stack(
        [
            jnp.repeat(peers, 2 * per_peer),
            column % (2 * per_peer),
            jnp.repeat(peer_dest, 2 * per_peer),
        ],
        axis=0,
    )
    keep, send = call(
        heads_kernel,
        [((chips, 2, model), f32), ((chips, 2, model), bf16)],
        [row_table, column_table, peers[None], upward, projection, *payloads],
        scratch=[pltpu.VMEM((devices, 2 * per_peer, KVR + chunk), bf16)],
    )

    other = lax.ppermute(send, "ep", siblings)
    (pair,) = call(pair_kernel, [((chips, 2, model), bf16)], [keep, other])
    attention = jnp.sum(exchange_core(pair).astype(f32), axis=0)
    hidden = residual_in[0].astype(f32) + attention
    inverse_rms = lax.rsqrt(jnp.mean(hidden * hidden, axis=-1, keepdims=True) + norm_epsilon)
    normed = (hidden * inverse_rms * norm_gain.astype(f32)).astype(bf16)

    own_rows = exchange_core(jnp.broadcast_to(normed[None], (chips, 2, model)))
    experts = []
    for matrix in (gate_proj, up_proj, down_proj):
        experts += [matrix, lax.ppermute(matrix, "ep", siblings)]
    (part,) = call(
        expert_kernel,
        [((chips, 2, model), bf16)],
        [own_rows.reshape(devices, model)],
        [matrix if at == 1 else distant(matrix) for at, matrix in enumerate(experts)],
        [pltpu.VMEM((2 * gate_proj.shape[0], model), bf16)] * 3
        + [pltpu.SemaphoreType.DMA((20,))],
    )
    returned = exchange_core(part)

    chip_expert = jnp.arange(chips, dtype=jnp.int32) * 2 // slice_count
    chosen = (expert_ids[0][..., None] == chip_expert).astype(f32)
    weights = jnp.sum(expert_gates[0][..., None] * chosen, axis=1)
    mixed = jnp.sum(weights.T[..., None] * returned.astype(f32), axis=0)
    return (hidden + mixed).astype(bf16)[None]


def solution(mesh):
    placed = (
        P(("groups", "ep"), None, None),
        P("groups"),
        P("groups"),
        P(("groups", "ep"), None, None),
        P(("groups", "ep")),
        P(None, ("groups", "ep"), None, None),
        P(None, ("groups", "ep"), None),
        P(None, ("groups", "ep"), None),
        P("ep", None, None),
        P("ep", None, None),
        P(),
        P(None, ("groups", "ep"), None),
        P(None, ("groups", "ep"), None),
        P("ep", None),
        P("ep", None),
        P("ep", None),
    )
    return jax.shard_map(
        shards,
        mesh=mesh,
        in_specs=placed,
        out_specs=P(None, ("groups", "ep"), None),
        check_vma=False,
    )
```

```python
import functools

import jax
import jax.numpy as jnp
from jax import lax
from jax.experimental import pallas as pl
from jax.experimental.pallas import tpu as pltpu
from jax.sharding import PartitionSpec as P

KVR = 512
MOE_FF = 1024
UNITS = 128
LANES = 128
BLOCK = 1024
PLANE = 4
FRESH_ROWS = 16

softmax_scale = 192.0 ** (-0.5)
norm_epsilon = 1e-06
contract_last = (((1,), (1,)), ((), ()))
f32 = jnp.float32
bf16 = jnp.bfloat16
whole = pl.BlockSpec(memory_space=pltpu.VMEM)
scalars = pl.BlockSpec(memory_space=pltpu.SMEM)


def three_parts(value):
    first = value.astype(bf16).astype(f32)
    second = (value - first).astype(bf16).astype(f32)
    third = value - first - second
    return first, second, third


def pack(rows):
    heads, width = rows.shape
    tail = width - KVR
    beside = LANES // tail
    high = heads // beside
    pieces = [rows[:, start : start + LANES] for start in range(0, KVR, LANES)]
    pieces.append(
        jnp.concatenate([rows[at * high : (at + 1) * high, KVR:] for at in range(beside)], axis=1)
    )
    return jnp.concatenate(pieces, axis=0)


def unpack(packed, heads, tail):
    pieces = [packed[at * heads : (at + 1) * heads] for at in range(KVR // LANES)]
    rest = packed[heads * (KVR // LANES) :]
    tails = [rest[:, start : start + tail] for start in range(0, LANES, tail)]
    return jnp.concatenate(pieces, axis=1), jnp.concatenate(tails, axis=0)


def spread_kernel(slots, query_hbm, spread_hbm, query_ref, blocks_ref, sems):
    peers = spread_hbm.shape[0]
    planes = peers // PLANE
    width, heads = query_ref.shape
    load = pltpu.make_async_copy(query_hbm.at[1], query_ref, sems.at[0])
    load.start()
    load.wait()
    by_peer = query_ref[...].astype(f32).T.reshape(planes, PLANE, heads // peers, width)
    copies = []
    for column in range(PLANE):
        rows = by_peer[:, column].reshape(heads // PLANE, width)
        blocks_ref[column] = pack(rows).astype(bf16)
        for plane in range(planes):
            peer = slots[plane * PLANE + column]
            copies.append(
                pltpu.make_async_copy(blocks_ref.at[column], spread_hbm.at[peer], sems.at[1 + peer])
            )
            copies[-1].start()
    for copy in copies:
        copy.wait()


def prefetch_kernel(after_ref, *refs):
    del after_ref
    count = (len(refs) - 1) // 2
    copies = [
        pltpu.make_async_copy(refs[at], refs[count + at], refs[-1].at[at]) for at in range(count)
    ]
    for copy in copies:
        copy.start()
    for copy in copies:
        copy.wait()


def resident_kernel(device_ref, length_ref, fresh_ref, after_ref, query_hbm, cache_hbm, *refs):
    message_refs, (query_ref, cache_ref, mixed_ref, sems) = refs[:-4], refs[-4:]
    del after_ref
    loads = [
        pltpu.make_async_copy(query_hbm.at[0], query_ref, sems.at[0]),
        pltpu.make_async_copy(cache_hbm, cache_ref, sems.at[1]),
    ]
    for load in loads:
        load.start()
    for load in loads:
        load.wait()
    query = query_ref[...].astype(f32).T
    fresh = fresh_ref[0:1].astype(f32)
    scores = jnp.dot(query.astype(bf16), cache_ref[...], preferred_element_type=f32)
    position = lax.broadcasted_iota(jnp.int32, scores.shape, 1)
    scores = jnp.where(position < length_ref[0], scores * softmax_scale, -jnp.inf)
    fresh_score = softmax_scale * jnp.sum(query * fresh, axis=1, keepdims=True)
    peak = jnp.maximum(jnp.max(scores, axis=1, keepdims=True), fresh_score)
    terms = jnp.exp(scores - peak)
    fresh_term = jnp.exp(fresh_score - peak)
    scale = 1.0 / (jnp.sum(terms, axis=1, keepdims=True) + fresh_term)
    mixed = lax.dot_general(
        (terms * scale).astype(bf16), cache_ref[:KVR], contract_last, preferred_element_type=f32
    )
    mixed_ref[...] = (mixed + fresh_term * scale * fresh[:, :KVR]).reshape(mixed_ref.shape)
    planes, _, per_peer, latent = mixed_ref.shape
    rows = planes * per_peer
    column = device_ref[0] % PLANE
    new_key = fresh_ref[1:2].astype(f32)
    rest = jnp.concatenate(
        [new_key[:, KVR:], jnp.zeros((1, 2 * KVR - new_key.shape[1]), f32)], axis=1
    )
    line = lax.broadcasted_iota(jnp.int32, (FRESH_ROWS, KVR), 0)
    key_rows = jnp.where(line == 0, new_key[:, :KVR], jnp.where(line == 1, rest, 0.0)).astype(bf16)
    for at, message_ref in enumerate(message_refs):
        message_ref[:rows] = mixed_ref[:, column ^ at].reshape(rows, latent).astype(bf16)
        message_ref[rows:] = key_rows


def prompt_kernel(device_ref, dest_ref, length_ref, slot_ref, *refs):
    key_refs, message_refs, query_hbm = refs[:PLANE], refs[PLANE : 2 * PLANE], refs[2 * PLANE]
    out_refs, (stage_ref, query_ref, sems) = refs[2 * PLANE + 1 : -3], refs[-3:]
    planes, _, rows, width = stage_ref.shape
    per_peer, chunk = rows // 2, width - KVR
    heads = planes * per_peer
    tail = key_refs[0].shape[0] - KVR
    device = device_ref[0]
    sources = [dest_ref[device ^ at] for at in range(PLANE)] + [device ^ at for at in range(PLANE)]
    loads = [
        pltpu.make_async_copy(query_hbm.at[slot_ref[source]], query_ref.at[at], sems.at[at])
        for at, source in enumerate(sources)
    ]
    for load in loads:
        load.start()
    for load in loads:
        load.wait()
    scores = []
    for at in range(PLANE):
        prompt = device ^ at
        latent, rest = unpack(query_ref[at], heads, tail)
        score = jnp.dot(latent, key_refs[at][:KVR], preferred_element_type=f32)
        score += jnp.dot(rest, key_refs[at][KVR:], preferred_element_type=f32)
        score *= softmax_scale
        position = lax.broadcasted_iota(jnp.int32, score.shape, 1)
        scores.append(jnp.where(position < length_ref[prompt], score, -jnp.inf))
    scores = jnp.concatenate(scores, axis=0)
    peak = jnp.max(scores, axis=1, keepdims=True)
    terms = jnp.exp(scores - peak)
    total = jnp.sum(terms, axis=1, keepdims=True)
    log_sum = peak + jnp.log(total)
    scale = 1.0 / total
    terms = terms.astype(bf16)
    lane = lax.broadcasted_iota(jnp.int32, (heads, chunk), 1)
    fold = lambda value: value.reshape(planes, per_peer, value.shape[1])
    for at in range(PLANE):
        part = slice(at * heads, (at + 1) * heads)
        mixed = lax.dot_general(
            terms[part], key_refs[at][:KVR], contract_last, preferred_element_type=f32
        )
        resident = message_refs[at][:heads, :KVR].astype(f32)
        stage_ref[:, at, :, :KVR] = jnp.concatenate(
            [fold(mixed * scale[part]), fold(resident)], axis=1
        ).astype(bf16)
        fresh = message_refs[at][heads : heads + FRESH_ROWS].astype(f32)
        fresh, fresh_rest = fresh[0:1], fresh[1:2, :tail]
        latent, rest = unpack(query_ref[PLANE + at], heads, tail)
        fresh_score = softmax_scale * (
            jnp.sum(latent.astype(f32) * fresh, axis=1, keepdims=True)
            + jnp.sum(rest.astype(f32) * fresh_rest, axis=1, keepdims=True)
        )
        stats = jnp.zeros((heads, chunk), f32)
        for lane_at, value in enumerate(three_parts(log_sum[part]) + three_parts(fresh_score)):
            stats = jnp.where(lane == lane_at, value, stats)
        fresh_rows = [fresh[:, start : start + chunk] for start in range(0, KVR, chunk)]
        if len(fresh_rows) < per_peer:
            fresh_rows.append(jnp.zeros((per_peer - len(fresh_rows), chunk), f32))
        fresh_rows = jnp.concatenate(fresh_rows, axis=0)[None]
        stage_ref[:, at, :, KVR:] = jnp.concatenate(
            [fold(stats), jnp.broadcast_to(fresh_rows, (planes, per_peer, chunk))], axis=1
        ).astype(bf16)
    for at, out_ref in enumerate(out_refs):
        out_ref[...] = stage_ref[(device // PLANE) ^ at]


def pair_kernel(keep_ref, other_ref, pair_ref):
    pair_ref[...] = (keep_ref[...] + other_ref[...].astype(f32)).astype(bf16)


def heads_kernel(row_ref, column_ref, peer_ref, upward_ref, proj_ref, *refs):
    payload_refs, (keep_ref, send_ref, rows_ref) = refs[:-3], refs[-3:]
    for at, payload_ref in enumerate(payload_refs):
        rows_ref[at * PLANE : (at + 1) * PLANE] = payload_ref[...]
    peers, rows, width = rows_ref.shape
    per_peer = rows // 2
    columns = peers * rows
    both = 2 * peers
    row_head, row_device, row_new = row_ref[:, 0:1], row_ref[:, 1:2], row_ref[:, 2:3]
    col_peer, col_row, col_dest = column_ref[0:1, :], column_ref[1:2, :], column_ref[2:3, :]
    stats = rows_ref[:, :, KVR : KVR + LANES].astype(f32).reshape(columns, LANES).T
    log_sum = stats[0:1] + stats[1:2] + stats[2:3]
    fresh_score = stats[3:4] + stats[4:5] + stats[5:6]
    same_head = col_row == row_head
    own = col_peer == row_device
    new_row = row_new == 1
    arrives = same_head & (col_dest == row_device) & new_row
    fresh = jnp.sum(jnp.where(same_head & own, fresh_score, 0.0), axis=1, keepdims=True)
    scored = jnp.where(arrives, log_sum, -jnp.inf)
    peak = jnp.maximum(jnp.max(scored, axis=1, keepdims=True), fresh)
    terms = jnp.exp(scored - peak)
    fresh_term = jnp.exp(fresh - peak)
    scale = 1.0 / (jnp.sum(terms, axis=1, keepdims=True) + fresh_term)
    resident = jnp.where(own & (col_row == row_head + per_peer), 1.0, 0.0)
    mixing = jnp.where(new_row, terms * scale, resident)
    fresh_mixing = jnp.where((peer_ref[...] == row_device) & new_row, fresh_term * scale, 0.0)
    chunk = width - KVR
    fresh_rows = jnp.concatenate(
        [rows_ref[:, per_peer + at, KVR:] for at in range(KVR // chunk)], axis=1
    )
    latents = rows_ref[:, :, :KVR].reshape(columns, KVR)
    mixed = jnp.zeros((row_ref.shape[0], KVR), f32)
    for weights, values in ((mixing, latents), (fresh_mixing, fresh_rows)):
        high = weights.astype(bf16)
        low = (weights - high.astype(f32)).astype(bf16)
        mixed = mixed + jnp.dot(high, values, preferred_element_type=f32)
        mixed = mixed + jnp.dot(low, values, preferred_element_type=f32)
    mixed = mixed.astype(bf16)
    value_rows = jnp.concatenate(
        [
            jnp.dot(
                mixed[head * both : (head + 1) * both], upward_ref[head], preferred_element_type=f32
            ).astype(bf16)
            for head in range(per_peer)
        ],
        axis=1,
    )
    for start in range(0, proj_ref.shape[1], BLOCK):
        part = jnp.dot(value_rows, proj_ref[:, start : start + BLOCK], preferred_element_type=f32)
        columns = slice(start, start + BLOCK)
        keep_ref[:, :, columns] = part[:peers].reshape(peers // 2, 2, BLOCK)
        send_ref[:, :, columns] = part[peers:].reshape(peers // 2, 2, BLOCK).astype(bf16)


def expert_kernel(rows_ref, *refs):
    out_ref, arrived = refs[6], refs[10]
    gate_ref, up_ref, down_ref = refs[7:10]
    units, model = refs[0].shape
    chips, pair = out_ref.shape[:2]
    first, second = model // 4, model // 2
    steps = [(range(4), start, first) for start in range(0, model, first)]
    steps += [(range(4, 6), start, second) for start in range(0, model, second)]
    copies = []
    for matrices, start, size in steps:
        copies.append([])
        for at in matrices:
            place = refs[7 + at // 2].at[pl.ds(at % 2 * units, units), pl.ds(start, size)]
            sem = arrived.at[sum(map(len, copies))]
            copies[-1].append(
                pltpu.make_async_copy(refs[at].at[:, pl.ds(start, size)], place, sem)
            )
            copies[-1][-1].start()
    gate = up_value = jnp.zeros((rows_ref.shape[0], 2 * units), f32)
    for step, (matrices, start, size) in enumerate(steps):
        for copy in copies[step]:
            copy.wait()
        columns = slice(start, start + size)
        if size == first:
            rows = rows_ref[:, columns]
            gate += lax.dot_general(
                rows, gate_ref[:, columns], contract_last, preferred_element_type=f32
            )
            up_value += lax.dot_general(
                rows, up_ref[:, columns], contract_last, preferred_element_type=f32
            )
        else:
            act = (gate / (1.0 + jnp.exp(-gate)) * up_value).astype(bf16)
            part = jnp.dot(act, down_ref[:, columns], preferred_element_type=f32)
            out_ref[:, :, columns] = part.reshape(chips, pair, size).astype(bf16)


def near(value):
    return pltpu.with_memory_space_constraint(value, pltpu.VMEM)


def distant(value):
    return pltpu.with_memory_space_constraint(value, pltpu.HBM)


def call(kernel, outputs, operands, far=(), scratch=(), cost=None):
    specs = [scalars if operand.ndim == 1 else whole for operand in operands]
    return pl.pallas_call(
        kernel,
        out_shape=[pltpu.VMEM(shape, dtype) for shape, dtype in outputs],
        in_specs=specs + [pl.BlockSpec(memory_space=pl.ANY)] * len(far),
        out_specs=[whole] * len(outputs),
        scratch_shapes=scratch,
        compiler_params=pltpu.CompilerParams(vmem_limit_bytes=32 << 20),
        cost_estimate=cost,
    )(
        *[operand if operand.ndim == 1 else near(operand) for operand in operands],
        *far,
    )


def call_far(kernel, shapes, operands, scratch, cost=None):
    far = pl.BlockSpec(memory_space=pltpu.HBM)
    return pl.pallas_call(
        kernel,
        out_shape=shapes,
        in_specs=[far] * len(operands),
        out_specs=jax.tree.map(lambda _: far, shapes),
        scratch_shapes=scratch,
        compiler_params=pltpu.CompilerParams(vmem_limit_bytes=16 << 20),
        cost_estimate=cost,
    )(*map(distant, operands))


def prefetch(after, weights):
    return pl.pallas_call(
        prefetch_kernel,
        out_shape=[pltpu.VMEM(weight.shape, weight.dtype) for weight in weights],
        in_specs=[pl.BlockSpec(memory_space=pl.ANY)] * (1 + len(weights)),
        out_specs=[whole] * len(weights),
        scratch_shapes=[pltpu.SemaphoreType.DMA((len(weights),))],
        compiler_params=pltpu.CompilerParams(vmem_limit_bytes=16 << 20),
    )(after, *map(distant, weights))


def middle_first(count):
    return sorted(range(count), key=lambda at: abs(4 * at - 2 * count + 1))


def shards(
    handoff_rows,
    handoff_dest,
    handoff_len,
    resident_cache,
    resident_len,
    queries,
    new_latent,
    residual_in,
    value_upward,
    out_proj,
    norm_gain,
    expert_ids,
    expert_gates,
    gate_proj,
    up_proj,
    down_proj,
):
    devices = lax.axis_size("ep")
    device = lax.axis_index("ep")
    core = device % 2
    chips = devices // 2
    siblings = [(i, i ^ 1) for i in range(devices)]
    chip_order = middle_first(chips)
    same_core = [[2 * chip + k for chip in chip_order] for k in range(2)]
    device_order = [2 * chip + k for k in range(2) for chip in chip_order]
    slots = sorted(range(devices), key=device_order.__getitem__)
    slice_count = MOE_FF // UNITS
    heads, width = queries.shape[2], queries.shape[3]
    per_peer = heads // devices
    model = residual_in.shape[2]

    def exchange(value, groups):
        return lax.all_to_all(
            value, "ep", split_axis=0, concat_axis=0, tiled=True, axis_index_groups=groups
        )


    planes = devices // PLANE
    toward = lambda value, bits: (
        lax.ppermute(value, "ep", [(i, i ^ bits) for i in range(devices)]) if bits else value
    )
    own_device = device.astype(jnp.int32)[None]

    flipped = jnp.swapaxes(queries[0], 1, 2)
    spread_shape = (devices, heads // PLANE * width // LANES, LANES)
    spread_rows = call_far(
        functools.partial(spread_kernel, slots),
        jax.ShapeDtypeStruct(spread_shape, bf16),
        [flipped],
        [
            pltpu.VMEM((width, heads), bf16),
            pltpu.VMEM((PLANE, *spread_shape[1:]), bf16),
            pltpu.SemaphoreType.DMA((1 + devices,)),
        ],
    )
    spread = exchange(spread_rows, [device_order])

    short = pl.CostEstimate(flops=1, bytes_accessed=1, transcendentals=0)
    flipped_keys = jnp.swapaxes(handoff_rows[0], 0, 1)
    plane_keys = [flipped_keys]
    bit = PLANE // 2
    while bit:
        crossing = [toward(keys, bit) for keys in plane_keys]
        plane_keys = [keys for pair in zip(plane_keys, crossing) for keys in pair]
        bit //= 2
    flipped_cache = jnp.swapaxes(resident_cache[0], 0, 1)
    messages = call(
        resident_kernel,
        [((planes * per_peer + FRESH_ROWS, KVR), bf16)] * PLANE,
        [own_device, resident_len, new_latent[0]],
        [spread_rows, distant(flipped), distant(flipped_cache)],
        [
            pltpu.VMEM((width, heads), bf16),
            pltpu.VMEM(flipped_cache.shape, bf16),
            pltpu.VMEM((planes, PLANE, per_peer, KVR), f32),
            pltpu.SemaphoreType.DMA((2,)),
        ],
        pl.CostEstimate(flops=6000000000, bytes_accessed=30000000, transcendentals=262144),
    )
    messages = [toward(message, at) for at, message in enumerate(messages)]

    chunk = max(LANES, KVR // per_peer)
    payloads = call(
        prompt_kernel,
        [((PLANE, 2 * per_peer, KVR + chunk), bf16)] * planes,
        [own_device, handoff_dest, handoff_len, jnp.array(slots, jnp.int32), *plane_keys, *messages],
        [spread],
        [
            pltpu.VMEM((planes, PLANE, 2 * per_peer, KVR + chunk), bf16),
            pltpu.VMEM((2 * PLANE, *spread_shape[1:]), bf16),
            pltpu.SemaphoreType.DMA((2 * PLANE,)),
        ],
    )
    upward, projection = prefetch(payloads[0], [value_upward, out_proj.reshape(-1, model)])
    payloads = [toward(payload, at * PLANE) for at, payload in enumerate(payloads)]

    row = jnp.arange(per_peer * 2 * devices, dtype=jnp.int32)
    row_core = (row // devices % 2) ^ core
    chip_at = jnp.array(chip_order, jnp.int32)
    row_device = chip_at[row // 2 % chips] * 2 + row_core
    row_table = jnp.stack([row // (2 * devices), row_device, row % 2], axis=1)
    peers = device.astype(jnp.int32) ^ jnp.arange(devices, dtype=jnp.int32)
    is_peer = peers[:, None] == jnp.arange(devices, dtype=jnp.int32)[None, :]
    peer_dest = jnp.sum(jnp.where(is_peer, handoff_dest[None, :], 0), axis=1)
    column = jnp.arange(devices * 2 * per_peer, dtype=jnp.int32)
    column_table = jnp.stack(
        [
            jnp.repeat(peers, 2 * per_peer),
            column % (2 * per_peer),
            jnp.repeat(peer_dest, 2 * per_peer),
        ],
        axis=0,
    )
    keep, send = call(
        heads_kernel,
        [((chips, 2, model), f32), ((chips, 2, model), bf16)],
        [row_table, column_table, peers[None], upward, projection, *payloads],
        scratch=[pltpu.VMEM((devices, 2 * per_peer, KVR + chunk), bf16)],
    )

    other = lax.ppermute(send, "ep", siblings)
    (pair,) = call(pair_kernel, [((chips, 2, model), bf16)], [keep, other])
    attention = jnp.sum(exchange(pair, same_core).astype(f32), axis=0)
    hidden = residual_in[0].astype(f32) + attention
    inverse_rms = lax.rsqrt(jnp.mean(hidden * hidden, axis=-1, keepdims=True) + norm_epsilon)
    normed = (hidden * inverse_rms * norm_gain.astype(f32)).astype(bf16)

    own_rows = exchange(jnp.broadcast_to(normed[None], (chips, 2, model)), same_core)
    experts = []
    for matrix in (gate_proj, up_proj, down_proj):
        experts += [matrix, lax.ppermute(matrix, "ep", siblings)]
    (part,) = call(
        expert_kernel,
        [((chips, 2, model), bf16)],
        [own_rows.reshape(devices, model)],
        [matrix if at == 1 else distant(matrix) for at, matrix in enumerate(experts)],
        [pltpu.VMEM((2 * gate_proj.shape[0], model), bf16)] * 3
        + [pltpu.SemaphoreType.DMA((20,))],
    )
    returned = exchange(part, same_core)

    chip_expert = chip_at * 2 // slice_count
    chosen = (expert_ids[0][..., None] == chip_expert).astype(f32)
    weights = jnp.sum(expert_gates[0][..., None] * chosen, axis=1)
    mixed = jnp.sum(weights.T[..., None] * returned.astype(f32), axis=0)
    return (hidden + mixed).astype(bf16)[None]


def solution(mesh):
    placed = (
        P(("groups", "ep"), None, None),
        P("groups"),
        P("groups"),
        P(("groups", "ep"), None, None),
        P(("groups", "ep")),
        P(None, ("groups", "ep"), None, None),
        P(None, ("groups", "ep"), None),
        P(None, ("groups", "ep"), None),
        P("ep", None, None),
        P("ep", None, None),
        P(),
        P(None, ("groups", "ep"), None),
        P(None, ("groups", "ep"), None),
        P("ep", None),
        P("ep", None),
        P("ep", None),
    )
    return jax.shard_map(
        shards,
        mesh=mesh,
        in_specs=placed,
        out_specs=P(None, ("groups", "ep"), None),
        check_vma=False,
    )
```

```python
import functools

import jax
import jax.numpy as jnp
from jax import lax
from jax.experimental import pallas as pl
from jax.experimental.pallas import tpu as pltpu
from jax.sharding import PartitionSpec as P

KVR = 512
MOE_FF = 1024
UNITS = 128
LANES = 128
BLOCK = 1024
EARLY = 5120
PLANE = 4

softmax_scale = 192.0 ** (-0.5)
norm_epsilon = 1e-06
contract_last = (((1,), (1,)), ((), ()))
f32 = jnp.float32
bf16 = jnp.bfloat16
whole = pl.BlockSpec(memory_space=pltpu.VMEM)
scalars = pl.BlockSpec(memory_space=pltpu.SMEM)


def three_parts(value):
    first = value.astype(bf16).astype(f32)
    second = (value - first).astype(bf16).astype(f32)
    third = value - first - second
    return first, second, third


def pack(rows):
    heads, width = rows.shape
    tail = width - KVR
    beside = LANES // tail
    high = heads // beside
    pieces = [rows[:, start : start + LANES] for start in range(0, KVR, LANES)]
    pieces.append(
        jnp.concatenate([rows[at * high : (at + 1) * high, KVR:] for at in range(beside)], axis=1)
    )
    return jnp.concatenate(pieces, axis=0)


def unpack(packed, heads, tail):
    pieces = [packed[at * heads : (at + 1) * heads] for at in range(KVR // LANES)]
    rest = packed[heads * (KVR // LANES) :]
    tails = [rest[:, start : start + tail] for start in range(0, LANES, tail)]
    return jnp.concatenate(pieces, axis=1), jnp.concatenate(tails, axis=0)


def spread_kernel(slots, query_hbm, spread_hbm, query_ref, blocks_ref, sems):
    peers = spread_hbm.shape[0]
    planes = peers // PLANE
    width, heads = query_ref.shape
    load = pltpu.make_async_copy(query_hbm.at[1], query_ref, sems.at[0])
    load.start()
    load.wait()
    by_peer = query_ref[...].astype(f32).T.reshape(planes, PLANE, heads // peers, width)
    copies = []
    for column in range(PLANE):
        rows = by_peer[:, column].reshape(heads // PLANE, width)
        blocks_ref[column] = pack(rows).astype(bf16)
        for plane in range(planes):
            peer = slots[plane * PLANE + column]
            copies.append(
                pltpu.make_async_copy(blocks_ref.at[column], spread_hbm.at[peer], sems.at[1 + peer])
            )
            copies[-1].start()
    for copy in copies:
        copy.wait()


def prefetch_kernel(after_ref, upward_hbm, proj_hbm, upward_ref, early_ref, sems):
    del after_ref
    copies = [
        pltpu.make_async_copy(proj_hbm.at[:, :EARLY], early_ref, sems.at[0]),
        pltpu.make_async_copy(upward_hbm, upward_ref, sems.at[1]),
    ]
    for copy in copies:
        copy.start()
    for copy in copies:
        copy.wait()


def resident_kernel(device_ref, length_ref, fresh_ref, after_ref, query_hbm, cache_hbm, *refs):
    message_refs, (query_ref, cache_ref, mixed_ref, sems) = refs[:-4], refs[-4:]
    del after_ref
    loads = [
        pltpu.make_async_copy(query_hbm.at[0], query_ref, sems.at[0]),
        pltpu.make_async_copy(cache_hbm, cache_ref, sems.at[1]),
    ]
    for load in loads:
        load.start()
    for load in loads:
        load.wait()
    query = query_ref[...].astype(f32).T
    fresh = fresh_ref[0:1].astype(f32)
    scores = jnp.dot(query.astype(bf16), cache_ref[...], preferred_element_type=f32)
    position = lax.broadcasted_iota(jnp.int32, scores.shape, 1)
    scores = jnp.where(position < length_ref[0], scores * softmax_scale, -jnp.inf)
    fresh_score = softmax_scale * jnp.sum(query * fresh, axis=1, keepdims=True)
    peak = jnp.maximum(jnp.max(scores, axis=1, keepdims=True), fresh_score)
    terms = jnp.exp(scores - peak)
    fresh_term = jnp.exp(fresh_score - peak)
    scale = 1.0 / (jnp.sum(terms, axis=1, keepdims=True) + fresh_term)
    mixed = lax.dot_general(
        (terms * scale).astype(bf16), cache_ref[:KVR], contract_last, preferred_element_type=f32
    )
    mixed_ref[...] = (mixed + fresh_term * scale * fresh[:, :KVR]).reshape(mixed_ref.shape)
    planes, _, per_peer, _ = mixed_ref.shape
    column = device_ref[0] % PLANE
    new_key = fresh_ref[1:2].astype(f32)
    rest = jnp.concatenate(
        [new_key[:, KVR:], jnp.zeros((1, 2 * KVR - new_key.shape[1]), f32)], axis=1
    )
    shape = message_refs[0].shape[1:]
    blocks = message_refs[0].shape[0] - planes
    for at, message_ref in enumerate(message_refs):
        message_ref[:planes] = mixed_ref[:, column ^ at].astype(bf16)
        for block in range(blocks):
            line = lax.broadcasted_iota(jnp.int32, shape, 0) + block * per_peer
            key_rows = jnp.where(line == 0, new_key[:, :KVR], jnp.where(line == 1, rest, 0.0))
            message_ref[planes + block] = key_rows.astype(bf16)


def regroup_kernel(device_ref, *refs):
    message_refs, out_refs = refs[:PLANE], refs[PLANE:]
    per_peer = out_refs[0].shape[1]
    plane = device_ref[0] // PLANE
    planes = len(out_refs)
    fresh = [message_ref[planes].astype(f32)[0:1] for message_ref in message_refs]
    blocks = out_refs[0].shape[0] - PLANE
    for at, out_ref in enumerate(out_refs):
        for source, message_ref in enumerate(message_refs):
            out_ref[source] = message_ref[plane ^ at]
        for block in range(blocks):
            line = lax.broadcasted_iota(jnp.int32, (per_peer, KVR), 0) + block * per_peer
            rows = jnp.zeros((per_peer, KVR), f32)
            for source, row in enumerate(fresh):
                rows = jnp.where(line == source, row, rows)
            out_ref[PLANE + block] = rows.astype(bf16)


def prompt_kernel(device_ref, dest_ref, length_ref, slot_ref, *refs):
    key_refs, message_refs, query_hbm = refs[:PLANE], refs[PLANE : 2 * PLANE], refs[2 * PLANE]
    out_refs, (stage_ref, query_ref, sems) = refs[2 * PLANE + 1 : -3], refs[-3:]
    planes, _, per_peer, width = stage_ref.shape
    heads = planes * per_peer
    tail = key_refs[0].shape[0] - KVR
    device = device_ref[0]
    sources = [dest_ref[device ^ at] for at in range(PLANE)] + [device ^ at for at in range(PLANE)]
    loads = [
        pltpu.make_async_copy(query_hbm.at[slot_ref[source]], query_ref.at[at], sems.at[at])
        for at, source in enumerate(sources)
    ]
    for load in loads:
        load.start()
    for load in loads:
        load.wait()
    scores = []
    for at in range(PLANE):
        prompt = device ^ at
        latent, rest = unpack(query_ref[at], heads, tail)
        score = jnp.dot(latent, key_refs[at][:KVR], preferred_element_type=f32)
        score += jnp.dot(rest, key_refs[at][KVR:], preferred_element_type=f32)
        score *= softmax_scale
        position = lax.broadcasted_iota(jnp.int32, score.shape, 1)
        scores.append(jnp.where(position < length_ref[prompt], score, -jnp.inf))
    scores = jnp.concatenate(scores, axis=0)
    peak = jnp.max(scores, axis=1, keepdims=True)
    terms = jnp.exp(scores - peak)
    total = jnp.sum(terms, axis=1, keepdims=True)
    log_sum = peak + jnp.log(total)
    scale = 1.0 / total
    terms = terms.astype(bf16)
    lane = lax.broadcasted_iota(jnp.int32, (heads, width - KVR), 1)
    for at in range(PLANE):
        part = slice(at * heads, (at + 1) * heads)
        mixed = lax.dot_general(
            terms[part], key_refs[at][:KVR], contract_last, preferred_element_type=f32
        )
        mixed = (mixed * scale[part]).reshape(planes, per_peer, KVR)
        stage_ref[:, at, :, :KVR] = mixed.astype(bf16)
        fresh = message_refs[at][planes:].astype(f32)
        fresh = fresh.reshape(fresh.shape[0] * per_peer, KVR)
        fresh, fresh_rest = fresh[0:1], fresh[1:2, :tail]
        latent, rest = unpack(query_ref[PLANE + at], heads, tail)
        fresh_score = softmax_scale * (
            jnp.sum(latent.astype(f32) * fresh, axis=1, keepdims=True)
            + jnp.sum(rest.astype(f32) * fresh_rest, axis=1, keepdims=True)
        )
        stats = jnp.zeros((heads, width - KVR), f32)
        for lane_at, value in enumerate(three_parts(log_sum[part]) + three_parts(fresh_score)):
            stats = jnp.where(lane == lane_at, value, stats)
        stats = stats.reshape(planes, per_peer, width - KVR)
        stage_ref[:, at, :, KVR:] = stats.astype(bf16)
    for at, out_ref in enumerate(out_refs):
        out_ref[...] = stage_ref[(device // PLANE) ^ at]


def pair_kernel(keep_ref, other_ref, pair_ref):
    pair_ref[...] = (keep_ref[...] + other_ref[...].astype(f32)).astype(bf16)


def heads_kernel(row_ref, column_ref, peer_ref, upward_ref, early_ref, *refs):
    proj_hbm, keep_ref, send_ref, partial_ref, resident_ref, fresh_ref, late_ref, sems = refs[-8:]
    planes = (len(refs) - 8) // 2
    depth, model = proj_hbm.shape
    loads = []
    for at in range(2):
        part = slice(at * depth // 2, (at + 1) * depth // 2)
        loads.append(
            pltpu.make_async_copy(proj_hbm.at[part, EARLY:], late_ref.at[part], sems.at[at])
        )
        loads[at].start()
    for at in range(planes):
        places = slice(at * PLANE, (at + 1) * PLANE)
        partial_ref[places] = refs[at][...]
        arrived = refs[planes + at]
        resident_ref[places] = arrived[:PLANE]
        fresh = arrived[PLANE:].astype(f32)
        fresh_ref[places] = fresh.reshape(fresh.shape[0] * fresh.shape[1], KVR)[:PLANE]
    peers, per_peer, _ = partial_ref.shape
    columns = peers * per_peer
    both = 2 * peers
    row_head, row_device, row_new = row_ref[:, 0:1], row_ref[:, 1:2], row_ref[:, 2:3]
    col_peer, col_head, col_dest = column_ref[0:1, :], column_ref[1:2, :], column_ref[2:3, :]
    stats = partial_ref[:, :, KVR:].astype(f32).reshape(columns, LANES).T
    log_sum = stats[0:1] + stats[1:2] + stats[2:3]
    fresh_score = stats[3:4] + stats[4:5] + stats[5:6]
    same_head = col_head == row_head
    own = same_head & (col_peer == row_device)
    new_row = row_new == 1
    arrives = same_head & (col_dest == row_device) & new_row
    fresh = jnp.sum(jnp.where(own, fresh_score, 0.0), axis=1, keepdims=True)
    scored = jnp.where(arrives, log_sum, -jnp.inf)
    peak = jnp.maximum(jnp.max(scored, axis=1, keepdims=True), fresh)
    terms = jnp.exp(scored - peak)
    fresh_term = jnp.exp(fresh - peak)
    scale = 1.0 / (jnp.sum(terms, axis=1, keepdims=True) + fresh_term)
    fresh_mixing = jnp.where((peer_ref[...] == row_device) & new_row, fresh_term * scale, 0.0)
    resident_mixing = jnp.where(own & (row_new == 0), 1.0, 0.0).astype(bf16)
    resident = resident_ref[...].reshape(columns, KVR)
    mixed = jnp.dot(resident_mixing, resident, preferred_element_type=f32)
    latents = partial_ref[:, :, :KVR].reshape(columns, KVR)
    for weights, values in ((terms * scale, latents), (fresh_mixing, fresh_ref[...].astype(bf16))):
        high = weights.astype(bf16)
        low = (weights - high.astype(f32)).astype(bf16)
        mixed = mixed + jnp.dot(high, values, preferred_element_type=f32)
        mixed = mixed + jnp.dot(low, values, preferred_element_type=f32)
    mixed = mixed.astype(bf16)
    value_rows = jnp.concatenate(
        [
            jnp.dot(
                mixed[head * both : (head + 1) * both], upward_ref[head], preferred_element_type=f32
            ).astype(bf16)
            for head in range(per_peer)
        ],
        axis=1,
    )
    for start in range(0, model, BLOCK):
        if start == EARLY - BLOCK:
            for load in loads:
                load.wait()
        if start < EARLY:
            weights = early_ref[:, start : start + BLOCK]
        else:
            weights = late_ref[:, start - EARLY : start - EARLY + BLOCK]
        part = jnp.dot(value_rows, weights, preferred_element_type=f32)
        columns = slice(start, start + BLOCK)
        keep_ref[:, :, columns] = part[:peers].reshape(peers // 2, 2, BLOCK)
        send_ref[:, :, columns] = part[peers:].reshape(peers // 2, 2, BLOCK).astype(bf16)


def expert_kernel(rows_ref, *refs):
    out_ref, arrived = refs[6], refs[10]
    gate_ref, up_ref, down_ref = refs[7:10]
    units, model = refs[0].shape
    chips, pair = out_ref.shape[:2]
    first, second = model // 4, model // 2
    steps = [(range(4), start, first) for start in range(0, model, first)]
    steps += [(range(4, 6), start, second) for start in range(0, model, second)]
    copies = []
    for matrices, start, size in steps:
        copies.append([])
        for at in matrices:
            place = refs[7 + at // 2].at[pl.ds(at % 2 * units, units), pl.ds(start, size)]
            sem = arrived.at[sum(map(len, copies))]
            copies[-1].append(
                pltpu.make_async_copy(refs[at].at[:, pl.ds(start, size)], place, sem)
            )
            copies[-1][-1].start()
    gate = up_value = jnp.zeros((rows_ref.shape[0], 2 * units), f32)
    for step, (matrices, start, size) in enumerate(steps):
        for copy in copies[step]:
            copy.wait()
        columns = slice(start, start + size)
        if size == first:
            rows = rows_ref[:, columns]
            gate += lax.dot_general(
                rows, gate_ref[:, columns], contract_last, preferred_element_type=f32
            )
            up_value += lax.dot_general(
                rows, up_ref[:, columns], contract_last, preferred_element_type=f32
            )
        else:
            act = (gate / (1.0 + jnp.exp(-gate)) * up_value).astype(bf16)
            part = jnp.dot(act, down_ref[:, columns], preferred_element_type=f32)
            out_ref[:, :, columns] = part.reshape(chips, pair, size).astype(bf16)


def near(value):
    return pltpu.with_memory_space_constraint(value, pltpu.VMEM)


def distant(value):
    return pltpu.with_memory_space_constraint(value, pltpu.HBM)


def call(kernel, outputs, operands, far=(), scratch=(), cost=None):
    specs = [scalars if operand.ndim == 1 else whole for operand in operands]
    return pl.pallas_call(
        kernel,
        out_shape=[pltpu.VMEM(shape, dtype) for shape, dtype in outputs],
        in_specs=specs + [pl.BlockSpec(memory_space=pl.ANY)] * len(far),
        out_specs=[whole] * len(outputs),
        scratch_shapes=scratch,
        compiler_params=pltpu.CompilerParams(vmem_limit_bytes=32 << 20),
        cost_estimate=cost,
    )(
        *[operand if operand.ndim == 1 else near(operand) for operand in operands],
        *far,
    )


def call_far(kernel, shapes, operands, scratch, cost=None):
    far = pl.BlockSpec(memory_space=pltpu.HBM)
    return pl.pallas_call(
        kernel,
        out_shape=shapes,
        in_specs=[far] * len(operands),
        out_specs=jax.tree.map(lambda _: far, shapes),
        scratch_shapes=scratch,
        compiler_params=pltpu.CompilerParams(vmem_limit_bytes=16 << 20),
        cost_estimate=cost,
    )(*map(distant, operands))


def prefetch(after, upward, projection):
    return pl.pallas_call(
        prefetch_kernel,
        out_shape=[pltpu.VMEM(upward.shape, bf16), pltpu.VMEM((len(projection), EARLY), bf16)],
        in_specs=[pl.BlockSpec(memory_space=pl.ANY)] * 3,
        out_specs=[whole] * 2,
        scratch_shapes=[pltpu.SemaphoreType.DMA((2,))],
        compiler_params=pltpu.CompilerParams(vmem_limit_bytes=16 << 20),
    )(after, distant(upward), distant(projection))


def middle_first(chips):
    middle = chips // 4
    return [
        2 * plane + chip
        for ring in range(middle)
        for chip in range(2)
        for plane in (middle + ring, middle - 1 - ring)
    ]


def shards(
    handoff_rows,
    handoff_dest,
    handoff_len,
    resident_cache,
    resident_len,
    queries,
    new_latent,
    residual_in,
    value_upward,
    out_proj,
    norm_gain,
    expert_ids,
    expert_gates,
    gate_proj,
    up_proj,
    down_proj,
):
    devices = lax.axis_size("ep")
    device = lax.axis_index("ep")
    core = device % 2
    chips = devices // 2
    siblings = [(i, i ^ 1) for i in range(devices)]
    chip_order = middle_first(chips)
    same_core = [[2 * chip + k for chip in chip_order] for k in range(2)]
    device_order = [2 * chip + k for k in range(2) for chip in chip_order]
    slots = sorted(range(devices), key=device_order.__getitem__)
    slice_count = MOE_FF // UNITS
    heads, width = queries.shape[2], queries.shape[3]
    per_peer = heads // devices
    model = residual_in.shape[2]

    def exchange(value, groups):
        return lax.all_to_all(
            value, "ep", split_axis=0, concat_axis=0, tiled=True, axis_index_groups=groups
        )


    planes = devices // PLANE
    toward = lambda value, bits: (
        lax.ppermute(value, "ep", [(i, i ^ bits) for i in range(devices)]) if bits else value
    )
    own_device = device.astype(jnp.int32)[None]

    flipped = jnp.swapaxes(queries[0], 1, 2)
    spread_shape = (devices, heads // PLANE * width // LANES, LANES)
    spread_rows = call_far(
        functools.partial(spread_kernel, slots),
        jax.ShapeDtypeStruct(spread_shape, bf16),
        [flipped],
        [
            pltpu.VMEM((width, heads), bf16),
            pltpu.VMEM((PLANE, *spread_shape[1:]), bf16),
            pltpu.SemaphoreType.DMA((1 + devices,)),
        ],
    )
    spread = exchange(spread_rows, [device_order])

    short = pl.CostEstimate(flops=1, bytes_accessed=1, transcendentals=0)
    flipped_keys = jnp.swapaxes(handoff_rows[0], 0, 1)
    plane_keys = [flipped_keys]
    bit = PLANE // 2
    while bit:
        crossing = [toward(keys, bit) for keys in plane_keys]
        plane_keys = [keys for pair in zip(plane_keys, crossing) for keys in pair]
        bit //= 2
    flipped_cache = jnp.swapaxes(resident_cache[0], 0, 1)
    messages = call(
        resident_kernel,
        [((planes + -(-2 // per_peer), per_peer, KVR), bf16)] * PLANE,
        [own_device, resident_len, new_latent[0]],
        [spread_rows, distant(flipped), distant(flipped_cache)],
        [
            pltpu.VMEM((width, heads), bf16),
            pltpu.VMEM(flipped_cache.shape, bf16),
            pltpu.VMEM((planes, PLANE, per_peer, KVR), f32),
            pltpu.SemaphoreType.DMA((2,)),
        ],
        pl.CostEstimate(flops=6000000000, bytes_accessed=30000000, transcendentals=262144),
    )
    messages = [toward(message, at) for at, message in enumerate(messages)]

    residents = call(
        regroup_kernel,
        [((PLANE + -(-PLANE // per_peer), per_peer, KVR), bf16)] * planes,
        [own_device, *messages],
        cost=short,
    )
    residents = [toward(resident, at * PLANE) for at, resident in enumerate(residents)]

    payloads = call(
        prompt_kernel,
        [((PLANE, per_peer, KVR + LANES), bf16)] * planes,
        [own_device, handoff_dest, handoff_len, jnp.array(slots, jnp.int32), *plane_keys, *messages],
        [spread],
        [
            pltpu.VMEM((planes, PLANE, per_peer, KVR + LANES), bf16),
            pltpu.VMEM((2 * PLANE, *spread_shape[1:]), bf16),
            pltpu.SemaphoreType.DMA((2 * PLANE,)),
        ],
    )
    projection = out_proj.reshape(-1, model)
    upward, early = prefetch(payloads[0], value_upward, projection)
    payloads = [toward(payload, at * PLANE) for at, payload in enumerate(payloads)]

    row = jnp.arange(per_peer * 2 * devices, dtype=jnp.int32)
    row_core = (row // devices % 2) ^ core
    chip_at = jnp.array(chip_order, jnp.int32)
    row_device = chip_at[row // 2 % chips] * 2 + row_core
    row_table = jnp.stack([row // (2 * devices), row_device, row % 2], axis=1)
    peers = device.astype(jnp.int32) ^ jnp.arange(devices, dtype=jnp.int32)
    is_peer = peers[:, None] == jnp.arange(devices, dtype=jnp.int32)[None, :]
    peer_dest = jnp.sum(jnp.where(is_peer, handoff_dest[None, :], 0), axis=1)
    column = jnp.arange(devices * per_peer, dtype=jnp.int32)
    column_table = jnp.stack(
        [jnp.repeat(peers, per_peer), column % per_peer, jnp.repeat(peer_dest, per_peer)], axis=0
    )
    keep, send = call(
        heads_kernel,
        [((chips, 2, model), f32), ((chips, 2, model), bf16)],
        [row_table, column_table, peers[None], upward, early, *payloads, *residents],
        [distant(projection)],
        [
            pltpu.VMEM((devices, per_peer, KVR + LANES), bf16),
            pltpu.VMEM((devices, per_peer, KVR), bf16),
            pltpu.VMEM((devices, KVR), f32),
            pltpu.VMEM((len(projection), model - EARLY), bf16),
            pltpu.SemaphoreType.DMA((2,)),
        ],
    )

    other = lax.ppermute(send, "ep", siblings)
    (pair,) = call(pair_kernel, [((chips, 2, model), bf16)], [keep, other])
    attention = jnp.sum(exchange(pair, same_core).astype(f32), axis=0)
    hidden = residual_in[0].astype(f32) + attention
    inverse_rms = lax.rsqrt(jnp.mean(hidden * hidden, axis=-1, keepdims=True) + norm_epsilon)
    normed = (hidden * inverse_rms * norm_gain.astype(f32)).astype(bf16)

    own_rows = exchange(jnp.broadcast_to(normed[None], (chips, 2, model)), same_core)
    experts = []
    for matrix in (gate_proj, up_proj, down_proj):
        experts += [matrix, lax.ppermute(matrix, "ep", siblings)]
    (part,) = call(
        expert_kernel,
        [((chips, 2, model), bf16)],
        [own_rows.reshape(devices, model)],
        [matrix if at == 1 else distant(matrix) for at, matrix in enumerate(experts)],
        [pltpu.VMEM((2 * gate_proj.shape[0], model), bf16)] * 3
        + [pltpu.SemaphoreType.DMA((20,))],
    )
    returned = exchange(part, same_core)

    chip_expert = chip_at * 2 // slice_count
    chosen = (expert_ids[0][..., None] == chip_expert).astype(f32)
    weights = jnp.sum(expert_gates[0][..., None] * chosen, axis=1)
    mixed = jnp.sum(weights.T[..., None] * returned.astype(f32), axis=0)
    return (hidden + mixed).astype(bf16)[None]


def solution(mesh):
    placed = (
        P(("groups", "ep"), None, None),
        P("groups"),
        P("groups"),
        P(("groups", "ep"), None, None),
        P(("groups", "ep")),
        P(None, ("groups", "ep"), None, None),
        P(None, ("groups", "ep"), None),
        P(None, ("groups", "ep"), None),
        P("ep", None, None),
        P("ep", None, None),
        P(),
        P(None, ("groups", "ep"), None),
        P(None, ("groups", "ep"), None),
        P("ep", None),
        P("ep", None),
        P("ep", None),
    )
    return jax.shard_map(
        shards,
        mesh=mesh,
        in_specs=placed,
        out_specs=P(None, ("groups", "ep"), None),
        check_vma=False,
    )
```

```python
import functools

import jax
import jax.numpy as jnp
from jax import lax
from jax.experimental import pallas as pl
from jax.experimental.pallas import tpu as pltpu
from jax.sharding import PartitionSpec as P

KVR = 512
MOE_FF = 1024
UNITS = 128
LANES = 128
BLOCK = 1024
EARLY = 5120
PLANE = 4

softmax_scale = 192.0 ** (-0.5)
norm_epsilon = 1e-06
contract_last = (((1,), (1,)), ((), ()))
f32 = jnp.float32
bf16 = jnp.bfloat16
whole = pl.BlockSpec(memory_space=pltpu.VMEM)
scalars = pl.BlockSpec(memory_space=pltpu.SMEM)


def three_parts(value):
    first = value.astype(bf16).astype(f32)
    second = (value - first).astype(bf16).astype(f32)
    third = value - first - second
    return first, second, third


def pack(rows):
    heads, width = rows.shape
    tail = width - KVR
    beside = LANES // tail
    high = heads // beside
    pieces = [rows[:, start : start + LANES] for start in range(0, KVR, LANES)]
    pieces.append(
        jnp.concatenate([rows[at * high : (at + 1) * high, KVR:] for at in range(beside)], axis=1)
    )
    return jnp.concatenate(pieces, axis=0)


def unpack(packed, heads, tail):
    pieces = [packed[at * heads : (at + 1) * heads] for at in range(KVR // LANES)]
    rest = packed[heads * (KVR // LANES) :]
    tails = [rest[:, start : start + tail] for start in range(0, LANES, tail)]
    return jnp.concatenate(pieces, axis=1), jnp.concatenate(tails, axis=0)


def spread_kernel(slots, query_hbm, spread_hbm, query_ref, blocks_ref, sems):
    peers = spread_hbm.shape[0]
    planes = peers // PLANE
    width, heads = query_ref.shape
    load = pltpu.make_async_copy(query_hbm.at[1], query_ref, sems.at[0])
    load.start()
    load.wait()
    by_peer = query_ref[...].astype(f32).T.reshape(planes, PLANE, heads // peers, width)
    copies = []
    for column in range(PLANE):
        rows = by_peer[:, column].reshape(heads // PLANE, width)
        blocks_ref[column] = pack(rows).astype(bf16)
        for plane in range(planes):
            peer = slots[plane * PLANE + column]
            copies.append(
                pltpu.make_async_copy(blocks_ref.at[column], spread_hbm.at[peer], sems.at[1 + peer])
            )
            copies[-1].start()
    for copy in copies:
        copy.wait()


def prefetch_kernel(after_ref, upward_hbm, proj_hbm, upward_ref, early_ref, sems):
    del after_ref
    copies = [
        pltpu.make_async_copy(proj_hbm.at[:, :EARLY], early_ref, sems.at[0]),
        pltpu.make_async_copy(upward_hbm, upward_ref, sems.at[1]),
    ]
    for copy in copies:
        copy.start()
    for copy in copies:
        copy.wait()


def resident_kernel(device_ref, length_ref, fresh_ref, after_ref, query_hbm, cache_hbm, *refs):
    message_refs, (query_ref, cache_ref, mixed_ref, sems) = refs[:-4], refs[-4:]
    del after_ref
    loads = [
        pltpu.make_async_copy(query_hbm.at[0], query_ref, sems.at[0]),
        pltpu.make_async_copy(cache_hbm, cache_ref, sems.at[1]),
    ]
    for load in loads:
        load.start()
    for load in loads:
        load.wait()
    query = query_ref[...].astype(f32).T
    fresh = fresh_ref[0:1].astype(f32)
    scores = jnp.dot(query.astype(bf16), cache_ref[...], preferred_element_type=f32)
    position = lax.broadcasted_iota(jnp.int32, scores.shape, 1)
    scores = jnp.where(position < length_ref[0], scores * softmax_scale, -jnp.inf)
    fresh_score = softmax_scale * jnp.sum(query * fresh, axis=1, keepdims=True)
    peak = jnp.maximum(jnp.max(scores, axis=1, keepdims=True), fresh_score)
    terms = jnp.exp(scores - peak)
    fresh_term = jnp.exp(fresh_score - peak)
    scale = 1.0 / (jnp.sum(terms, axis=1, keepdims=True) + fresh_term)
    mixed = lax.dot_general(
        (terms * scale).astype(bf16), cache_ref[:KVR], contract_last, preferred_element_type=f32
    )
    mixed_ref[...] = (mixed + fresh_term * scale * fresh[:, :KVR]).reshape(mixed_ref.shape)
    planes, _, per_peer, _ = mixed_ref.shape
    column = device_ref[0] % PLANE
    new_key = fresh_ref[1:2].astype(f32)
    rest = jnp.concatenate(
        [new_key[:, KVR:], jnp.zeros((1, 2 * KVR - new_key.shape[1]), f32)], axis=1
    )
    shape = message_refs[0].shape[1:]
    blocks = message_refs[0].shape[0] - planes
    for at, message_ref in enumerate(message_refs):
        message_ref[:planes] = mixed_ref[:, column ^ at].astype(bf16)
        for block in range(blocks):
            line = lax.broadcasted_iota(jnp.int32, shape, 0) + block * per_peer
            key_rows = jnp.where(line == 0, new_key[:, :KVR], jnp.where(line == 1, rest, 0.0))
            message_ref[planes + block] = key_rows.astype(bf16)


def regroup_kernel(device_ref, *refs):
    message_refs, out_refs = refs[:PLANE], refs[PLANE:]
    per_peer = out_refs[0].shape[1]
    plane = device_ref[0] // PLANE
    planes = len(out_refs)
    fresh = [message_ref[planes].astype(f32)[0:1] for message_ref in message_refs]
    blocks = out_refs[0].shape[0] - PLANE
    for at, out_ref in enumerate(out_refs):
        for source, message_ref in enumerate(message_refs):
            out_ref[source] = message_ref[plane ^ at]
        for block in range(blocks):
            line = lax.broadcasted_iota(jnp.int32, (per_peer, KVR), 0) + block * per_peer
            rows = jnp.zeros((per_peer, KVR), f32)
            for source, row in enumerate(fresh):
                rows = jnp.where(line == source, row, rows)
            out_ref[PLANE + block] = rows.astype(bf16)


def prompt_kernel(device_ref, dest_ref, length_ref, slot_ref, *refs):
    key_refs, message_refs, query_ref = refs[:PLANE], refs[PLANE : 2 * PLANE], refs[2 * PLANE]
    out_refs, stage_ref = refs[2 * PLANE + 1 : -1], refs[-1]
    planes, _, per_peer, width = stage_ref.shape
    heads = planes * per_peer
    tail = key_refs[0].shape[0] - KVR
    device = device_ref[0]
    prompts = [slot_ref[dest_ref[device ^ at]] for at in range(PLANE)]
    owners = [slot_ref[device ^ at] for at in range(PLANE)]
    scores = []
    for at in range(PLANE):
        prompt = device ^ at
        latent, rest = unpack(query_ref[prompts[at]], heads, tail)
        score = jnp.dot(latent, key_refs[at][:KVR], preferred_element_type=f32)
        score += jnp.dot(rest, key_refs[at][KVR:], preferred_element_type=f32)
        score *= softmax_scale
        position = lax.broadcasted_iota(jnp.int32, score.shape, 1)
        scores.append(jnp.where(position < length_ref[prompt], score, -jnp.inf))
    scores = jnp.concatenate(scores, axis=0)
    peak = jnp.max(scores, axis=1, keepdims=True)
    terms = jnp.exp(scores - peak)
    total = jnp.sum(terms, axis=1, keepdims=True)
    log_sum = peak + jnp.log(total)
    scale = 1.0 / total
    terms = terms.astype(bf16)
    lane = lax.broadcasted_iota(jnp.int32, (heads, width - KVR), 1)
    for at in range(PLANE):
        part = slice(at * heads, (at + 1) * heads)
        mixed = lax.dot_general(
            terms[part], key_refs[at][:KVR], contract_last, preferred_element_type=f32
        )
        mixed = (mixed * scale[part]).reshape(planes, per_peer, KVR)
        stage_ref[:, at, :, :KVR] = mixed.astype(bf16)
        fresh = message_refs[at][planes:].astype(f32)
        fresh = fresh.reshape(fresh.shape[0] * per_peer, KVR)
        fresh, fresh_rest = fresh[0:1], fresh[1:2, :tail]
        latent, rest = unpack(query_ref[owners[at]], heads, tail)
        fresh_score = softmax_scale * (
            jnp.sum(latent.astype(f32) * fresh, axis=1, keepdims=True)
            + jnp.sum(rest.astype(f32) * fresh_rest, axis=1, keepdims=True)
        )
        stats = jnp.zeros((heads, width - KVR), f32)
        for lane_at, value in enumerate(three_parts(log_sum[part]) + three_parts(fresh_score)):
            stats = jnp.where(lane == lane_at, value, stats)
        stats = stats.reshape(planes, per_peer, width - KVR)
        stage_ref[:, at, :, KVR:] = stats.astype(bf16)
    for at, out_ref in enumerate(out_refs):
        out_ref[...] = stage_ref[(device // PLANE) ^ at]


def pair_kernel(keep_ref, other_ref, pair_ref):
    pair_ref[...] = (keep_ref[...] + other_ref[...].astype(f32)).astype(bf16)


def heads_kernel(row_ref, column_ref, peer_ref, upward_ref, early_ref, *refs):
    proj_hbm, keep_ref, send_ref, partial_ref, resident_ref, fresh_ref, late_ref, sems = refs[-8:]
    planes = (len(refs) - 8) // 2
    depth, model = proj_hbm.shape
    loads = []
    for at in range(2):
        part = slice(at * depth // 2, (at + 1) * depth // 2)
        loads.append(
            pltpu.make_async_copy(proj_hbm.at[part, EARLY:], late_ref.at[part], sems.at[at])
        )
        loads[at].start()
    for at in range(planes):
        places = slice(at * PLANE, (at + 1) * PLANE)
        partial_ref[places] = refs[at][...]
        arrived = refs[planes + at]
        resident_ref[places] = arrived[:PLANE]
        fresh = arrived[PLANE:].astype(f32)
        fresh_ref[places] = fresh.reshape(fresh.shape[0] * fresh.shape[1], KVR)[:PLANE]
    peers, per_peer, _ = partial_ref.shape
    columns = peers * per_peer
    both = 2 * peers
    row_head, row_device, row_new = row_ref[:, 0:1], row_ref[:, 1:2], row_ref[:, 2:3]
    col_peer, col_head, col_dest = column_ref[0:1, :], column_ref[1:2, :], column_ref[2:3, :]
    stats = partial_ref[:, :, KVR:].astype(f32).reshape(columns, LANES).T
    log_sum = stats[0:1] + stats[1:2] + stats[2:3]
    fresh_score = stats[3:4] + stats[4:5] + stats[5:6]
    same_head = col_head == row_head
    own = same_head & (col_peer == row_device)
    new_row = row_new == 1
    arrives = same_head & (col_dest == row_device) & new_row
    fresh = jnp.sum(jnp.where(own, fresh_score, 0.0), axis=1, keepdims=True)
    scored = jnp.where(arrives, log_sum, -jnp.inf)
    peak = jnp.maximum(jnp.max(scored, axis=1, keepdims=True), fresh)
    terms = jnp.exp(scored - peak)
    fresh_term = jnp.exp(fresh - peak)
    scale = 1.0 / (jnp.sum(terms, axis=1, keepdims=True) + fresh_term)
    fresh_mixing = jnp.where((peer_ref[...] == row_device) & new_row, fresh_term * scale, 0.0)
    resident_mixing = jnp.where(own & (row_new == 0), 1.0, 0.0).astype(bf16)
    resident = resident_ref[...].reshape(columns, KVR)
    mixed = jnp.dot(resident_mixing, resident, preferred_element_type=f32)
    latents = partial_ref[:, :, :KVR].reshape(columns, KVR)
    for weights, values in ((terms * scale, latents), (fresh_mixing, fresh_ref[...].astype(bf16))):
        high = weights.astype(bf16)
        low = (weights - high.astype(f32)).astype(bf16)
        mixed = mixed + jnp.dot(high, values, preferred_element_type=f32)
        mixed = mixed + jnp.dot(low, values, preferred_element_type=f32)
    mixed = mixed.astype(bf16)
    value_rows = jnp.concatenate(
        [
            jnp.dot(
                mixed[head * both : (head + 1) * both], upward_ref[head], preferred_element_type=f32
            ).astype(bf16)
            for head in range(per_peer)
        ],
        axis=1,
    )
    for start in range(0, model, BLOCK):
        if start == EARLY - BLOCK:
            for load in loads:
                load.wait()
        if start < EARLY:
            weights = early_ref[:, start : start + BLOCK]
        else:
            weights = late_ref[:, start - EARLY : start - EARLY + BLOCK]
        part = jnp.dot(value_rows, weights, preferred_element_type=f32)
        columns = slice(start, start + BLOCK)
        keep_ref[:, :, columns] = part[:peers].reshape(peers // 2, 2, BLOCK)
        send_ref[:, :, columns] = part[peers:].reshape(peers // 2, 2, BLOCK).astype(bf16)


def expert_kernel(rows_ref, *refs):
    out_ref, arrived = refs[6], refs[10]
    gate_ref, up_ref, down_ref = refs[7:10]
    units, model = refs[0].shape
    chips, pair = out_ref.shape[:2]
    first, second = model // 4, model // 2
    steps = [(range(4), start, first) for start in range(0, model, first)]
    steps += [(range(4, 6), start, second) for start in range(0, model, second)]
    copies = []
    for matrices, start, size in steps:
        copies.append([])
        for at in matrices:
            place = refs[7 + at // 2].at[pl.ds(at % 2 * units, units), pl.ds(start, size)]
            sem = arrived.at[sum(map(len, copies))]
            copies[-1].append(
                pltpu.make_async_copy(refs[at].at[:, pl.ds(start, size)], place, sem)
            )
            copies[-1][-1].start()
    gate = up_value = jnp.zeros((rows_ref.shape[0], 2 * units), f32)
    for step, (matrices, start, size) in enumerate(steps):
        for copy in copies[step]:
            copy.wait()
        columns = slice(start, start + size)
        if size == first:
            rows = rows_ref[:, columns]
            gate += lax.dot_general(
                rows, gate_ref[:, columns], contract_last, preferred_element_type=f32
            )
            up_value += lax.dot_general(
                rows, up_ref[:, columns], contract_last, preferred_element_type=f32
            )
        else:
            act = (gate / (1.0 + jnp.exp(-gate)) * up_value).astype(bf16)
            part = jnp.dot(act, down_ref[:, columns], preferred_element_type=f32)
            out_ref[:, :, columns] = part.reshape(chips, pair, size).astype(bf16)


def near(value):
    return pltpu.with_memory_space_constraint(value, pltpu.VMEM)


def distant(value):
    return pltpu.with_memory_space_constraint(value, pltpu.HBM)


def call(kernel, outputs, operands, far=(), scratch=(), cost=None):
    specs = [scalars if operand.ndim == 1 else whole for operand in operands]
    return pl.pallas_call(
        kernel,
        out_shape=[pltpu.VMEM(shape, dtype) for shape, dtype in outputs],
        in_specs=specs + [pl.BlockSpec(memory_space=pl.ANY)] * len(far),
        out_specs=[whole] * len(outputs),
        scratch_shapes=scratch,
        compiler_params=pltpu.CompilerParams(vmem_limit_bytes=32 << 20),
        cost_estimate=cost,
    )(
        *[operand if operand.ndim == 1 else near(operand) for operand in operands],
        *far,
    )


def call_far(kernel, shapes, operands, scratch, cost=None):
    far = pl.BlockSpec(memory_space=pltpu.HBM)
    return pl.pallas_call(
        kernel,
        out_shape=shapes,
        in_specs=[far] * len(operands),
        out_specs=jax.tree.map(lambda _: far, shapes),
        scratch_shapes=scratch,
        compiler_params=pltpu.CompilerParams(vmem_limit_bytes=16 << 20),
        cost_estimate=cost,
    )(*map(distant, operands))


def prefetch(after, upward, projection):
    return pl.pallas_call(
        prefetch_kernel,
        out_shape=[pltpu.VMEM(upward.shape, bf16), pltpu.VMEM((len(projection), EARLY), bf16)],
        in_specs=[pl.BlockSpec(memory_space=pl.ANY)] * 3,
        out_specs=[whole] * 2,
        scratch_shapes=[pltpu.SemaphoreType.DMA((2,))],
        compiler_params=pltpu.CompilerParams(vmem_limit_bytes=16 << 20),
    )(after, distant(upward), distant(projection))


def middle_first(chips):
    middle = chips // 4
    return [
        2 * plane + chip
        for ring in range(middle)
        for chip in range(2)
        for plane in (middle + ring, middle - 1 - ring)
    ]


def shards(
    handoff_rows,
    handoff_dest,
    handoff_len,
    resident_cache,
    resident_len,
    queries,
    new_latent,
    residual_in,
    value_upward,
    out_proj,
    norm_gain,
    expert_ids,
    expert_gates,
    gate_proj,
    up_proj,
    down_proj,
):
    devices = lax.axis_size("ep")
    device = lax.axis_index("ep")
    core = device % 2
    chips = devices // 2
    siblings = [(i, i ^ 1) for i in range(devices)]
    chip_order = middle_first(chips)
    same_core = [[2 * chip + k for chip in chip_order] for k in range(2)]
    device_order = [2 * chip + k for k in range(2) for chip in chip_order]
    slots = sorted(range(devices), key=device_order.__getitem__)
    slice_count = MOE_FF // UNITS
    heads, width = queries.shape[2], queries.shape[3]
    per_peer = heads // devices
    model = residual_in.shape[2]

    def exchange(value, groups):
        return lax.all_to_all(
            value, "ep", split_axis=0, concat_axis=0, tiled=True, axis_index_groups=groups
        )


    planes = devices // PLANE
    toward = lambda value, bits: (
        lax.ppermute(value, "ep", [(i, i ^ bits) for i in range(devices)]) if bits else value
    )
    own_device = device.astype(jnp.int32)[None]

    flipped = jnp.swapaxes(queries[0], 1, 2)
    spread_shape = (devices, heads // PLANE * width // LANES, LANES)
    spread_rows = call_far(
        functools.partial(spread_kernel, slots),
        jax.ShapeDtypeStruct(spread_shape, bf16),
        [flipped],
        [
            pltpu.VMEM((width, heads), bf16),
            pltpu.VMEM((PLANE, *spread_shape[1:]), bf16),
            pltpu.SemaphoreType.DMA((1 + devices,)),
        ],
    )
    spread = exchange(spread_rows, [device_order])

    short = pl.CostEstimate(flops=1, bytes_accessed=1, transcendentals=0)
    flipped_keys = jnp.swapaxes(handoff_rows[0], 0, 1)
    plane_keys = [flipped_keys]
    bit = PLANE // 2
    while bit:
        crossing = [toward(keys, bit) for keys in plane_keys]
        plane_keys = [keys for pair in zip(plane_keys, crossing) for keys in pair]
        bit //= 2
    flipped_cache = jnp.swapaxes(resident_cache[0], 0, 1)
    messages = call(
        resident_kernel,
        [((planes + -(-2 // per_peer), per_peer, KVR), bf16)] * PLANE,
        [own_device, resident_len, new_latent[0]],
        [spread_rows, distant(flipped), distant(flipped_cache)],
        [
            pltpu.VMEM((width, heads), bf16),
            pltpu.VMEM(flipped_cache.shape, bf16),
            pltpu.VMEM((planes, PLANE, per_peer, KVR), f32),
            pltpu.SemaphoreType.DMA((2,)),
        ],
        pl.CostEstimate(flops=6000000000, bytes_accessed=30000000, transcendentals=262144),
    )
    messages = [toward(message, at) for at, message in enumerate(messages)]

    residents = call(
        regroup_kernel,
        [((PLANE + -(-PLANE // per_peer), per_peer, KVR), bf16)] * planes,
        [own_device, *messages],
        cost=short,
    )
    residents = [toward(resident, at * PLANE) for at, resident in enumerate(residents)]

    payloads = call(
        prompt_kernel,
        [((PLANE, per_peer, KVR + LANES), bf16)] * planes,
        [
            own_device,
            handoff_dest,
            handoff_len,
            jnp.array(slots, jnp.int32),
            *plane_keys,
            *messages,
            spread,
        ],
        scratch=[pltpu.VMEM((planes, PLANE, per_peer, KVR + LANES), bf16)],
    )
    projection = out_proj.reshape(-1, model)
    upward, early = prefetch(payloads[0], value_upward, projection)
    payloads = [toward(payload, at * PLANE) for at, payload in enumerate(payloads)]

    row = jnp.arange(per_peer * 2 * devices, dtype=jnp.int32)
    row_core = (row // devices % 2) ^ core
    chip_at = jnp.array(chip_order, jnp.int32)
    row_device = chip_at[row // 2 % chips] * 2 + row_core
    row_table = jnp.stack([row // (2 * devices), row_device, row % 2], axis=1)
    peers = device.astype(jnp.int32) ^ jnp.arange(devices, dtype=jnp.int32)
    is_peer = peers[:, None] == jnp.arange(devices, dtype=jnp.int32)[None, :]
    peer_dest = jnp.sum(jnp.where(is_peer, handoff_dest[None, :], 0), axis=1)
    column = jnp.arange(devices * per_peer, dtype=jnp.int32)
    column_table = jnp.stack(
        [jnp.repeat(peers, per_peer), column % per_peer, jnp.repeat(peer_dest, per_peer)], axis=0
    )
    keep, send = call(
        heads_kernel,
        [((chips, 2, model), f32), ((chips, 2, model), bf16)],
        [row_table, column_table, peers[None], upward, early, *payloads, *residents],
        [distant(projection)],
        [
            pltpu.VMEM((devices, per_peer, KVR + LANES), bf16),
            pltpu.VMEM((devices, per_peer, KVR), bf16),
            pltpu.VMEM((devices, KVR), f32),
            pltpu.VMEM((len(projection), model - EARLY), bf16),
            pltpu.SemaphoreType.DMA((2,)),
        ],
    )

    other = lax.ppermute(send, "ep", siblings)
    (pair,) = call(pair_kernel, [((chips, 2, model), bf16)], [keep, other])
    attention = jnp.sum(exchange(pair, same_core).astype(f32), axis=0)
    hidden = residual_in[0].astype(f32) + attention
    inverse_rms = lax.rsqrt(jnp.mean(hidden * hidden, axis=-1, keepdims=True) + norm_epsilon)
    normed = (hidden * inverse_rms * norm_gain.astype(f32)).astype(bf16)

    own_rows = exchange(jnp.broadcast_to(normed[None], (chips, 2, model)), same_core)
    experts = []
    for matrix in (gate_proj, up_proj, down_proj):
        experts += [matrix, lax.ppermute(matrix, "ep", siblings)]
    (part,) = call(
        expert_kernel,
        [((chips, 2, model), bf16)],
        [own_rows.reshape(devices, model)],
        [matrix if at == 1 else distant(matrix) for at, matrix in enumerate(experts)],
        [pltpu.VMEM((2 * gate_proj.shape[0], model), bf16)] * 3
        + [pltpu.SemaphoreType.DMA((20,))],
    )
    returned = exchange(part, same_core)

    chip_expert = chip_at * 2 // slice_count
    chosen = (expert_ids[0][..., None] == chip_expert).astype(f32)
    weights = jnp.sum(expert_gates[0][..., None] * chosen, axis=1)
    mixed = jnp.sum(weights.T[..., None] * returned.astype(f32), axis=0)
    return (hidden + mixed).astype(bf16)[None]


def solution(mesh):
    placed = (
        P(("groups", "ep"), None, None),
        P("groups"),
        P("groups"),
        P(("groups", "ep"), None, None),
        P(("groups", "ep")),
        P(None, ("groups", "ep"), None, None),
        P(None, ("groups", "ep"), None),
        P(None, ("groups", "ep"), None),
        P("ep", None, None),
        P("ep", None, None),
        P(),
        P(None, ("groups", "ep"), None),
        P(None, ("groups", "ep"), None),
        P("ep", None),
        P("ep", None),
        P("ep", None),
    )
    return jax.shard_map(
        shards,
        mesh=mesh,
        in_specs=placed,
        out_specs=P(None, ("groups", "ep"), None),
        check_vma=False,
    )
```

```python
import functools

import jax
import jax.numpy as jnp
from jax import lax
from jax.experimental import pallas as pl
from jax.experimental.pallas import tpu as pltpu
from jax.sharding import PartitionSpec as P

KVR = 512
MOE_FF = 1024
UNITS = 128
LANES = 128
BLOCK = 1024
EARLY = 5120
PLANE = 4

softmax_scale = 192.0 ** (-0.5)
norm_epsilon = 1e-06
contract_last = (((1,), (1,)), ((), ()))
f32 = jnp.float32
bf16 = jnp.bfloat16
whole = pl.BlockSpec(memory_space=pltpu.VMEM)
scalars = pl.BlockSpec(memory_space=pltpu.SMEM)


def three_parts(value):
    first = value.astype(bf16).astype(f32)
    second = (value - first).astype(bf16).astype(f32)
    third = value - first - second
    return first, second, third


def pack(rows):
    heads, width = rows.shape
    tail = width - KVR
    beside = LANES // tail
    high = heads // beside
    pieces = [rows[:, start : start + LANES] for start in range(0, KVR, LANES)]
    pieces.append(
        jnp.concatenate([rows[at * high : (at + 1) * high, KVR:] for at in range(beside)], axis=1)
    )
    return jnp.concatenate(pieces, axis=0)


def unpack(packed, heads, tail):
    pieces = [packed[at * heads : (at + 1) * heads] for at in range(KVR // LANES)]
    rest = packed[heads * (KVR // LANES) :]
    tails = [rest[:, start : start + tail] for start in range(0, LANES, tail)]
    return jnp.concatenate(pieces, axis=1), jnp.concatenate(tails, axis=0)


def spread_kernel(slots, query_hbm, spread_hbm, query_ref, blocks_ref, sems):
    peers = spread_hbm.shape[0]
    planes = peers // PLANE
    width, heads = query_ref.shape
    load = pltpu.make_async_copy(query_hbm.at[1], query_ref, sems.at[0])
    load.start()
    load.wait()
    by_peer = query_ref[...].astype(f32).T.reshape(planes, PLANE, heads // peers, width)
    copies = []
    for column in range(PLANE):
        rows = by_peer[:, column].reshape(heads // PLANE, width)
        blocks_ref[column] = pack(rows).astype(bf16)
        for plane in range(planes):
            peer = slots[plane * PLANE + column]
            copies.append(
                pltpu.make_async_copy(blocks_ref.at[column], spread_hbm.at[peer], sems.at[1 + peer])
            )
            copies[-1].start()
    for copy in copies:
        copy.wait()


def prefetch_kernel(after_ref, upward_hbm, proj_hbm, upward_ref, early_ref, sems):
    del after_ref
    copies = [
        pltpu.make_async_copy(proj_hbm.at[:, :EARLY], early_ref, sems.at[0]),
        pltpu.make_async_copy(upward_hbm, upward_ref, sems.at[1]),
    ]
    for copy in copies:
        copy.start()
    for copy in copies:
        copy.wait()


def resident_kernel(device_ref, length_ref, fresh_ref, after_ref, query_hbm, cache_hbm, *refs):
    message_refs, (query_ref, cache_ref, mixed_ref, sems) = refs[:-4], refs[-4:]
    del after_ref
    loads = [
        pltpu.make_async_copy(query_hbm.at[0], query_ref, sems.at[0]),
        pltpu.make_async_copy(cache_hbm, cache_ref, sems.at[1]),
    ]
    for load in loads:
        load.start()
    for load in loads:
        load.wait()
    query = query_ref[...].astype(f32).T
    fresh = fresh_ref[0:1].astype(f32)
    scores = jnp.dot(query.astype(bf16), cache_ref[...], preferred_element_type=f32)
    position = lax.broadcasted_iota(jnp.int32, scores.shape, 1)
    scores = jnp.where(position < length_ref[0], scores * softmax_scale, -jnp.inf)
    fresh_score = softmax_scale * jnp.sum(query * fresh, axis=1, keepdims=True)
    peak = jnp.maximum(jnp.max(scores, axis=1, keepdims=True), fresh_score)
    terms = jnp.exp(scores - peak)
    fresh_term = jnp.exp(fresh_score - peak)
    scale = 1.0 / (jnp.sum(terms, axis=1, keepdims=True) + fresh_term)
    mixed = lax.dot_general(
        (terms * scale).astype(bf16), cache_ref[:KVR], contract_last, preferred_element_type=f32
    )
    mixed_ref[...] = (mixed + fresh_term * scale * fresh[:, :KVR]).reshape(mixed_ref.shape)
    planes, _, per_peer, _ = mixed_ref.shape
    column = device_ref[0] % PLANE
    new_key = fresh_ref[1:2].astype(f32)
    rest = jnp.concatenate(
        [new_key[:, KVR:], jnp.zeros((1, 2 * KVR - new_key.shape[1]), f32)], axis=1
    )
    shape = message_refs[0].shape[1:]
    blocks = message_refs[0].shape[0] - planes
    for at, message_ref in enumerate(message_refs):
        message_ref[:planes] = mixed_ref[:, column ^ at].astype(bf16)
        for block in range(blocks):
            line = lax.broadcasted_iota(jnp.int32, shape, 0) + block * per_peer
            key_rows = jnp.where(line == 0, new_key[:, :KVR], jnp.where(line == 1, rest, 0.0))
            message_ref[planes + block] = key_rows.astype(bf16)


def regroup_kernel(device_ref, *refs):
    message_refs, out_refs = refs[:PLANE], refs[PLANE:]
    per_peer = out_refs[0].shape[1]
    plane = device_ref[0] // PLANE
    planes = len(out_refs)
    fresh = [message_ref[planes].astype(f32)[0:1] for message_ref in message_refs]
    blocks = out_refs[0].shape[0] - PLANE
    for at, out_ref in enumerate(out_refs):
        for source, message_ref in enumerate(message_refs):
            out_ref[source] = message_ref[plane ^ at]
        for block in range(blocks):
            line = lax.broadcasted_iota(jnp.int32, (per_peer, KVR), 0) + block * per_peer
            rows = jnp.zeros((per_peer, KVR), f32)
            for source, row in enumerate(fresh):
                rows = jnp.where(line == source, row, rows)
            out_ref[PLANE + block] = rows.astype(bf16)


def prompt_kernel(device_ref, dest_ref, length_ref, slot_ref, *refs):
    key_refs, message_refs, query_ref = refs[:PLANE], refs[PLANE : 2 * PLANE], refs[2 * PLANE]
    out_refs, stage_ref = refs[2 * PLANE + 1 : -1], refs[-1]
    planes, _, per_peer, width = stage_ref.shape
    heads = planes * per_peer
    tail = key_refs[0].shape[0] - KVR
    device = device_ref[0]
    prompts = [slot_ref[dest_ref[device ^ at]] for at in range(PLANE)]
    owners = [slot_ref[device ^ at] for at in range(PLANE)]
    scores = []
    for at in range(PLANE):
        prompt = device ^ at
        latent, rest = unpack(query_ref[prompts[at]], heads, tail)
        score = jnp.dot(latent, key_refs[at][:KVR], preferred_element_type=f32)
        score += jnp.dot(rest, key_refs[at][KVR:], preferred_element_type=f32)
        score *= softmax_scale
        position = lax.broadcasted_iota(jnp.int32, score.shape, 1)
        scores.append(jnp.where(position < length_ref[prompt], score, -jnp.inf))
    scores = jnp.concatenate(scores, axis=0)
    peak = jnp.max(scores, axis=1, keepdims=True)
    terms = jnp.exp(scores - peak)
    total = jnp.sum(terms, axis=1, keepdims=True)
    log_sum = peak + jnp.log(total)
    scale = 1.0 / total
    terms = terms.astype(bf16)
    lane = lax.broadcasted_iota(jnp.int32, (heads, width - KVR), 1)
    for at in range(PLANE):
        part = slice(at * heads, (at + 1) * heads)
        mixed = lax.dot_general(
            terms[part], key_refs[at][:KVR], contract_last, preferred_element_type=f32
        )
        mixed = (mixed * scale[part]).reshape(planes, per_peer, KVR)
        stage_ref[:, at, :, :KVR] = mixed.astype(bf16)
        fresh = message_refs[at][planes:].astype(f32)
        fresh = fresh.reshape(fresh.shape[0] * per_peer, KVR)
        fresh, fresh_rest = fresh[0:1], fresh[1:2, :tail]
        latent, rest = unpack(query_ref[owners[at]], heads, tail)
        fresh_score = softmax_scale * (
            jnp.sum(latent.astype(f32) * fresh, axis=1, keepdims=True)
            + jnp.sum(rest.astype(f32) * fresh_rest, axis=1, keepdims=True)
        )
        stats = jnp.zeros((heads, width - KVR), f32)
        for lane_at, value in enumerate(three_parts(log_sum[part]) + three_parts(fresh_score)):
            stats = jnp.where(lane == lane_at, value, stats)
        stats = stats.reshape(planes, per_peer, width - KVR)
        stage_ref[:, at, :, KVR:] = stats.astype(bf16)
    for at, out_ref in enumerate(out_refs):
        out_ref[...] = stage_ref[(device // PLANE) ^ at]


def pair_kernel(keep_ref, other_ref, pair_ref):
    pair_ref[...] = (keep_ref[...] + other_ref[...].astype(f32)).astype(bf16)


def heads_kernel(row_ref, column_ref, peer_ref, upward_ref, early_ref, *refs):
    proj_hbm, keep_ref, send_ref, partial_ref, resident_ref, fresh_ref, late_ref, sems = refs[-8:]
    planes = (len(refs) - 8) // 2
    depth, model = proj_hbm.shape
    loads = []
    for at in range(2):
        part = slice(at * depth // 2, (at + 1) * depth // 2)
        loads.append(
            pltpu.make_async_copy(proj_hbm.at[part, EARLY:], late_ref.at[part], sems.at[at])
        )
        loads[at].start()
    for at in range(planes):
        places = slice(at * PLANE, (at + 1) * PLANE)
        partial_ref[places] = refs[at][...]
        arrived = refs[planes + at]
        resident_ref[places] = arrived[:PLANE]
        fresh = arrived[PLANE:].astype(f32)
        fresh_ref[places] = fresh.reshape(fresh.shape[0] * fresh.shape[1], KVR)[:PLANE]
    peers, per_peer, _ = partial_ref.shape
    columns = peers * per_peer
    both = 2 * peers
    row_head, row_device, row_new = row_ref[:, 0:1], row_ref[:, 1:2], row_ref[:, 2:3]
    col_peer, col_head, col_dest = column_ref[0:1, :], column_ref[1:2, :], column_ref[2:3, :]
    stats = partial_ref[:, :, KVR:].astype(f32).reshape(columns, LANES).T
    log_sum = stats[0:1] + stats[1:2] + stats[2:3]
    fresh_score = stats[3:4] + stats[4:5] + stats[5:6]
    same_head = col_head == row_head
    own = same_head & (col_peer == row_device)
    new_row = row_new == 1
    arrives = same_head & (col_dest == row_device) & new_row
    fresh = jnp.sum(jnp.where(own, fresh_score, 0.0), axis=1, keepdims=True)
    scored = jnp.where(arrives, log_sum, -jnp.inf)
    peak = jnp.maximum(jnp.max(scored, axis=1, keepdims=True), fresh)
    terms = jnp.exp(scored - peak)
    fresh_term = jnp.exp(fresh - peak)
    scale = 1.0 / (jnp.sum(terms, axis=1, keepdims=True) + fresh_term)
    fresh_mixing = jnp.where((peer_ref[...] == row_device) & new_row, fresh_term * scale, 0.0)
    resident_mixing = jnp.where(own & (row_new == 0), 1.0, 0.0).astype(bf16)
    resident = resident_ref[...].reshape(columns, KVR)
    mixed = jnp.dot(resident_mixing, resident, preferred_element_type=f32)
    latents = partial_ref[:, :, :KVR].reshape(columns, KVR)
    for weights, values in ((terms * scale, latents), (fresh_mixing, fresh_ref[...].astype(bf16))):
        high = weights.astype(bf16)
        low = (weights - high.astype(f32)).astype(bf16)
        mixed = mixed + jnp.dot(high, values, preferred_element_type=f32)
        mixed = mixed + jnp.dot(low, values, preferred_element_type=f32)
    mixed = mixed.astype(bf16)
    value_rows = jnp.concatenate(
        [
            jnp.dot(
                mixed[head * both : (head + 1) * both], upward_ref[head], preferred_element_type=f32
            ).astype(bf16)
            for head in range(per_peer)
        ],
        axis=1,
    )
    for start in range(0, model, BLOCK):
        if start == EARLY - BLOCK:
            for load in loads:
                load.wait()
        if start < EARLY:
            weights = early_ref[:, start : start + BLOCK]
        else:
            weights = late_ref[:, start - EARLY : start - EARLY + BLOCK]
        part = jnp.dot(value_rows, weights, preferred_element_type=f32)
        columns = slice(start, start + BLOCK)
        keep_ref[:, :, columns] = part[:peers].reshape(peers // 2, 2, BLOCK)
        send_ref[:, :, columns] = part[peers:].reshape(peers // 2, 2, BLOCK).astype(bf16)


def expert_kernel(rows_ref, *refs):
    out_ref, arrived = refs[6], refs[10]
    gate_ref, up_ref, down_ref = refs[7:10]
    units, model = refs[0].shape
    chips, pair = out_ref.shape[:2]
    first, second = model // 4, model // 2
    steps = [(range(4), start, first) for start in range(0, model, first)]
    steps += [(range(4, 6), start, second) for start in range(0, model, second)]
    copies = []
    for matrices, start, size in steps:
        copies.append([])
        for at in matrices:
            place = refs[7 + at // 2].at[pl.ds(at % 2 * units, units), pl.ds(start, size)]
            sem = arrived.at[sum(map(len, copies))]
            copies[-1].append(
                pltpu.make_async_copy(refs[at].at[:, pl.ds(start, size)], place, sem)
            )
            copies[-1][-1].start()
    gate = up_value = jnp.zeros((rows_ref.shape[0], 2 * units), f32)
    for step, (matrices, start, size) in enumerate(steps):
        for copy in copies[step]:
            copy.wait()
        columns = slice(start, start + size)
        if size == first:
            rows = rows_ref[:, columns]
            gate += lax.dot_general(
                rows, gate_ref[:, columns], contract_last, preferred_element_type=f32
            )
            up_value += lax.dot_general(
                rows, up_ref[:, columns], contract_last, preferred_element_type=f32
            )
        else:
            act = (gate / (1.0 + jnp.exp(-gate)) * up_value).astype(bf16)
            part = jnp.dot(act, down_ref[:, columns], preferred_element_type=f32)
            out_ref[:, :, columns] = part.reshape(chips, pair, size).astype(bf16)


def near(value):
    return pltpu.with_memory_space_constraint(value, pltpu.VMEM)


def distant(value):
    return pltpu.with_memory_space_constraint(value, pltpu.HBM)


def call(kernel, outputs, operands, far=(), scratch=(), cost=None):
    specs = [scalars if operand.ndim == 1 else whole for operand in operands]
    return pl.pallas_call(
        kernel,
        out_shape=[pltpu.VMEM(shape, dtype) for shape, dtype in outputs],
        in_specs=specs + [pl.BlockSpec(memory_space=pl.ANY)] * len(far),
        out_specs=[whole] * len(outputs),
        scratch_shapes=scratch,
        compiler_params=pltpu.CompilerParams(vmem_limit_bytes=32 << 20),
        cost_estimate=cost,
    )(
        *[operand if operand.ndim == 1 else near(operand) for operand in operands],
        *far,
    )


def call_far(kernel, shapes, operands, scratch, cost=None):
    far = pl.BlockSpec(memory_space=pltpu.HBM)
    return pl.pallas_call(
        kernel,
        out_shape=shapes,
        in_specs=[far] * len(operands),
        out_specs=jax.tree.map(lambda _: far, shapes),
        scratch_shapes=scratch,
        compiler_params=pltpu.CompilerParams(vmem_limit_bytes=16 << 20),
        cost_estimate=cost,
    )(*map(distant, operands))


def prefetch(after, upward, projection):
    return pl.pallas_call(
        prefetch_kernel,
        out_shape=[pltpu.VMEM(upward.shape, bf16), pltpu.VMEM((len(projection), EARLY), bf16)],
        in_specs=[pl.BlockSpec(memory_space=pl.ANY)] * 3,
        out_specs=[whole] * 2,
        scratch_shapes=[pltpu.SemaphoreType.DMA((2,))],
        compiler_params=pltpu.CompilerParams(vmem_limit_bytes=16 << 20),
    )(after, distant(upward), distant(projection))


def middle_first(chips):
    middle = chips // 4
    return [
        2 * plane + chip
        for ring in range(middle)
        for chip in range(2)
        for plane in (middle + ring, middle - 1 - ring)
    ]


def shards(
    handoff_rows,
    handoff_dest,
    handoff_len,
    resident_cache,
    resident_len,
    queries,
    new_latent,
    residual_in,
    value_upward,
    out_proj,
    norm_gain,
    expert_ids,
    expert_gates,
    gate_proj,
    up_proj,
    down_proj,
):
    devices = lax.axis_size("ep")
    device = lax.axis_index("ep")
    core = device % 2
    chips = devices // 2
    siblings = [(i, i ^ 1) for i in range(devices)]
    chip_order = middle_first(chips)
    flips = [chip % 2 for chip in range(chips)]
    chip_orders = [[chip ^ 1 for chip in chip_order], chip_order]
    same_core = [
        [2 * chip + (group ^ flips[chip]) for chip in chip_orders[group]] for group in range(2)
    ]
    device_order = same_core[1] + same_core[0]
    slots = sorted(range(devices), key=device_order.__getitem__)
    slice_count = MOE_FF // UNITS
    heads, width = queries.shape[2], queries.shape[3]
    per_peer = heads // devices
    model = residual_in.shape[2]

    def exchange(value, groups):
        return lax.all_to_all(
            value, "ep", split_axis=0, concat_axis=0, tiled=True, axis_index_groups=groups
        )


    planes = devices // PLANE
    toward = lambda value, bits: (
        lax.ppermute(value, "ep", [(i, i ^ bits) for i in range(devices)]) if bits else value
    )
    own_device = device.astype(jnp.int32)[None]

    flipped = jnp.swapaxes(queries[0], 1, 2)
    spread_shape = (devices, heads // PLANE * width // LANES, LANES)
    spread_rows = call_far(
        functools.partial(spread_kernel, slots),
        jax.ShapeDtypeStruct(spread_shape, bf16),
        [flipped],
        [
            pltpu.VMEM((width, heads), bf16),
            pltpu.VMEM((PLANE, *spread_shape[1:]), bf16),
            pltpu.SemaphoreType.DMA((1 + devices,)),
        ],
    )
    spread = exchange(spread_rows, [device_order])

    short = pl.CostEstimate(flops=1, bytes_accessed=1, transcendentals=0)
    flipped_keys = jnp.swapaxes(handoff_rows[0], 0, 1)
    plane_keys = [flipped_keys]
    bit = PLANE // 2
    while bit:
        crossing = [toward(keys, bit) for keys in plane_keys]
        plane_keys = [keys for pair in zip(plane_keys, crossing) for keys in pair]
        bit //= 2
    flipped_cache = jnp.swapaxes(resident_cache[0], 0, 1)
    messages = call(
        resident_kernel,
        [((planes + -(-2 // per_peer), per_peer, KVR), bf16)] * PLANE,
        [own_device, resident_len, new_latent[0]],
        [spread_rows, distant(flipped), distant(flipped_cache)],
        [
            pltpu.VMEM((width, heads), bf16),
            pltpu.VMEM(flipped_cache.shape, bf16),
            pltpu.VMEM((planes, PLANE, per_peer, KVR), f32),
            pltpu.SemaphoreType.DMA((2,)),
        ],
        pl.CostEstimate(flops=6000000000, bytes_accessed=30000000, transcendentals=262144),
    )
    messages = [toward(message, at) for at, message in enumerate(messages)]

    residents = call(
        regroup_kernel,
        [((PLANE + -(-PLANE // per_peer), per_peer, KVR), bf16)] * planes,
        [own_device, *messages],
        cost=short,
    )
    residents = [toward(resident, at * PLANE) for at, resident in enumerate(residents)]

    payloads = call(
        prompt_kernel,
        [((PLANE, per_peer, KVR + LANES), bf16)] * planes,
        [
            own_device,
            handoff_dest,
            handoff_len,
            jnp.array(slots, jnp.int32),
            *plane_keys,
            *messages,
            spread,
        ],
        scratch=[pltpu.VMEM((planes, PLANE, per_peer, KVR + LANES), bf16)],
    )
    projection = out_proj.reshape(-1, model)
    upward, early = prefetch(payloads[0], value_upward, projection)
    payloads = [toward(payload, at * PLANE) for at, payload in enumerate(payloads)]

    row = jnp.arange(per_peer * 2 * devices, dtype=jnp.int32)
    own_group = core ^ jnp.array(flips, jnp.int32)[device // 2]
    row_group = (row // devices % 2) ^ own_group
    chip_at = jnp.array(chip_orders, jnp.int32)
    flip_at = jnp.array(flips, jnp.int32)
    row_chip = chip_at[row_group, row // 2 % chips]
    row_device = row_chip * 2 + (row_group ^ flip_at[row_chip])
    row_table = jnp.stack([row // (2 * devices), row_device, row % 2], axis=1)
    peers = device.astype(jnp.int32) ^ jnp.arange(devices, dtype=jnp.int32)
    is_peer = peers[:, None] == jnp.arange(devices, dtype=jnp.int32)[None, :]
    peer_dest = jnp.sum(jnp.where(is_peer, handoff_dest[None, :], 0), axis=1)
    column = jnp.arange(devices * per_peer, dtype=jnp.int32)
    column_table = jnp.stack(
        [jnp.repeat(peers, per_peer), column % per_peer, jnp.repeat(peer_dest, per_peer)], axis=0
    )
    keep, send = call(
        heads_kernel,
        [((chips, 2, model), f32), ((chips, 2, model), bf16)],
        [row_table, column_table, peers[None], upward, early, *payloads, *residents],
        [distant(projection)],
        [
            pltpu.VMEM((devices, per_peer, KVR + LANES), bf16),
            pltpu.VMEM((devices, per_peer, KVR), bf16),
            pltpu.VMEM((devices, KVR), f32),
            pltpu.VMEM((len(projection), model - EARLY), bf16),
            pltpu.SemaphoreType.DMA((2,)),
        ],
    )

    other = lax.ppermute(send, "ep", siblings)
    (pair,) = call(pair_kernel, [((chips, 2, model), bf16)], [keep, other])
    attention = jnp.sum(exchange(pair, same_core).astype(f32), axis=0)
    hidden = residual_in[0].astype(f32) + attention
    inverse_rms = lax.rsqrt(jnp.mean(hidden * hidden, axis=-1, keepdims=True) + norm_epsilon)
    normed = (hidden * inverse_rms * norm_gain.astype(f32)).astype(bf16)

    own_rows = exchange(jnp.broadcast_to(normed[None], (chips, 2, model)), same_core)
    experts = []
    for matrix in (gate_proj, up_proj, down_proj):
        experts += [matrix, lax.ppermute(matrix, "ep", siblings)]
    (part,) = call(
        expert_kernel,
        [((chips, 2, model), bf16)],
        [own_rows.reshape(devices, model)],
        [matrix if at == 1 else distant(matrix) for at, matrix in enumerate(experts)],
        [pltpu.VMEM((2 * gate_proj.shape[0], model), bf16)] * 3
        + [pltpu.SemaphoreType.DMA((20,))],
    )
    returned = exchange(part, same_core)

    chip_expert = chip_at[own_group] * 2 // slice_count
    chosen = (expert_ids[0][..., None] == chip_expert).astype(f32)
    weights = jnp.sum(expert_gates[0][..., None] * chosen, axis=1)
    mixed = jnp.sum(weights.T[..., None] * returned.astype(f32), axis=0)
    return (hidden + mixed).astype(bf16)[None]


def solution(mesh):
    placed = (
        P(("groups", "ep"), None, None),
        P("groups"),
        P("groups"),
        P(("groups", "ep"), None, None),
        P(("groups", "ep")),
        P(None, ("groups", "ep"), None, None),
        P(None, ("groups", "ep"), None),
        P(None, ("groups", "ep"), None),
        P("ep", None, None),
        P("ep", None, None),
        P(),
        P(None, ("groups", "ep"), None),
        P(None, ("groups", "ep"), None),
        P("ep", None),
        P("ep", None),
        P("ep", None),
    )
    return jax.shard_map(
        shards,
        mesh=mesh,
        in_specs=placed,
        out_specs=P(None, ("groups", "ep"), None),
        check_vma=False,
    )
```
